32 devices in a mesh: dp: 16 (over z, x, core), tensor: 2 (over y).
Axes of the slice: x: 2, y: 2, z: 4, core: 2. Of those that a mesh axis runs over, the one named last changes fastest.
Arguments:
- rows_in: bfloat16 [532, 16, 768], P('tensor', 'dp'), may hold values from -6 to 6
- d_out: bfloat16 [532, 16, 768], P('tensor', 'dp'), may hold values from -6 to 6
- starts: int32 [16, 8], P('dp'), may hold values from 0 to 511, as said below
- lengths: int32 [16], P('dp'), may hold values from 257 to 512, as said below
- resets: int32 [16], P('dp'), may hold values 0 or 1
- qkv_weight: bfloat16 [768, 2304], P(('dp', 'tensor')), may hold values from -0.21875 to 0.21875
- out_weight: bfloat16 [768, 768], P(('dp', 'tensor')), may hold values from -0.875 to 0.875
- bias_vec: bfloat16 [6, 768], P(None, ('dp', 'tensor')), may hold values from -2 to 2
- gains: bfloat16 [2, 768], P(None, ('dp', 'tensor')), may hold values from 0.5 to 1.5
- mem_init: bfloat16 [20, 768], P(None, ('dp', 'tensor')), may hold values from -6 to 6
- ffn_up: bfloat16 [768, 3072], P('dp', 'tensor'), may hold values from -0.21875 to 0.21875
- up_bias: bfloat16 [3072], P(('dp', 'tensor')), may hold values from -2 to 2
- ffn_down: bfloat16 [3072, 768], P('tensor', 'dp'), may hold values from -0.109375 to 0.109375
Outputs:
- layer_out: bfloat16 [532, 16, 768], P('tensor', 'dp')
- grad_rows: float32 [532, 16, 768], P('tensor', 'dp')
- grad_qkv: float32 [768, 2304], P(('dp', 'tensor'))
- grad_out_weight: float32 [768, 768], P(('dp', 'tensor'))
- grad_bias_vec: float32 [6, 768], P(None, ('dp', 'tensor'))
- grad_gains: float32 [2, 768], P(None, ('dp', 'tensor'))
- grad_mem_init: float32 [20, 768], P(None, ('dp', 'tensor'))
- grad_ffn_up: float32 [768, 3072], P('dp', 'tensor')
- grad_up_bias: float32 [3072], P(('dp', 'tensor'))
- grad_ffn_down: float32 [3072, 768], P('tensor', 'dp')
The draws below stay inside these ranges and needn't reach their ends.
Inputs may be any that keep to these rules, and one draw needn't show every extreme that they name: `starts`: each row begins with 0 and rises strictly. `lengths`: every fourth segment, counted from the first, is full.
All inputs are finite; a program needn't handle non-finite values. No bound on the sum of `resets` on one device may be relied on, other than what follows from the above.
Results may differ from the reference program's by a relative error of at most 0.015.
Values may be sent and summed in bfloat16 or wider, within the bound.
No kernel may reach another device: no remote copies, remote signals or barrier semaphores. Data moves between devices by JAX's collectives and lax.ppermute only.
A program may use at most 128 MiB of HBM per device.

```python
import jax
import jax.numpy as jnp
from jax import lax

D = 768
HEADS = 12
HEAD = 64
FF = 3072
SEG = 512
MEM = 20
DOCS = 8
ROWS = 532
SEGS = 16


def draw_starts(key, part):
    key = jax.random.fold_in(key, 11)
    seg_keys = jax.random.split(key, SEGS)

    def draw_one(seg_key):
        chosen = jax.random.permutation(seg_key, SEG - 1)[:DOCS - 1] + 1
        return jnp.concatenate([jnp.zeros((1,), jnp.int32), jnp.sort(chosen.astype(jnp.int32))])
    return jax.vmap(draw_one)(seg_keys).astype(jnp.int32)


def draw_lengths(key, part):
    key = jax.random.fold_in(key, 12)
    drawn = jax.random.randint(key, (SEGS,), SEG // 2 + 1, SEG + 1)
    return jnp.where(jnp.arange(SEGS) % 4 == 0, SEG, drawn).astype(jnp.int32)


def set_ends(values, own_key, smallest, largest):
    index_at = [jax.random.randint(jax.random.fold_in(own_key, axis), (), 0, length) for axis, length in enumerate(values.shape)]
    main_axis = values.shape.index(max(values.shape))
    next_to = index_at[:main_axis] + [(index_at[main_axis] + 1) % values.shape[main_axis]] + index_at[main_axis + 1:]
    return values.at[tuple(index_at)].set(smallest).at[tuple(next_to)].set(largest)


def block_levels(rng, shape, cuts, low, top_value):
    factor_of = 1.0
    for dim, parts in cuts:
        steps = jax.random.uniform(jax.random.fold_in(jax.random.fold_in(rng, 6), dim), (parts,), jnp.float32, low / len(cuts), top_value / len(cuts))
        factor_of = factor_of * jnp.repeat(jnp.exp(steps), shape[dim] // parts).reshape((-1,) + (1,) * (len(shape) - 1 - dim))
    return factor_of


def scatter_about(stream_key, shape, scale, most, cuts=(), kind=jnp.bfloat16):
    loudness = block_levels(stream_key, shape, cuts, -0.22, 0.18) if cuts else 1.0
    values = jax.random.normal(stream_key, shape, jnp.float32) * scale * loudness
    return jnp.minimum(jnp.maximum(values, -most), most).astype(kind)


def setup_inputs(seed: int = 0) -> dict:
    keys = jax.random.split(jax.random.key(seed), 14)
    rows_in = scatter_about(keys[0], (ROWS, SEGS, D), 1.0, 6.0, ((0, 2), (1, 16)))
    d_out = scatter_about(keys[1], (ROWS, SEGS, D), 1.0, 6.0, ((0, 2), (1, 16)))
    starts = draw_starts(jax.random.fold_in(keys[13], 71), 0)
    lengths = draw_lengths(jax.random.fold_in(keys[13], 71), 0)
    resets = set_ends((jax.random.randint(keys[4], (SEGS,), 0, 2) < 1).astype(jnp.int32), jax.random.fold_in(keys[4], 1), 0, 1)
    qkv_weight = scatter_about(keys[5], (D, 3 * D), D ** -0.5, 0.21875, ((0, 32),))
    out_weight = scatter_about(keys[6], (D, D), (D // 16) ** -0.5, 0.875, ((0, 32),))
    bias_vec = scatter_about(keys[7], (6, D), 0.3, 2.0, ((1, 32),))
    gains = jnp.clip(1.0 + 0.1 * jax.random.normal(keys[8], (2, D), jnp.float32), 0.5, 1.5).astype(jnp.bfloat16)
    mem_init = scatter_about(keys[9], (MEM, D), 1.0, 6.0, ((1, 32),))
    ffn_up = scatter_about(keys[10], (D, FF), D ** -0.5, 0.21875, ((0, 16), (1, 2)))
    up_bias = scatter_about(keys[11], (FF,), 0.3, 2.0, ((0, 32),))
    ffn_down = scatter_about(keys[12], (FF, D), FF ** -0.5, 0.109375, ((0, 2), (1, 16)))
    return {"rows_in": rows_in, "d_out": d_out, "starts": starts, "lengths": lengths, "resets": resets, "qkv_weight": qkv_weight, "out_weight": out_weight, "bias_vec": bias_vec, "gains": gains, "mem_init": mem_init, "ffn_up": ffn_up, "up_bias": up_bias, "ffn_down": ffn_down}


@jax.custom_vjp
def low(v):
    return lax.optimization_barrier(v.astype(jnp.bfloat16)).astype(jnp.float32)

@jax.custom_vjp
def low_back(v):
    return v

def low_keep(v):
    return (low(v), None)

def low_pass(kept, grad):
    return (grad,)

def back_keep(v):
    return (v, None)

def back_low(kept, grad):
    return (low(grad),)
low.defvjp(low_keep, low_pass)
low_back.defvjp(back_keep, back_low)
HIGHEST_MODE = lax.Precision.HIGHEST
NORM_EPSILON = 1e-06

def norm_rows(inputs, scale_row, shift_row):
    centered = inputs - lax.optimization_barrier(jnp.mean(inputs, axis=-1, keepdims=True))
    spread = lax.optimization_barrier(jnp.mean(centered * centered, axis=-1, keepdims=True))
    return centered * lax.rsqrt(spread + NORM_EPSILON) * scale_row + shift_row

def allowed_mask(query_ids, key_ids, starts, lengths, mem_count):
    query_doc = lax.optimization_barrier(jnp.sum((starts[:, None, :] <= (query_ids - mem_count)[None, :, None]).astype(jnp.int32), axis=-1))
    key_doc = lax.optimization_barrier(jnp.sum((starts[:, None, :] <= (key_ids - mem_count)[None, :, None]).astype(jnp.int32), axis=-1))
    key_valid = (key_ids[None, :] < mem_count) | ((key_ids - mem_count)[None, :] < lengths[:, None])
    same_doc = (query_ids < mem_count)[None, :, None] | (key_ids < mem_count)[None, None, :] | (query_doc[:, :, None] == key_doc[:, None, :])
    return same_doc & key_valid[:, None, :]

def layer(params_in, rows_x, starts, lengths, resets):
    qkv_w, out_w, biases, gain_rows, memory, up_w, up_b, down_w = params_in
    row_count, seg_count, model_width = rows_x.shape
    mem_count = memory.shape[0]
    row_ids = jnp.arange(row_count, dtype=jnp.int32)
    reset_rows = (row_ids[:, None] < mem_count) & (resets[None, :] == 1)
    mem_full = jnp.pad(memory, ((0, row_count - mem_count), (0, 0)))
    layer_in = jnp.where(reset_rows[:, :, None], mem_full[:, None, :], rows_x)
    proj_bias = jnp.concatenate([biases[0], jnp.zeros_like(biases[0]), biases[1]])
    projected = jnp.einsum('rsd,de->rse', low(layer_in), qkv_w, precision=HIGHEST_MODE) + proj_bias
    projected = low(low_back(projected))
    queries = projected[..., :model_width].reshape(row_count, seg_count, HEADS, HEAD)
    key_rows = projected[..., model_width:2 * model_width].reshape(row_count, seg_count, HEADS, HEAD)
    value_rows = projected[..., 2 * model_width:].reshape(row_count, seg_count, HEADS, HEAD)
    scores = low_back(jnp.einsum('rshe,tshe->shrt', queries, key_rows, precision=HIGHEST_MODE) * 0.125)
    allowed = allowed_mask(row_ids, row_ids, starts, lengths, mem_count)
    scores = jnp.where(allowed[:, None], scores, -1000000000.0)
    row_top = lax.optimization_barrier(jnp.max(scores, axis=-1, keepdims=True))
    expo = jnp.exp(scores - row_top)
    attn_probs = expo / lax.optimization_barrier(jnp.sum(expo, axis=-1, keepdims=True))
    mixed = jnp.einsum('shrt,tshe->rshe', low(attn_probs), value_rows, precision=HIGHEST_MODE).reshape(row_count, seg_count, model_width)
    mixed = low(low_back(mixed))
    attn_out = low_back(jnp.einsum('rsd,de->rse', mixed, out_w, precision=HIGHEST_MODE) + biases[2])
    normed_first = norm_rows(layer_in + attn_out, gain_rows[0], biases[3])
    pre_act = low_back(jnp.einsum('rsd,df->rsf', low(normed_first), up_w, precision=HIGHEST_MODE) + up_b)
    hidden = low(jax.nn.gelu(pre_act, approximate=False))
    ffn_out = low_back(jnp.einsum('rsf,fd->rsd', hidden, down_w, precision=HIGHEST_MODE) + biases[4])
    return norm_rows(normed_first + ffn_out, gain_rows[1], biases[5])

def reference(rows_in, d_out, starts, lengths, resets, qkv_weight, out_weight, bias_vec, gains, mem_init, ffn_up, up_bias, ffn_down):
    params_in = tuple((w.astype(jnp.float32) for w in (qkv_weight, out_weight, bias_vec, gains, mem_init, ffn_up, up_bias, ffn_down)))
    row_count, seg_count, model_width = rows_in.shape
    group_size = 8
    group_count = seg_count // group_size

    def to_groups(array):
        return array.reshape(row_count, group_count, group_size, model_width).transpose(1, 0, 2, 3)

    def from_groups(array):
        return array.transpose(1, 0, 2, 3).reshape(row_count, seg_count, model_width)
    pieces_all = (to_groups(rows_in.astype(jnp.float32)), to_groups(d_out.astype(jnp.float32)), starts.reshape(group_count, group_size, -1), lengths.reshape(group_count, group_size), resets.reshape(group_count, group_size))

    def step(totals, pieces):
        rows_x, cotangent, start_rows, length_rows, reset_rows = pieces
        layer_rows, pullback = jax.vjp(lambda given, inputs: layer(given, inputs, start_rows, length_rows, reset_rows), params_in, rows_x)
        grad_params, grad_x = pullback(cotangent)
        totals = jax.tree.map(lambda first, second: first + second, totals, grad_params)
        return (totals, (layer_rows, grad_x))
    zero_grads = jax.tree.map(jnp.zeros_like, params_in)
    grads, (outputs, grad_inputs) = lax.scan(step, zero_grads, pieces_all)
    return (from_groups(outputs).astype(jnp.bfloat16), from_groups(grad_inputs), grads[0], grads[1], grads[2], grads[3], grads[4], grads[5], grads[6], grads[7])
```

```python
import jax
import jax.numpy as jnp
from jax import lax
from jax.sharding import PartitionSpec as P

HEADS = 12
HEAD = 64
NORM_EPSILON = 1e-06
LOW = jnp.bfloat16
WIDE = jnp.float32


def dot(a, b, dims):
    return lax.dot_general(a, b, (dims, ((), ())), preferred_element_type=WIDE)


def ceil_to(count, unit):
    return -(-count // unit) * unit


def digits_of(dp_count):
    sizes = []
    left = dp_count
    for size in (2, 2):
        if left % size == 0 and left > 1:
            sizes.append(size)
            left //= size
    while left > 1:
        size = next((s for s in (4, 2, 3) if left % s == 0), left)
        sizes.append(size)
        left //= size
    digits, stride = [], 1
    for size in sizes:
        digits.append((stride, size))
        stride *= size
    return digits[::-1]


def digit_at(digit):
    stride, size = digit
    return (lax.axis_index("dp") // stride) % size


def rotate(value, digit, step):
    stride, size = digit
    pairs = []
    for at in range(lax.axis_size("dp")):
        mine = (at // stride) % size
        pairs.append((at, at + ((mine + step) % size - mine) * stride))
    return lax.ppermute(value, "dp", pairs)


def swap_tensor(value):
    return lax.ppermute(value, "tensor", [(0, 1), (1, 0)])


def in_order(mine, other, at, axis):
    return jnp.stack(
        [jnp.where(at == 0, mine, other), jnp.where(at == 0, other, mine)], axis=axis
    )


def spread(value, digit, axis):
    _, size = digit
    at = digit_at(digit)
    if size == 2:
        return in_order(value, rotate(value, digit, 1), at, axis)
    got = [value] + [rotate(value, digit, step) for step in range(1, size)]
    ring = jnp.stack(got[::-1] + got[::-1][:-1], axis=axis)
    return lax.dynamic_slice_in_dim(ring, (size - 1 - at) % size, size, axis)


def spread_all(value, digits):
    out = value
    for axis, digit in enumerate(digits):
        out = spread(out, digit, axis)
    return out.reshape((-1,) + value.shape)


def fold(total, digit, axis):
    _, size = digit
    at = digit_at(digit)
    kept = lax.dynamic_index_in_dim(total, at, axis, keepdims=False).astype(WIDE)
    for step in range(1, size):
        part = lax.dynamic_index_in_dim(total, (at + step) % size, axis, keepdims=False)
        kept = kept + rotate(part.astype(LOW), digit, step).astype(WIDE)
    return kept


def fold_all(total, digits):
    out = total.reshape(tuple(size for _, size in digits) + total.shape[1:])
    for axis in reversed(range(len(digits))):
        out = fold(out, digits[axis], axis)
    return out


def norm_forward(inputs):
    centered = inputs - jnp.mean(inputs, axis=-1, keepdims=True)
    scale = lax.rsqrt(jnp.mean(centered * centered, axis=-1, keepdims=True) + NORM_EPSILON)
    return centered * scale, scale


def norm_backward(cotangent, unit, scale, gain):
    d_unit = cotangent * gain
    mean_d = jnp.mean(d_unit, axis=-1, keepdims=True)
    mean_du = jnp.mean(d_unit * unit, axis=-1, keepdims=True)
    return scale * (d_unit - mean_d - unit * mean_du)


def gelu_parts(pre):
    cdf = 0.5 * (1.0 + lax.erf(pre * 0.7071067811865476))
    density = jnp.exp(-0.5 * pre * pre) * 0.3989422804014327
    return pre * cdf, cdf + pre * density


def shards(
    rows_in,
    d_out,
    starts,
    lengths,
    resets,
    qkv_weight,
    out_weight,
    bias_vec,
    gains,
    mem_init,
    ffn_up,
    up_bias,
    ffn_down,
):
    half_rows, seg_count, width = rows_in.shape
    assert seg_count == 1
    t = lax.axis_index("tensor")
    dp_count, t_count = lax.axis_size("dp"), lax.axis_size("tensor")
    assert t_count == 2
    device_count = dp_count * t_count
    digits = digits_of(dp_count)
    padded = ceil_to(half_rows, 16)
    extra = padded - half_rows
    mem_count = mem_init.shape[0]
    heads = HEADS // t_count
    part = heads * HEAD
    cols = 3 * part
    hidden_mine = ffn_up.shape[1]
    hidden_all = hidden_mine * t_count
    feat = bias_vec.shape[1]
    up_each = up_bias.shape[0]
    shard_rows = qkv_weight.shape[0]

    rows_low = jnp.pad(rows_in[:, 0, :], ((0, extra), (0, 0)))
    cotangent = jnp.pad(d_out[:, 0, :], ((0, extra), (0, 0))).astype(WIDE)
    rows_other = swap_tensor(rows_low)

    small = jnp.concatenate([bias_vec, gains, mem_init], axis=0).reshape(-1)
    small = jnp.concatenate([small, up_bias])
    small_count = small.shape[0]
    by_half = qkv_weight.reshape(shard_rows, 3, t_count, part).transpose(2, 0, 1, 3)
    by_half = by_half.reshape(t_count, shard_rows, cols)
    small_lines = -(-small_count // cols)
    small_sent = jnp.pad(small, (0, small_lines * cols - small_count)).reshape(small_lines, cols)
    w_mine = lax.dynamic_index_in_dim(by_half, t, 0, keepdims=False)
    w_other = lax.dynamic_index_in_dim(by_half, 1 - t, 0, keepdims=False)
    got = swap_tensor(jnp.concatenate([w_other, small_sent], axis=0))
    w_pair = in_order(w_mine, got[:shard_rows], t, 0).reshape(t_count * shard_rows, cols)
    small_pair = in_order(small_sent, got[shard_rows:], t, 0).reshape(t_count * small_lines, cols)
    lines = t_count * shard_rows
    lines_sent = ceil_to(lines + t_count * small_lines, 8)
    message = jnp.concatenate([w_pair, small_pair], axis=0)
    message = jnp.pad(message, ((0, lines_sent - message.shape[0]), (0, 0)))
    qkv_all = spread_all(message, digits)
    wqkv = qkv_all[:, :lines].reshape(width, cols)
    small_all = qkv_all[:, lines : lines + t_count * small_lines]
    small_all = small_all.reshape(device_count, small_lines * cols)[:, :small_count]
    n_small = (small_count - up_each) // feat
    small_rows = (
        small_all[:, : n_small * feat]
        .reshape(device_count, n_small, feat)
        .transpose(1, 0, 2)
        .reshape(n_small, width)
    )
    up_b = lax.dynamic_slice_in_dim(
        small_all[:, n_small * feat :].reshape(hidden_all), t * hidden_mine, hidden_mine, 0
    ).astype(WIDE)
    biases = small_rows[:6].astype(WIDE)
    gain_rows = small_rows[6:8].astype(WIDE)
    memory = small_rows[8:]

    out_part = out_weight
    for axis, digit in enumerate(digits[:-1]):
        out_part = spread(out_part, digit, axis)
    out_part = in_order(out_part, swap_tensor(out_part), t, len(digits) - 1)
    wout = spread(out_part, digits[-1], len(digits) - 1).reshape(width, width)
    up = spread_all(ffn_up, digits).reshape(width, hidden_mine)
    down_t = spread_all(ffn_down.T, digits).reshape(width, hidden_mine)

    rows_all = in_order(rows_low, rows_other, t, 0).reshape(2 * padded, width)
    at = jnp.arange(2 * padded, dtype=jnp.int32)
    half, within = at // padded, at % padded
    ids = half * half_rows + within
    real = within < half_rows
    fresh = resets[0] == 1
    layer_in = jnp.concatenate(
        [jnp.where(fresh, memory, rows_all[:mem_count]), rows_all[mem_count:]], axis=0
    )
    in_own = lax.dynamic_slice_in_dim(layer_in, t * padded, padded, 0)
    own_bias = lax.dynamic_slice_in_dim(biases, t * part, part, 1)
    proj_bias = jnp.concatenate([own_bias[0], jnp.zeros((part,), WIDE), own_bias[1]])
    projected = (dot(layer_in, wqkv, ((1,), (0,))) + proj_bias).astype(LOW)
    parts = projected.reshape(2 * padded, 3, heads, HEAD).transpose(1, 2, 0, 3)
    q, k, v = parts[0], parts[1], parts[2]
    doc = jnp.sum((starts[0][None, :] <= (ids - mem_count)[:, None]).astype(jnp.int32), axis=-1)
    is_mem = ids < mem_count
    key_ok = real & (is_mem | (ids - mem_count < lengths[0]))
    allowed = (is_mem[:, None] | is_mem[None, :] | (doc[:, None] == doc[None, :])) & key_ok[None, :]
    batch = lambda a, b, i, j: lax.dot_general(
        a, b, (((i,), (j,)), ((0,), (0,))), preferred_element_type=WIDE
    )
    scores = jnp.where(allowed[None], batch(q, k, 2, 2) * 0.125, -1e9)
    top = jnp.max(scores, axis=-1, keepdims=True)
    expo = jnp.exp(scores - top)
    probs = expo / jnp.sum(expo, axis=-1, keepdims=True)
    probs_low = probs.astype(LOW)
    mixed_heads = batch(probs_low, v, 2, 1).astype(LOW)
    mixed_all = mixed_heads.transpose(1, 0, 2).reshape(2, padded, part)
    mix_own = lax.dynamic_index_in_dim(mixed_all, t, 0, keepdims=False)
    mix_got = swap_tensor(lax.dynamic_index_in_dim(mixed_all, 1 - t, 0, keepdims=False))
    mixed = in_order(mix_own, mix_got, t, 1).reshape(padded, width)
    attn_out = dot(mixed, wout, ((1,), (0,))) + biases[2]
    unit_first, scale_first = norm_forward(in_own.astype(WIDE) + attn_out)
    normed_first = unit_first * gain_rows[0] + biases[3]

    normed_low = normed_first.astype(LOW)
    normed_all = jnp.concatenate([normed_low, swap_tensor(normed_low)], axis=0)
    pre_act = dot(normed_all, up, ((1,), (0,))) + up_b
    hidden, gelu_slope = gelu_parts(pre_act)
    hidden = hidden.astype(LOW)
    ffn_sums = dot(hidden, down_t, ((1,), (1,)))
    ffn_out = (
        ffn_sums[:padded] + swap_tensor(ffn_sums[padded:].astype(LOW)).astype(WIDE) + biases[4]
    )
    unit_second, scale_second = norm_forward(normed_first + ffn_out)
    layer_out = (unit_second * gain_rows[1] + biases[5]).astype(LOW)

    d_second = norm_backward(cotangent, unit_second, scale_second, gain_rows[1])
    grad_gain_two = jnp.sum(cotangent * unit_second, axis=0)
    grad_shift_two = jnp.sum(cotangent, axis=0)
    d_ffn = d_second.astype(LOW)
    grad_ffn_bias = jnp.sum(d_ffn.astype(WIDE), axis=0)
    d_ffn_all = jnp.concatenate([d_ffn, swap_tensor(d_ffn)], axis=0)
    grad_down_part = dot(d_ffn_all, hidden, ((0,), (0,)))
    grad_ffn_down = fold_all(grad_down_part.reshape(dp_count, -1, hidden_mine), digits)
    d_pre_wide = gelu_slope * dot(d_ffn_all, down_t, ((1,), (0,)))
    d_pre = d_pre_wide.astype(LOW)
    grad_up_bias_mine = jnp.sum(d_pre.astype(WIDE), axis=0)
    grad_up_part = dot(normed_all, d_pre, ((0,), (0,)))
    grad_ffn_up = fold_all(grad_up_part.reshape(dp_count, -1, hidden_mine), digits)
    d_first_sums = dot(d_pre, up, ((1,), (1,)))
    d_first = (
        d_second
        + d_first_sums[:padded]
        + swap_tensor(d_first_sums[padded:].astype(LOW)).astype(WIDE)
    )
    d_attn_in = norm_backward(d_first, unit_first, scale_first, gain_rows[0])
    grad_gain_one = jnp.sum(d_first * unit_first, axis=0)
    grad_shift_one = jnp.sum(d_first, axis=0)
    d_attn = d_attn_in.astype(LOW)
    grad_attn_bias = jnp.sum(d_attn.astype(WIDE), axis=0)
    grad_out_part = dot(mixed, d_attn, ((0,), (0,)))
    d_mixed = dot(d_attn, wout, ((1,), (1,))).astype(LOW).reshape(padded, 2, part)
    d_mix_own = lax.dynamic_index_in_dim(d_mixed, t, 1, keepdims=False)
    d_mix_got = swap_tensor(lax.dynamic_index_in_dim(d_mixed, 1 - t, 1, keepdims=False))
    d_mix = in_order(d_mix_own, d_mix_got, t, 0).reshape(2 * padded, heads, HEAD)
    d_mix = d_mix.transpose(1, 0, 2)
    d_probs = batch(d_mix, v, 2, 2)
    row_dot = jnp.sum(probs * d_probs, axis=-1, keepdims=True)
    d_scores = (probs * (d_probs - row_dot)).astype(LOW)
    d_q = batch(d_scores, k, 2, 1) * 0.125
    d_k = batch(d_scores, q, 1, 1) * 0.125
    d_v = batch(probs_low, d_mix, 1, 1)
    d_projected = jnp.stack([d_q, d_k, d_v]).astype(LOW)
    d_projected = d_projected.transpose(2, 0, 1, 3).reshape(2 * padded, cols)
    grad_out = grad_out_part.reshape(-1, t_count, out_weight.shape[0], width)
    keep = lax.dynamic_index_in_dim(grad_out, t, 1, keepdims=False)
    sent = lax.dynamic_index_in_dim(grad_out, 1 - t, 1, keepdims=False)
    grad_out = keep + swap_tensor(sent.astype(LOW)).astype(WIDE)
    grad_out_weight = fold_all(grad_out, digits)

    proj_sums = jnp.sum(d_projected.astype(WIDE), axis=0)
    grad_qkv_part = dot(layer_in, d_projected, ((0,), (0,)))
    d_in_sums = dot(d_projected, wqkv, ((1,), (1,))).reshape(2, padded, width)
    d_in_own = lax.dynamic_index_in_dim(d_in_sums, t, 0, keepdims=False)
    d_in_sent = lax.dynamic_index_in_dim(d_in_sums, 1 - t, 0, keepdims=False)
    d_in = d_attn_in + d_in_own + swap_tensor(d_in_sent.astype(LOW)).astype(WIDE)
    mem_first = fresh & (t == 0)
    mem_rows = d_in[:mem_count]
    grad_memory = jnp.where(mem_first, mem_rows, 0.0)
    grad_rows = jnp.concatenate(
        [jnp.where(mem_first, 0.0, mem_rows), d_in[mem_count:half_rows]], axis=0
    )[:, None, :]

    place = lambda vec, whole, here: lax.dynamic_update_slice(
        jnp.zeros((whole,), WIDE), vec, (here,)
    )
    small_grads = jnp.concatenate(
        [
            jnp.stack(
                [
                    place(proj_sums[:part], width, t * part),
                    place(proj_sums[2 * part :], width, t * part),
                    grad_attn_bias,
                    grad_shift_one,
                    grad_ffn_bias,
                    grad_shift_two,
                    grad_gain_one,
                    grad_gain_two,
                ]
            ),
            grad_memory,
        ],
        axis=0,
    )
    small_grads = small_grads.reshape(n_small, device_count, feat).transpose(1, 0, 2)
    up_grads = place(grad_up_bias_mine, hidden_all, t * hidden_mine)
    small_grads = jnp.concatenate(
        [small_grads.reshape(device_count, -1), up_grads.reshape(device_count, up_each)], axis=1
    )
    room = small_lines * cols
    small_grads = jnp.pad(small_grads, ((0, 0), (0, room - small_count)))
    small_grads = small_grads.reshape(dp_count, t_count * small_lines, cols)
    qkv_lines = jnp.concatenate(
        [grad_qkv_part.reshape(dp_count, lines, cols), small_grads], axis=1
    )
    qkv_lines = jnp.pad(qkv_lines, ((0, 0), (0, lines_sent - qkv_lines.shape[1]), (0, 0)))
    qkv_sum = fold_all(qkv_lines, digits)
    qkv_grad = qkv_sum[:lines].reshape(t_count, shard_rows, cols)
    small_sum = qkv_sum[lines : lines + t_count * small_lines]
    small_sum = small_sum.reshape(t_count, small_lines, cols)
    give = jnp.concatenate(
        [
            lax.dynamic_index_in_dim(qkv_grad, 1 - t, 0, keepdims=False),
            lax.dynamic_index_in_dim(small_sum, 1 - t, 0, keepdims=False),
        ],
        axis=0,
    )
    got = swap_tensor(give.astype(LOW)).astype(WIDE)
    own_grad = lax.dynamic_index_in_dim(qkv_grad, t, 0, keepdims=False)
    grad_qkv = in_order(
        own_grad.reshape(shard_rows, 3, part), got[:shard_rows].reshape(shard_rows, 3, part), t, 2
    ).reshape(shard_rows, 3 * width)
    small_out = lax.dynamic_index_in_dim(small_sum, t, 0, keepdims=False) + got[shard_rows:]
    small_out = small_out.reshape(-1)[:small_count]
    small_mat = small_out[: n_small * feat].reshape(n_small, feat)
    return (
        layer_out[:half_rows, None, :],
        grad_rows,
        grad_qkv,
        grad_out_weight,
        small_mat[:6],
        small_mat[6:8],
        small_mat[8:],
        grad_ffn_up,
        small_out[n_small * feat :],
        grad_ffn_down.T,
    )


def solution(mesh):
    both = ("dp", "tensor")
    in_specs = (
        P("tensor", "dp", None),
        P("tensor", "dp", None),
        P("dp", None),
        P("dp"),
        P("dp"),
        P(both, None),
        P(both, None),
        P(None, both),
        P(None, both),
        P(None, both),
        P("dp", "tensor"),
        P(both),
        P("tensor", "dp"),
    )
    out_specs = (
        P("tensor", "dp", None),
        P("tensor", "dp", None),
        P(both, None),
        P(both, None),
        P(None, both),
        P(None, both),
        P(None, both),
        P("dp", "tensor"),
        P(both),
        P("tensor", "dp"),
    )
    return jax.shard_map(shards, mesh=mesh, in_specs=in_specs, out_specs=out_specs, check_vma=False)
```

```python
import functools

import jax
import jax.numpy as jnp
import numpy as np
from jax import lax
from jax.experimental import pallas as pl
from jax.experimental.pallas import tpu as pltpu
from jax.sharding import PartitionSpec as P

HEADS = 12
HEAD = 64
NORM_EPSILON = 1e-06
LOW = jnp.bfloat16
WIDE = jnp.float32
CHUNK = 32
ROWS = 16
PAIR = 2 * HEAD
QUICK = pl.CostEstimate(flops=1, bytes_accessed=1, transcendentals=0)
T, X, CORE, OUTER, DP, FRESH, LENGTH, STARTS = range(8)


def ceil_to(count, unit):
    return -(-count // unit) * unit


def nn(a, b):
    return lax.dot_general(a, b, (((1,), (0,)), ((), ())), preferred_element_type=WIDE)


def nt(a, b):
    return lax.dot_general(a, b, (((1,), (1,)), ((), ())), preferred_element_type=WIDE)


def tn(a, b):
    return lax.dot_general(a, b, (((0,), (0,)), ((), ())), preferred_element_type=WIDE)


def low_of(*shape):
    return jax.ShapeDtypeStruct(shape, LOW)


def wide_of(*shape):
    return jax.ShapeDtypeStruct(shape, WIDE)


def held_bytes(array):
    rows, cols = ((1,) + tuple(array.shape))[-2:]
    lead = int(np.prod(array.shape[:-2])) if len(array.shape) > 2 else 1
    return lead * ceil_to(rows, 16) * ceil_to(cols, 128) * jnp.dtype(array.dtype).itemsize


def call(kernel, outs, at, *arrays, scratch=(), room=0):
    room += sum(held_bytes(array) for array in (*arrays, *outs))
    room += sum(held_bytes(ref) for ref in scratch)
    return pl.pallas_call(
        kernel,
        in_specs=[pl.BlockSpec(memory_space=pltpu.SMEM)]
        + [pl.BlockSpec(memory_space=pltpu.VMEM)] * len(arrays),
        out_specs=[pl.BlockSpec(memory_space=pltpu.VMEM)] * len(outs),
        out_shape=list(outs),
        scratch_shapes=list(scratch),
        compiler_params=pltpu.CompilerParams(vmem_limit_bytes=room + (3 << 20)),
        cost_estimate=QUICK,
    )(at, *arrays)


def digits_of(dp_count):
    assert dp_count % 4 == 0
    sizes = [2, 2]
    left = dp_count // 4
    while left > 1:
        size = next((s for s in (4, 2, 3) if left % s == 0), left)
        sizes.append(size)
        left //= size
    if len(sizes) == 2:
        sizes.append(1)
    digits, stride = [], 1
    for size in sizes:
        digits.append((stride, size))
        stride *= size
    return digits[::-1]


def digit_at(digit):
    stride, size = digit
    return (lax.axis_index("dp") // stride) % size


def rotate(value, digit, step):
    stride, size = digit
    pairs = []
    for at in range(lax.axis_size("dp")):
        mine = (at // stride) % size
        pairs.append((at, at + ((mine + step) % size - mine) * stride))
    return lax.ppermute(value, "dp", pairs)


def swap_tensor(value):
    return lax.ppermute(value, "tensor", [(0, 1), (1, 0)])


def tie(value, *others):
    return lax.optimization_barrier((value,) + others)[0]


join = lambda *values: lax.optimization_barrier(values)


def spread_outer(value, digits):
    for digit in reversed(digits[:-2]):
        got = [value] + [rotate(value, digit, step) for step in range(1, digit[1])]
        value = jnp.stack(got)
    return value.reshape((-1,) + value.shape[-2:])


def assemble_kernel(sizes, cuts, at, *refs):
    parts, wholes = refs[:4], refs[4:]
    outer = sizes[:-2]
    me, digits = at[DP], []
    for size in reversed(sizes):
        digits.append(lax.rem(me, size))
        me = lax.div(me, size)
    digits = digits[::-1]
    for swap_core in range(2):
        for swap_x in range(2):
            source = parts[2 * swap_core + swap_x]
            for slot in range(source.shape[0]):
                left, steps = slot, []
                for size in reversed(outer):
                    steps.append(left % size)
                    left //= size
                place = 0
                for size, digit, step in zip(outer, digits, steps[::-1]):
                    place = place * size + lax.rem(digit + (size - step), size)
                x, core = digits[-2], digits[-1]
                place = place * 2 + (1 - x if swap_x else x)
                place = place * 2 + (1 - core if swap_core else core)
                for whole, low, high in zip(wholes, cuts[:-1], cuts[1:]):
                    whole[place] = source[slot, :, low:high]


def assemble(at, mine, x_got, digits, *cuts):
    core = digits[-1]
    parts = [mine, x_got, rotate(mine, core, 1), rotate(x_got, core, 1)]
    slots, rows, cols = mine.shape
    cuts = (0, *cuts, cols)
    outs = [low_of(4 * slots, rows, b - a) for a, b in zip(cuts[:-1], cuts[1:])]
    sizes = tuple(size for _, size in digits)
    wholes = call(functools.partial(assemble_kernel, sizes, cuts), outs, at, *parts)
    wholes = [whole.reshape(4 * slots * rows, -1) for whole in wholes]
    return wholes if len(wholes) > 1 else wholes[0]


def columns_kernel(part, small_rows, at, weight, vectors, gains, memory, up, out, kept, sent, turn):
    lines, width = weight.shape[0], weight.shape[1] // 3
    first = at[T] == 0
    for pair in range(part // PAIR):
        for kind in range(3):
            low = kind * width + pair * PAIR
            a, b = weight[:, low : low + PAIR], weight[:, low + part : low + part + PAIR]
            here = (3 * pair + kind) * PAIR
            kept[:, here : here + PAIR] = jnp.where(first, a, b)
            sent[:, here : here + PAIR] = jnp.where(first, b, a)
    turn[...] = jnp.zeros_like(turn)
    for source, (low, high) in zip((memory, vectors, gains, up), small_rows):
        turn[low:high, :lines] = source[...].astype(WIDE)
    columns = turn[...].T[:lines].astype(LOW)
    for target in (kept, sent):
        target[:, 3 * part : 3 * part + PAIR] = columns
        target[:, 3 * part + PAIR :] = out[...]


def pair_kernel(at, kept, got, pair):
    lines = kept.shape[0]
    first = at[T] == 0
    pair[:lines] = jnp.where(first, kept[...], got[...])
    pair[lines:] = jnp.where(first, got[...], kept[...])


def put_blocks(total, kept, sent, core, at):
    groups, rows, _ = kept.shape
    cols = total.shape[1]
    total = total.astype(LOW).reshape(2 * groups, rows, cols)
    second = core == 1
    for group in range(groups):
        even, odd = total[2 * group], total[2 * group + 1]
        kept[group, :, at : at + cols] = jnp.where(second, odd, even)
        sent[group, :, at : at + cols] = jnp.where(second, even, odd)


def put_gradient(a, b, outs, core, tile=384, own=None):
    for low in range(0, b.shape[1], tile):
        total = tn(a[...], b[:, low : low + tile])
        if own is not None:
            total = total + own[:, low : low + tile]
        if len(outs) == 1:
            outs[0][:, low : low + tile] = total.astype(LOW)
        else:
            put_blocks(total, *outs, core, low)


def gradient_outs(width, cols, dp_count):
    rows = width // dp_count
    if rows % 16:
        return [low_of(width, cols)]
    return [low_of(dp_count // 2, rows, cols)] * 2


def split_cores(outs, dp_count, core):
    if len(outs) == 2:
        return outs
    whole = outs[0].reshape(dp_count // 2, 2, -1, outs[0].shape[1])
    take = lambda which: lax.dynamic_index_in_dim(whole, which, 1, keepdims=False)
    return take(core), take(1 - core)


def gradient_kernel(at, a, b, *outs):
    put_gradient(a, b, outs, at[CORE])


def own_kernel(at, a_down, b_down, a_up, b_up, down, up, sums):
    tile = 384
    for low in range(0, b_down.shape[1], tile):
        here = slice(low, low + tile)
        down[:, here] = tn(a_down[...], b_down[:, here])
        up[:, here] = tn(a_up[...], b_up[:, here])
    sums[...] = jnp.sum(b_up[...].astype(WIDE), axis=0, keepdims=True)


def rest_kernel(at, own, a, b, *outs):
    put_gradient(a, b, outs, at[CORE], own=own)


def rest_sums_kernel(spots, at, own, own_sums, a, b, target, sums, *outs):
    put_gradient(a, b, outs, at[CORE], own=own)
    total = (own_sums[...] + jnp.sum(b[...].astype(WIDE), axis=0, keepdims=True)).astype(LOW)
    total = jnp.broadcast_to(total, (8, total.shape[1]))
    for spot in range(spots):
        sums[spot : spot + 1, :] = nt(total, one_hot(target, spot, total.shape[1]))[:1]


def one_hot(target, spot, count):
    at = lax.broadcasted_iota(jnp.int32, (target.shape[0], count), 1)
    return (at == target[:, :1] + spot * target[0, 1]).astype(WIDE).astype(LOW)


def up_row_kernel(first_row, spots, at, small, target, row):
    part = target.shape[0]
    total = jnp.zeros((8, row.shape[1]), WIDE)
    for spot in range(spots):
        line = small[first_row + spot : first_row + spot + 1, :]
        line = jnp.where(at[T] == 0, line[:, :part], line[:, part:]).astype(LOW)
        line = jnp.broadcast_to(line, (8, part))
        total = total + nn(line, one_hot(target, spot, row.shape[1]))
    row[...] = jnp.broadcast_to(total[:1], row.shape)


def halve_kernel(at, mine, got, kept, sent):
    x = at[X]
    for group in range(kept.shape[0]):
        for other, out in ((0, kept), (1, sent)):
            place = 2 * group + (1 - x if other else x)
            out[group] = (mine[place].astype(WIDE) + got[place].astype(WIDE)).astype(LOW)


def halve(at, mine, got):
    groups, rows, cols = mine.shape
    return call(halve_kernel, [low_of(groups // 2, rows, cols)] * 2, at, mine, got)


def parts_kernel(size, count, at, *refs):
    mine, got, outs = refs[:count], refs[count : 2 * count], refs[2 * count :]
    me = at[OUTER]
    for group in range(outs[0].shape[0]):
        low = 0
        for a, b in zip(mine, got):
            high = low + a.shape[2]
            for step, out in enumerate(outs):
                place = group * size + lax.rem(me + step, size)
                total = a[place].astype(WIDE) + b[place].astype(WIDE)
                out[group, :, low:high] = total.astype(out.dtype)
            low = high


def outer_parts(at, mine, got, digits):
    size = digits[-3][1]
    blocks, rows, _ = mine[0].shape
    cols = sum(array.shape[2] for array in mine)
    shape = (blocks // size, rows, cols)
    outs = [wide_of(*shape)] + [low_of(*shape)] * (size - 1)
    kept, *sent = call(
        functools.partial(parts_kernel, size, len(mine)), outs, at, *mine, *got
    )
    return kept, sent


def outer_send(sent, digits):
    return [rotate(part, digits[-3], step + 1) for step, part in enumerate(sent)]


def outer_sum(kept, got, digits):
    for part in got:
        kept = kept + part.astype(WIDE)
    for digit in reversed(digits[:-3]):
        size = digit[1]
        kept = kept.reshape((-1, size) + kept.shape[1:])
        at = digit_at(digit)
        take = lambda step: lax.dynamic_index_in_dim(kept, (at + step) % size, 1, keepdims=False)
        total = take(0)
        for step in range(1, size):
            total = total + rotate(take(step).astype(LOW), digit, step).astype(WIDE)
        kept = total
    return kept[0]


def fill_mask(mask, at, half_rows, mem_count, starts):
    rows = mask.shape[0]
    padded = rows // 2

    def places(shape, axis):
        spot = lax.broadcasted_iota(jnp.int32, shape, axis)
        second = spot >= padded
        within = jnp.where(second, spot - padded, spot)
        pos = within + jnp.where(second, half_rows, 0) - mem_count
        doc = jnp.zeros(shape, jnp.int32)
        for i in range(starts):
            doc = doc + (at[STARTS + i] <= pos).astype(jnp.int32)
        return within < half_rows, pos, doc

    _, q_pos, q_doc = places((rows, 1), 0)
    real, k_pos, k_doc = places((1, rows), 1)
    key_ok = real & (k_pos < at[LENGTH])
    for low in range(0, rows, CHUNK):
        qp, qd = q_pos[low : low + CHUNK], q_doc[low : low + CHUNK]
        same = (qd == k_doc) | (qp < 0) | (k_pos < 0)
        mask[low : low + CHUNK, :] = jnp.where(same & key_ok, 0.0, -1e9)


def lanes(pair, count):
    return pl.ds(pl.multiple_of(pair * count, PAIR), count)


def forward_kernel(
    half_rows, mem_count, starts, first_bias,
    at, own, other, w, qkv, mix_own, mix_sent, lse, x, small, mask, s, p, mixed,
):
    rows, padded = x.shape[0], own.shape[0]
    t = at[T]
    part = mix_own.shape[1]
    fill_mask(mask, at, half_rows, mem_count, starts)
    lse[...] = jnp.zeros_like(lse)
    small[...] = w[:, 3 * part :].astype(WIDE).T[: small.shape[0]]
    x[pl.ds(pl.multiple_of(t * padded, 16), padded), :] = own[...]
    x[pl.ds(pl.multiple_of((1 - t) * padded, 16), padded), :] = other[...]
    row = lax.broadcasted_iota(jnp.int32, (32, 1), 0)
    fresh = (row < mem_count) & (at[FRESH] == 1)
    x[:32, :] = jnp.where(fresh, small[:32, :], x[:32, :].astype(WIDE)).astype(LOW)
    lane = lax.broadcasted_iota(jnp.int32, (1, PAIR), 1)
    scale = jnp.where(lax.broadcasted_iota(jnp.int32, (1, 3 * PAIR), 1) < PAIR, 0.125, 1.0)

    def one_pair(pair, _):
        here = pl.ds(pl.multiple_of(t * part + pair * PAIR, PAIR), PAIR)
        q_bias = small[first_bias : first_bias + 1, here]
        v_bias = small[first_bias + 1 : first_bias + 2, here]
        bias = jnp.concatenate([q_bias, jnp.zeros_like(q_bias), v_bias], axis=1)
        got = (nn(x[...], w[:, lanes(pair, 3 * PAIR)]) + bias).astype(LOW)
        got = (got.astype(WIDE) * scale).astype(LOW)
        qkv[:, lanes(pair, 3 * PAIR)] = got
        keys, values = got[:, PAIR : 2 * PAIR], got[:, 2 * PAIR :]
        for h in range(2):
            mine = (lane < HEAD) if h == 0 else (lane >= HEAD)
            s[...] = nt(jnp.where(mine, got[:, :PAIR], jnp.zeros((), LOW)), keys)

            def body(i, _):
                here = pl.ds(pl.multiple_of(i * CHUNK, CHUNK), CHUNK)
                v = s[here, :] + mask[here, :]
                top = jnp.max(v, axis=-1, keepdims=True)
                e = jnp.exp(v - top)
                total = jnp.sum(e, axis=-1, keepdims=True)
                p[here, :] = (e * (1.0 / total)).astype(LOW)
                spot = lane == 2 * pair + h
                lse[here, :] = jnp.where(spot, top + jnp.log(total), lse[here, :])
                return 0

            lax.fori_loop(0, rows // CHUNK, body, 0, unroll=True)
            out = nn(p[...], values).astype(LOW)
            if h == 0:
                mixed[...] = out
            else:
                mixed[...] = jnp.where(mine, out, mixed[...])
        mix_own[:, lanes(pair, PAIR)] = mixed[pl.ds(pl.multiple_of(t * padded, 16), padded), :]
        mix_sent[:, lanes(pair, PAIR)] = mixed[
            pl.ds(pl.multiple_of((1 - t) * padded, 16), padded), :
        ]
        return 0

    lax.fori_loop(0, part // PAIR, one_pair, 0)


def backward_kernel(
    half_rows, mem_count, starts, at, qkv, own, got, lse, dproj, sums, mask, s, dp, p, ds, dmix
):
    rows, padded = qkv.shape[0], own.shape[0]
    part = own.shape[1]
    t = at[T]
    fill_mask(mask, at, half_rows, mem_count, starts)
    dmix[pl.ds(pl.multiple_of(t * padded, 16), padded), :] = own[...]
    dmix[pl.ds(pl.multiple_of((1 - t) * padded, 16), padded), :] = got[...]
    lane = lax.broadcasted_iota(jnp.int32, (1, PAIR), 1)
    zero = jnp.zeros((), LOW)

    def one_pair(pair, _):
        here = lanes(pair, 3 * PAIR)
        whole = qkv[:, here]
        keys, values = whole[:, PAIR : 2 * PAIR], whole[:, 2 * PAIR :]
        dm_pair = dmix[:, lanes(pair, PAIR)]
        parts = []
        for h in range(2):
            mine = (lane < HEAD) if h == 0 else (lane >= HEAD)
            q = jnp.where(mine, whole[:, :PAIR], zero)
            dm = jnp.where(mine, dm_pair, zero)
            s[...] = nt(q, keys)
            dp[...] = nt(dm, values)

            def body(i, _):
                here = pl.ds(pl.multiple_of(i * CHUNK, CHUNK), CHUNK)
                spot = lane == 2 * pair + h
                stat = jnp.sum(jnp.where(spot, lse[here, :], 0.0), axis=-1, keepdims=True)
                e = jnp.exp(s[here, :] + mask[here, :] - stat)
                d = dp[here, :]
                dot = jnp.sum(e * d, axis=-1, keepdims=True)
                p[here, :] = e.astype(LOW)
                ds[here, :] = (e * (d - dot)).astype(LOW)
                return 0

            lax.fori_loop(0, rows // CHUNK, body, 0, unroll=True)
            parts.append((nn(ds[...], keys) * 0.125, tn(ds[...], q), tn(p[...], dm)))
        dq = jnp.where(lane < HEAD, parts[0][0], parts[1][0])
        dk, dv = parts[0][1] + parts[1][1], parts[0][2] + parts[1][2]
        out = jnp.concatenate([dq, dk, dv], axis=1).astype(LOW)
        dproj[:, here] = out
        sums[:, here] = jnp.sum(out.astype(WIDE), axis=0, keepdims=True)
        return 0

    lax.fori_loop(0, part // PAIR, one_pair, 0)


def projection_back_kernel(
    small_rows, at, layer_in, d_projected, proj_sums, sums_one, sums_two, up_sums, wqkv, d_attn,
    *outs,
):
    d_own, d_sent = outs[:2]
    grads, turn = outs[2:-1], outs[-1]
    padded, part = d_own.shape[0], up_sums.shape[1]
    cols = d_projected.shape[1]
    t = at[T]
    first = t == 0
    half = lambda which: d_projected[pl.ds(pl.multiple_of(which * padded, 16), padded), :]
    weights = wqkv[:, :cols]
    own = nt(half(t), weights)
    other = nt(half(1 - t), weights)
    d_own[...] = d_attn[...] + own
    d_sent[...] = other.astype(LOW)
    turn[...] = jnp.zeros_like(turn)
    (m0, m1), (v0, _), (g0, _), (u0, _) = small_rows
    count = m1 - m0
    memory = jnp.where(first, own[:count] + d_attn[:count, :], other[:count])
    turn[m0:m1, :] = jnp.where(at[FRESH] == 1, memory, 0.0)
    sums = [
        jnp.concatenate(
            [proj_sums[:, (3 * p + k) * PAIR : (3 * p + k + 1) * PAIR] for p in range(part // PAIR)],
            axis=1,
        )
        for k in (0, 2)
    ]
    for value, low in zip(sums + [up_sums[...]], (v0, v0 + 1, u0)):
        high = low + value.shape[0]
        turn[low:high, :part] = jnp.where(first, value, 0.0)
        turn[low:high, part:] = jnp.where(first, 0.0, value)
    turn[v0 + 2 : v0 + 4, :] = sums_one[0:2, :]
    turn[v0 + 4 : v0 + 6, :] = sums_two[0:2, :]
    turn[g0 : g0 + 1, :] = sums_one[2:3, :]
    turn[g0 + 1 : g0 + 2, :] = sums_two[2:3, :]
    small = turn[...].T
    put_gradient(layer_in, d_projected, grads, at[CORE])
    if len(grads) == 1:
        grads[0][:, cols:] = small.astype(LOW)
    else:
        put_blocks(small, *grads, at[CORE], cols)


def halves_kernel(count, at, *refs):
    parts, (mine, give) = refs[:count], refs[count:]
    lines = mine.shape[0]
    total = parts[0][...]
    for part in parts[1:]:
        total = total + part[...].astype(WIDE)
    first = at[T] == 0
    mine[...] = jnp.where(first, total[:lines], total[lines:])
    give[...] = jnp.where(first, total[lines:], total[:lines]).astype(LOW)


def finish_kernel(part, small_rows, at, mine, got, qkv, out, memory, vectors, gains, up, turn):
    lines = mine.shape[0]
    cols, width = 3 * part, 2 * part
    first = at[T] == 0
    for pair in range(part // PAIR):
        for kind in range(3):
            here = (3 * pair + kind) * PAIR
            a = mine[:, here : here + PAIR]
            b = got[:, here : here + PAIR].astype(WIDE)
            low = kind * width + pair * PAIR
            qkv[:, low : low + PAIR] = jnp.where(first, a, b)
            qkv[:, low + part : low + part + PAIR] = jnp.where(first, b, a)
    turn[...] = jnp.zeros_like(turn)
    turn[:lines, :] = mine[:, cols : cols + PAIR] + got[:, cols : cols + PAIR].astype(WIDE)
    out[...] = mine[:, cols + PAIR :] + got[:, cols + PAIR :].astype(WIDE)
    small = turn[...].T
    for target, (low, high) in zip((memory, vectors, gains, up), small_rows):
        target[...] = small[low:high, :lines]


def spread_of(v):
    return jnp.mean(v, axis=-1, keepdims=True)


def first_norm_kernel(bias, gain, at, own, got, wout, layer_in, small, mixed, unit, scale, normed, s):
    padded, part = own.shape
    first = at[T] == 0
    mixed[:, :part] = jnp.where(first, own[...], got[...])
    mixed[:, part:] = jnp.where(first, got[...], own[...])
    s[...] = nn(mixed[...], wout[...])
    for low in range(0, padded, ROWS):
        here = slice(low, low + ROWS)
        rows = layer_in[pl.ds(pl.multiple_of(at[T] * padded + low, ROWS), ROWS), :]
        total = rows.astype(WIDE) + (s[here, :] + small[bias + 2 : bias + 3, :])
        centered = total - spread_of(total)
        factor = lax.rsqrt(spread_of(centered * centered) + NORM_EPSILON)
        value = centered * factor
        unit[here, :] = value
        scale[here, :] = jnp.broadcast_to(factor, (ROWS, PAIR))
        value = value * small[gain : gain + 1, :] + small[bias + 3 : bias + 4, :]
        normed[here, :] = value.astype(LOW)


def add_sums(sums, values):
    sums[...] = jnp.zeros_like(sums)
    for n, value in enumerate(values):
        sums[n : n + 1, :] = jnp.sum(value, axis=0, keepdims=True)


def second_norm_kernel(
    bias, gain, at, unit, small, own, got, d_out, layer_out, d_second, d_ffn, sums
):
    padded, width = unit.shape
    real = d_out.shape[0]
    totals = [jnp.zeros((ROWS, width), WIDE)] * 3
    for low in range(0, padded, ROWS):
        here = slice(low, low + ROWS)
        count = min(ROWS, real - low)
        first = unit[here, :] * small[gain : gain + 1, :] + small[bias + 3 : bias + 4, :]
        ffn = own[here, :] + got[here, :].astype(WIDE) + small[bias + 4 : bias + 5, :]
        total = first + ffn
        centered = total - spread_of(total)
        factor = lax.rsqrt(spread_of(centered * centered) + NORM_EPSILON)
        value = centered * factor
        out = value * small[gain + 1 : gain + 2, :] + small[bias + 5 : bias + 6, :]
        layer_out[low : low + count, :] = out[:count].astype(LOW)
        cotangent = d_out[low : low + count, :].astype(WIDE)
        if count < ROWS:
            cotangent = jnp.concatenate(
                [cotangent, jnp.zeros((ROWS - count, width), WIDE)], axis=0
            )
        d_unit = cotangent * small[gain + 1 : gain + 2, :]
        back = factor * (d_unit - spread_of(d_unit) - value * spread_of(d_unit * value))
        d_second[here, :] = back
        rounded = back.astype(LOW)
        d_ffn[here, :] = rounded
        terms = (rounded.astype(WIDE), cotangent, cotangent * value)
        totals = [a + b for a, b in zip(totals, terms)]
    add_sums(sums, totals)


def first_back_kernel(
    gain, at, d_second, own, got, unit, scale, small, wout, d_attn_in, d_attn, mix_own, mix_sent, sums
):
    padded, width = unit.shape
    part = mix_own.shape[1]
    totals = [jnp.zeros((ROWS, width), WIDE)] * 3
    for low in range(0, padded, ROWS):
        here = slice(low, low + ROWS)
        cotangent = d_second[here, :] + own[here, :] + got[here, :].astype(WIDE)
        value = unit[here, :]
        d_unit = cotangent * small[gain : gain + 1, :]
        back = d_unit - spread_of(d_unit) - value * spread_of(d_unit * value)
        back = scale[here, :1] * back
        d_attn_in[here, :] = back
        rounded = back.astype(LOW)
        d_attn[here, :] = rounded
        terms = (rounded.astype(WIDE), cotangent, cotangent * value)
        totals = [a + b for a, b in zip(totals, terms)]
    add_sums(sums, totals)
    mixed = nt(d_attn[...], wout[...]).astype(LOW)
    first = at[T] == 0
    mix_own[...] = jnp.where(first, mixed[:, :part], mixed[:, part:])
    mix_sent[...] = jnp.where(first, mixed[:, part:], mixed[:, :part])


def rows_kernel(mem_count, at, own, got, out):
    real = out.shape[0]
    row = lax.broadcasted_iota(jnp.int32, (32, 1), 0)
    fresh = (row < mem_count) & (at[FRESH] == 1) & (at[T] == 0)
    out[:32, :] = jnp.where(fresh, 0.0, own[:32, :] + got[:32, :].astype(WIDE))
    out[32:, :] = own[32:real, :] + got[32:real, :].astype(WIDE)


def gelu_parts(pre):
    cdf = 0.5 * (1.0 + lax.erf(pre * 0.7071067811865476))
    density = jnp.exp(-0.5 * pre * pre) * 0.3989422804014327
    return pre * cdf, cdf + pre * density


def shards(
    rows_in,
    d_out,
    starts,
    lengths,
    resets,
    qkv_weight,
    out_weight,
    bias_vec,
    gains,
    mem_init,
    ffn_up,
    up_bias,
    ffn_down,
):
    half_rows, seg_count, width = rows_in.shape
    assert seg_count == 1
    dp_count, t_count = lax.axis_size("dp"), lax.axis_size("tensor")
    assert t_count == 2
    digits = digits_of(dp_count)
    x_digit, core_digit = digits[-2:]
    padded = ceil_to(half_rows, 16)
    rows = 2 * padded
    mem_count = mem_init.shape[0]
    part = HEADS // t_count * HEAD
    cols = 3 * part
    hidden_mine = ffn_up.shape[1]
    feat = bias_vec.shape[1]
    lines = qkv_weight.shape[0]
    spots = up_bias.shape[0] // feat
    doc_count = starts.shape[1]
    counts = (mem_count, bias_vec.shape[0], gains.shape[0], spots)
    edges = [sum(counts[:n]) for n in range(len(counts) + 1)]
    small_rows = tuple(zip(edges[:-1], edges[1:]))
    bias, gain = edges[1], edges[2]
    target = np.arange(part)
    target = (target // feat) * (spots * feat) + target % feat
    target = np.stack([target, np.full(part, feat)], axis=1).astype(np.int32)

    integers = [
        lax.axis_index("tensor"),
        digit_at(x_digit),
        digit_at(core_digit),
        digit_at(digits[-3]),
        lax.axis_index("dp"),
        resets[0],
        lengths[0],
    ]
    at = jnp.concatenate([jnp.stack(integers).astype(jnp.int32), starts[0]])

    kept, sent = call(
        functools.partial(columns_kernel, part, small_rows),
        [low_of(lines, cols + PAIR + width)] * 2,
        lax.axis_index("tensor").astype(jnp.int32).reshape(1),
        qkv_weight, bias_vec, gains, mem_init, up_bias.reshape(spots, feat), out_weight,
        scratch=[pltpu.VMEM((PAIR, PAIR), WIDE)],
        room=48 << 20,
    )
    got = swap_tensor(sent)
    (first_pair,) = call(pair_kernel, [low_of(2 * lines, kept.shape[1])], at, kept, got)
    rows_low = jnp.pad(rows_in[:, 0, :], ((0, padded - half_rows), (0, 0)))
    rows_other = swap_tensor(tie(rows_low, first_pair))
    first_z = spread_outer(first_pair, digits)
    first_z, rows_other = join(first_z, rows_other)
    first_x = rotate(first_z, x_digit, 1)
    up_z = spread_outer(tie(ffn_up, first_z), digits)
    first_z, first_x, up_z = join(first_z, first_x, up_z)
    wqkv, wout = assemble(at, first_z, first_x, digits, cols + PAIR)
    up_x = rotate(up_z, x_digit, 1)
    down_z = spread_outer(tie(ffn_down.T, up_z), digits)

    projected, mix_own, mix_sent, log_total, layer_in, small = call(
        functools.partial(forward_kernel, half_rows, mem_count, doc_count, bias),
        [
            low_of(rows, cols),
            low_of(padded, part),
            low_of(padded, part),
            wide_of(rows, PAIR),
            low_of(rows, width),
            wide_of(edges[-1], width),
        ],
        at, rows_low, rows_other, wqkv,
        scratch=[
            pltpu.VMEM((rows, rows), WIDE),
            pltpu.VMEM((rows, rows), WIDE),
            pltpu.VMEM((rows, rows), LOW),
            pltpu.VMEM((rows, PAIR), LOW),
        ],
    )
    mix_got = swap_tensor(mix_sent)
    mixed, unit, scale, normed_own = call(
        functools.partial(first_norm_kernel, bias, gain),
        [low_of(padded, width), wide_of(padded, width), wide_of(padded, PAIR), low_of(padded, width)],
        at, mix_own, mix_got, wout, layer_in, small,
        scratch=[pltpu.VMEM((padded, width), WIDE)],
    )

    normed_got = swap_tensor(normed_own)
    up_x, up_z, down_z = tie(up_x, mix_sent), tie(up_z, mix_sent), tie(down_z, mix_sent)
    up = assemble(at, up_z, up_x, digits)
    (up_b,) = call(
        functools.partial(up_row_kernel, edges[3], spots),
        [wide_of(ROWS, hidden_mine)], at, small, jnp.asarray(target),
    )
    down_x = rotate(down_z, x_digit, 1)
    normed_got, down_x, up_b, up = join(normed_got, down_x, up_b, up)
    down_t = assemble(at, down_z, down_x, digits)

    def feed_forward(rows):
        pre_act = nn(rows, up).reshape(-1, *up_b.shape) + up_b
        hidden, slope = (part.reshape(rows.shape[0], -1) for part in gelu_parts(pre_act))
        hidden = hidden.astype(LOW)
        return hidden, slope, nt(hidden, down_t)

    hidden_got, slope_got, ffn_sent = feed_forward(normed_got)
    ffn_sent = ffn_sent.astype(LOW)
    ffn_got = swap_tensor(ffn_sent)
    hidden_own, slope_own, ffn_own = feed_forward(tie(normed_own, ffn_sent))
    layer_out, d_second, d_ffn_own, sums_two = call(
        functools.partial(second_norm_kernel, bias, gain),
        [low_of(half_rows, width), wide_of(padded, width), low_of(padded, width), wide_of(8, width)],
        at, unit, small, ffn_own, ffn_got, d_out.reshape(half_rows, width),
    )

    d_ffn_got = swap_tensor(d_ffn_own)

    def feed_back(rows, slope):
        d_pre = (slope * nn(rows, down_t)).astype(LOW)
        return d_pre, nt(d_pre, up)

    d_pre_own, d_first_own = feed_back(d_ffn_own, slope_own)
    down_own, up_own, sums_own = call(
        own_kernel,
        [wide_of(width, hidden_mine), wide_of(width, hidden_mine), wide_of(1, hidden_mine)],
        at, d_ffn_own, hidden_own, normed_own, d_pre_own,
    )
    d_ffn_got, d_first_own, down_own, up_own = join(d_ffn_got, d_first_own, down_own, up_own)
    d_pre_got, d_first_sent = feed_back(d_ffn_got, slope_got)
    d_first_sent = d_first_sent.astype(LOW)
    d_first_got = swap_tensor(d_first_sent)

    core = lax.axis_index("dp") % 2
    outs = gradient_outs(width, hidden_mine, dp_count)
    down_grads = call(
        rest_kernel, outs, at, down_own, tie(d_ffn_got, d_first_sent), hidden_got
    )
    down_kept, down_sent = split_cores(down_grads, dp_count, core)
    down_kept, down_sent = halve(at, down_kept, rotate(down_sent, core_digit, 1))
    down_got = rotate(down_sent, x_digit, 1)
    up_sums, *up_grads = call(
        functools.partial(rest_sums_kernel, spots), [wide_of(spots, part)] + outs, at,
        up_own, sums_own, normed_got, tie(d_pre_got, d_first_sent), jnp.asarray(target),
    )
    up_kept, up_sent = split_cores(up_grads, dp_count, core)
    up_kept, up_sent = halve(at, up_kept, rotate(up_sent, core_digit, 1))
    up_got = rotate(tie(up_sent, down_got), x_digit, 1)

    d_attn_in, d_attn, d_mix_own, d_mix_sent, sums_one = call(
        functools.partial(first_back_kernel, gain),
        [
            wide_of(padded, width),
            low_of(padded, width),
            low_of(padded, part),
            low_of(padded, part),
            wide_of(8, width),
        ],
        at, d_second, d_first_own, d_first_got, unit, scale, small, wout,
    )
    d_mix_got = swap_tensor(d_mix_sent)
    out_grads = call(
        gradient_kernel, gradient_outs(width, width, dp_count), at, mixed, tie(d_attn, d_mix_sent)
    )
    out_kept, out_sent = split_cores(out_grads, dp_count, core)
    out_kept, out_sent = halve(at, out_kept, rotate(out_sent, core_digit, 1))
    out_got = rotate(tie(out_sent, up_got), x_digit, 1)
    down_kept, down_sent = outer_parts(at, [down_kept], [down_got], digits)
    d_mix_got, *down_sent = join(d_mix_got, *down_sent)
    down_got = outer_send(down_sent, digits)

    d_projected, proj_sums = call(
        functools.partial(backward_kernel, half_rows, mem_count, doc_count),
        [low_of(rows, cols), wide_of(1, cols)],
        at, projected, d_mix_own, d_mix_got, log_total,
        scratch=[
            pltpu.VMEM((rows, rows), WIDE),
            pltpu.VMEM((rows, rows), WIDE),
            pltpu.VMEM((rows, rows), WIDE),
            pltpu.VMEM((rows, rows), LOW),
            pltpu.VMEM((rows, rows), LOW),
            pltpu.VMEM((rows, part), LOW),
        ],
    )
    up_kept, up_sent = outer_parts(at, [up_kept], [up_got], digits)
    d_in_own, d_in_sent, *qkv_grads = call(
        functools.partial(projection_back_kernel, small_rows),
        [wide_of(padded, width), low_of(padded, width)]
        + gradient_outs(width, cols + PAIR, dp_count),
        at, layer_in, d_projected, proj_sums, sums_one, sums_two, up_sums, wqkv, d_attn_in,
        scratch=[pltpu.VMEM((PAIR, width), WIDE)],
    )
    qkv_kept, qkv_sent = split_cores(qkv_grads, dp_count, core)
    qkv_sent, *up_sent = join(qkv_sent, *up_sent, *down_got)[: 1 + len(up_sent)]
    qkv_kept, qkv_sent = halve(at, qkv_kept, rotate(qkv_sent, core_digit, 1))

    qkv_got = rotate(qkv_sent, x_digit, 1)
    up_got = outer_send(up_sent, digits)
    qkv_got, d_in_sent, out_got, *up_got = join(qkv_got, d_in_sent, out_got, *up_got)
    d_in_got = swap_tensor(d_in_sent)
    both_kept, both_sent = outer_parts(at, [qkv_kept, out_kept], [qkv_got, out_got], digits)
    both_got = outer_send(both_sent, digits)
    grad_ffn_down = outer_sum(down_kept, down_got, digits)
    grad_ffn_up = outer_sum(up_kept, up_got, digits)
    (grad_rows,) = call(
        functools.partial(rows_kernel, mem_count), [wide_of(half_rows, width)], at, d_in_own, d_in_got
    )
    grad_ffn_down, grad_ffn_up, grad_rows, *both_got = join(
        grad_ffn_down, grad_ffn_up, grad_rows, *both_got
    )

    if len(digits) == 3:
        parts = [both_kept[0], *[part[0] for part in both_got]]
    else:
        parts = [outer_sum(both_kept, both_got, digits)]
    mine, give = call(
        functools.partial(halves_kernel, len(parts)),
        [wide_of(lines, kept.shape[1]), low_of(lines, kept.shape[1])],
        at, *parts,
    )
    grad_qkv, grad_out_weight, grad_mem, grad_vec, grad_gains, grad_up_bias = call(
        functools.partial(finish_kernel, part, small_rows),
        [wide_of(lines, 3 * width), wide_of(lines, width)] + [wide_of(n, feat) for n in counts],
        at, mine, swap_tensor(give),
        scratch=[pltpu.VMEM((PAIR, PAIR), WIDE)],
    )
    return (
        layer_out.reshape(half_rows, 1, width),
        grad_rows.reshape(half_rows, 1, width),
        grad_qkv,
        grad_out_weight,
        grad_vec,
        grad_gains,
        grad_mem,
        grad_ffn_up,
        grad_up_bias.reshape(up_bias.shape),
        grad_ffn_down.T,
    )


def solution(mesh):
    both = ("dp", "tensor")
    in_specs = (
        P("tensor", "dp", None),
        P("tensor", "dp", None),
        P("dp", None),
        P("dp"),
        P("dp"),
        P(both, None),
        P(both, None),
        P(None, both),
        P(None, both),
        P(None, both),
        P("dp", "tensor"),
        P(both),
        P("tensor", "dp"),
    )
    out_specs = (
        P("tensor", "dp", None),
        P("tensor", "dp", None),
        P(both, None),
        P(both, None),
        P(None, both),
        P(None, both),
        P(None, both),
        P("dp", "tensor"),
        P(both),
        P("tensor", "dp"),
    )
    return jax.shard_map(shards, mesh=mesh, in_specs=in_specs, out_specs=out_specs, check_vma=False)
```

```python
import functools

import jax
import jax.numpy as jnp
import numpy as np
from jax import lax
from jax.experimental import pallas as pl
from jax.experimental.pallas import tpu as pltpu
from jax.sharding import PartitionSpec as P

HEADS = 12
HEAD = 64
NORM_EPSILON = 1e-06
LOW = jnp.bfloat16
WIDE = jnp.float32
CHUNK = 32
TILE = 384
OUT_TILE = 256
ROWS = 16
PAIR = 2 * HEAD
QUICK = pl.CostEstimate(flops=1, bytes_accessed=1, transcendentals=0)
T, X, CORE, OUTER, DP, FRESH, LENGTH, STARTS = range(8)


def ceil_to(count, unit):
    return -(-count // unit) * unit


def nn(a, b):
    return lax.dot_general(a, b, (((1,), (0,)), ((), ())), preferred_element_type=WIDE)


def nt(a, b):
    return lax.dot_general(a, b, (((1,), (1,)), ((), ())), preferred_element_type=WIDE)


def tn(a, b):
    return lax.dot_general(a, b, (((0,), (0,)), ((), ())), preferred_element_type=WIDE)


def low_of(*shape):
    return jax.ShapeDtypeStruct(shape, LOW)


def wide_of(*shape):
    return jax.ShapeDtypeStruct(shape, WIDE)


def held_bytes(array):
    rows, cols = ((1,) + tuple(array.shape))[-2:]
    lead = int(np.prod(array.shape[:-2])) if len(array.shape) > 2 else 1
    return lead * ceil_to(rows, 16) * ceil_to(cols, 128) * jnp.dtype(array.dtype).itemsize


def call(kernel, outs, at, *arrays, scratch=(), room=0):
    room += sum(held_bytes(array) for array in (*arrays, *outs))
    room += sum(held_bytes(ref) for ref in scratch)
    return pl.pallas_call(
        kernel,
        in_specs=[pl.BlockSpec(memory_space=pltpu.SMEM)]
        + [pl.BlockSpec(memory_space=pltpu.VMEM)] * len(arrays),
        out_specs=[pl.BlockSpec(memory_space=pltpu.VMEM)] * len(outs),
        out_shape=list(outs),
        scratch_shapes=list(scratch),
        compiler_params=pltpu.CompilerParams(vmem_limit_bytes=room + (3 << 20)),
        cost_estimate=QUICK,
    )(at, *arrays)


def digits_of(dp_count):
    assert dp_count % 4 == 0
    sizes = [2, 2]
    left = dp_count // 4
    while left > 1:
        size = next((s for s in (4, 2, 3) if left % s == 0), left)
        sizes.append(size)
        left //= size
    if len(sizes) == 2:
        sizes.append(1)
    digits, stride = [], 1
    for size in sizes:
        digits.append((stride, size))
        stride *= size
    return digits[::-1]


def digit_at(digit):
    stride, size = digit
    return (lax.axis_index("dp") // stride) % size


def rotate(value, digit, step):
    stride, size = digit
    pairs = []
    for at in range(lax.axis_size("dp")):
        mine = (at // stride) % size
        pairs.append((at, at + ((mine + step) % size - mine) * stride))
    return lax.ppermute(value, "dp", pairs)


def swap_tensor(value):
    return lax.ppermute(value, "tensor", [(0, 1), (1, 0)])


def tie(value, *others):
    return lax.optimization_barrier((value,) + others)[0]


join = lambda *values: lax.optimization_barrier(values)


def spread_outer(value, digits):
    for digit in reversed(digits[:-2]):
        got = [value] + [rotate(value, digit, step) for step in range(1, digit[1])]
        value = jnp.stack(got)
    return value.reshape((-1,) + value.shape[-2:])


def placer(sizes, me):
    outer, digits = sizes[:-2], []
    for size in reversed(sizes):
        digits.append(lax.rem(me, size))
        me = lax.div(me, size)
    digits = digits[::-1]

    def place_of(swap_core, swap_x, slot):
        steps = []
        for size in reversed(outer):
            steps.append(slot % size)
            slot //= size
        place = 0
        for size, digit, step in zip(outer, digits, steps[::-1]):
            place = place * size + lax.rem(digit + (size - step), size)
        x, core = digits[-2], digits[-1]
        place = place * 2 + (1 - x if swap_x else x)
        return place * 2 + (1 - core if swap_core else core)

    return place_of


def assemble_kernel(sizes, at, *refs):
    parts, whole = refs[:4], refs[4]
    cols = whole.shape[2]
    place_of = placer(sizes, at[DP])
    for swap_core in range(2):
        for swap_x in range(2):
            source = parts[2 * swap_core + swap_x]
            for slot in range(source.shape[0]):
                whole[place_of(swap_core, swap_x, slot)] = source[slot, :, :cols]


def swap_blocks(mine, x_got, digits):
    core = digits[-1]
    return [mine, x_got, rotate(mine, core, 1), rotate(x_got, core, 1)]


def assemble(at, parts, digits, cols):
    slots, rows, _ = parts[0].shape
    sizes = tuple(size for _, size in digits)
    (whole,) = call(
        functools.partial(assemble_kernel, sizes), [low_of(4 * slots, rows, cols)], at, *parts
    )
    return whole.reshape(4 * slots * rows, cols)


def assemble_out_kernel(sizes, cols, at, *refs):
    parts, gots, whole = refs[:4], refs[4:6], refs[6]
    place_of = placer(sizes, at[DP])
    first = at[T] == 0
    lines = whole.shape[1] // 2
    for swap_core in range(2):
        for swap_x in range(2):
            source, got = parts[2 * swap_core + swap_x], gots[swap_core]
            slots = source.shape[0]
            for slot in range(slots):
                mine = jnp.concatenate(
                    [source[slot, :lines, cols:], source[slot, lines:, cols:]], axis=1
                )
                other = got[swap_x * slots + slot]
                place = place_of(swap_core, swap_x, slot)
                whole[place, :lines] = jnp.where(first, mine, other)
                whole[place, lines:] = jnp.where(first, other, mine)


def columns_kernel(part, small_rows, at, weight, vectors, gains, memory, up, kept, sent, turn):
    lines, width = weight.shape[0], weight.shape[1] // 3
    first = at[T] == 0
    for pair in range(part // PAIR):
        for kind in range(3):
            low = kind * width + pair * PAIR
            a, b = weight[:, low : low + PAIR], weight[:, low + part : low + part + PAIR]
            here = (3 * pair + kind) * PAIR
            kept[:, here : here + PAIR] = jnp.where(first, a, b)
            sent[:, here : here + PAIR] = jnp.where(first, b, a)
    turn[...] = jnp.zeros_like(turn)
    for source, (low, high) in zip((memory, vectors, gains, up), small_rows):
        turn[low:high, :lines] = source[...].astype(WIDE)
    columns = turn[...].T[:lines].astype(LOW)
    kept[:, 3 * part :] = columns
    sent[:, 3 * part :] = columns


def pair_kernel(at, kept, got, out, pair):
    lines, cols = kept.shape
    fold = out.shape[1] // 2
    first = at[T] == 0
    pair[:lines, :cols] = jnp.where(first, kept[...], got[...])
    pair[lines:, :cols] = jnp.where(first, got[...], kept[...])
    pair[:lines, cols:] = out[:, :fold]
    pair[lines:, cols:] = out[:, fold:]


def unfold_kernel(cols, at, mine, x_got, out):
    slots, lines, fold = mine.shape[0], out.shape[1], out.shape[2] // 2
    for n, source in enumerate((mine, x_got)):
        for slot in range(slots):
            out[n * slots + slot, :, :fold] = source[slot, :lines, cols:]
            out[n * slots + slot, :, fold:] = source[slot, lines:, cols:]


def put_blocks(total, kept, sent, core, at):
    groups, rows, _ = kept.shape
    cols = total.shape[1]
    total = total.astype(LOW).reshape(2 * groups, rows, cols)
    second = core == 1
    for group in range(groups):
        even, odd = total[2 * group], total[2 * group + 1]
        kept[group, :, at : at + cols] = jnp.where(second, odd, even)
        sent[group] = jnp.where(second, even, odd)


def put_gradient(a, b, outs, core, own=None, tile=TILE):
    for n, low in enumerate(range(0, b.shape[1], tile)):
        total = tn(a[...], b[:, low : low + tile])
        if own is not None:
            total = total + own[:, low : low + tile]
        if len(outs) == 1:
            outs[0][:, low : low + tile] = total.astype(LOW)
        else:
            put_blocks(total, outs[0], outs[1 + n], core, low)


def gradient_outs(width, cols, dp_count, tile=TILE):
    rows = width // dp_count
    if rows % 16:
        return [low_of(width, cols)]
    tiles = [min(tile, cols - low) for low in range(0, cols, tile)]
    return [low_of(dp_count // 2, rows, n) for n in [cols] + tiles]


def swap_cores(outs, dp_count, digit):
    if len(outs) == 1:
        whole = outs[0].reshape(dp_count // 2, 2, -1, outs[0].shape[1])
        core = digit_at(digit)
        take = lambda which: lax.dynamic_index_in_dim(whole, which, 1, keepdims=False)
        outs = [take(core), take(1 - core)]
    return outs[0], [rotate(part, digit, 1) for part in outs[1:]]


def out_gradient_kernel(at, a, b, *outs):
    put_gradient(a, b, outs, at[CORE], tile=OUT_TILE)


def rows_halves_kernel(at, mine, *refs):
    got, (kept, sent) = refs[:-2], refs[-2:]
    lines = kept.shape[1]
    first = at[T] == 0
    for group in range(mine.shape[0]):
        low = 0
        for part in got:
            high = low + part.shape[2]
            total = mine[group, :, low:high].astype(WIDE) + part[group].astype(WIDE)
            a, b = total[:lines], total[lines:]
            kept[group, :, low:high] = jnp.where(first, a, b).astype(LOW)
            sent[group, :, low:high] = jnp.where(first, b, a).astype(LOW)
            low = high


def own_kernel(at, a_down, b_down, a_up, b_up, down, up, sums):
    tile = 384
    for low in range(0, b_down.shape[1], tile):
        here = slice(low, low + tile)
        down[:, here] = tn(a_down[...], b_down[:, here])
        up[:, here] = tn(a_up[...], b_up[:, here])
    sums[...] = jnp.sum(b_up[...].astype(WIDE), axis=0, keepdims=True)


def rest_kernel(at, own, a, b, *outs):
    put_gradient(a, b, outs, at[CORE], own=own)


def rest_sums_kernel(spots, at, own, own_sums, a, b, target, sums, *outs):
    put_gradient(a, b, outs, at[CORE], own=own)
    total = (own_sums[...] + jnp.sum(b[...].astype(WIDE), axis=0, keepdims=True)).astype(LOW)
    total = jnp.broadcast_to(total, (8, total.shape[1]))
    for spot in range(spots):
        sums[spot : spot + 1, :] = nt(total, one_hot(target, spot, total.shape[1]))[:1]


def one_hot(target, spot, count):
    at = lax.broadcasted_iota(jnp.int32, (target.shape[0], count), 1)
    return (at == target[:, :1] + spot * target[0, 1]).astype(WIDE).astype(LOW)


def up_row_kernel(first_row, spots, at, small, target, row):
    part = target.shape[0]
    total = jnp.zeros((8, row.shape[1]), WIDE)
    for spot in range(spots):
        line = small[first_row + spot : first_row + spot + 1, :]
        line = jnp.where(at[T] == 0, line[:, :part], line[:, part:]).astype(LOW)
        line = jnp.broadcast_to(line, (8, part))
        total = total + nn(line, one_hot(target, spot, row.shape[1]))
    row[...] = jnp.broadcast_to(total[:1], row.shape)


def halve_kernel(at, mine, *refs):
    got, (kept, sent) = refs[:-2], refs[-2:]
    x = at[X]
    for group in range(kept.shape[0]):
        for other, out in ((0, kept), (1, sent)):
            place = 2 * group + (1 - x if other else x)
            low = 0
            for part in got:
                high = low + part.shape[2]
                total = mine[place, :, low:high].astype(WIDE) + part[place].astype(WIDE)
                out[group, :, low:high] = total.astype(LOW)
                low = high


def halve(at, mine, got):
    groups, rows, cols = mine.shape
    return call(halve_kernel, [low_of(groups // 2, rows, cols)] * 2, at, mine, *got)


def parts_kernel(size, at, mine, got, *refs):
    folded, outs = refs[: len(refs) - size], refs[len(refs) - size :]
    me = at[OUTER]
    cols = mine.shape[2]
    for group in range(outs[0].shape[0]):
        for step, out in enumerate(outs):
            place = group * size + lax.rem(me + step, size)
            total = mine[place].astype(WIDE) + got[place].astype(WIDE)
            out[group, :, :cols] = total.astype(out.dtype)
            if folded:
                total = folded[0][place].astype(WIDE) + folded[1][place].astype(WIDE)
                lines, fold = total.shape[0], total.shape[1] // 2
                out[group, :lines, cols:] = total[:, :fold].astype(out.dtype)
                out[group, lines:, cols:] = total[:, fold:].astype(out.dtype)


def outer_parts(at, mine, got, digits, *folded):
    size = digits[-3][1]
    blocks, rows, cols = mine.shape
    if folded:
        cols += folded[0].shape[2] // 2
    shape = (blocks // size, rows, cols)
    outs = [wide_of(*shape)] + [low_of(*shape)] * (size - 1)
    kept, *sent = call(functools.partial(parts_kernel, size), outs, at, mine, got, *folded)
    return kept, sent


def outer_send(sent, digits):
    return [rotate(part, digits[-3], step + 1) for step, part in enumerate(sent)]


def outer_sum(kept, got, digits):
    for part in got:
        kept = kept + part.astype(WIDE)
    for digit in reversed(digits[:-3]):
        size = digit[1]
        kept = kept.reshape((-1, size) + kept.shape[1:])
        at = digit_at(digit)
        take = lambda step: lax.dynamic_index_in_dim(kept, (at + step) % size, 1, keepdims=False)
        total = take(0)
        for step in range(1, size):
            total = total + rotate(take(step).astype(LOW), digit, step).astype(WIDE)
        kept = total
    return kept[0]


def fill_mask(mask, at, half_rows, mem_count, starts):
    rows = mask.shape[0]
    padded = rows // 2

    def places(shape, axis):
        spot = lax.broadcasted_iota(jnp.int32, shape, axis)
        second = spot >= padded
        within = jnp.where(second, spot - padded, spot)
        pos = within + jnp.where(second, half_rows, 0) - mem_count
        doc = jnp.zeros(shape, jnp.int32)
        for i in range(starts):
            doc = doc + (at[STARTS + i] <= pos).astype(jnp.int32)
        return within < half_rows, pos, doc

    _, q_pos, q_doc = places((rows, 1), 0)
    real, k_pos, k_doc = places((1, rows), 1)
    key_ok = real & (k_pos < at[LENGTH])
    for low in range(0, rows, CHUNK):
        qp, qd = q_pos[low : low + CHUNK], q_doc[low : low + CHUNK]
        same = (qd == k_doc) | (qp < 0) | (k_pos < 0)
        mask[low : low + CHUNK, :] = jnp.where(same & key_ok, 0.0, -1e9)


def lanes(pair, count):
    return pl.ds(pl.multiple_of(pair * count, PAIR), count)


def forward_kernel(
    half_rows, mem_count, starts, first_bias,
    at, own, other, w, qkv, mix_own, mix_sent, lse, x, small, mask, s, p, mixed,
):
    rows, padded = x.shape[0], own.shape[0]
    t = at[T]
    part = mix_own.shape[1]
    fill_mask(mask, at, half_rows, mem_count, starts)
    lse[...] = jnp.zeros_like(lse)
    small[...] = w[:, 3 * part :].astype(WIDE).T[: small.shape[0]]
    x[pl.ds(pl.multiple_of(t * padded, 16), padded), :] = own[...]
    x[pl.ds(pl.multiple_of((1 - t) * padded, 16), padded), :] = other[...]
    row = lax.broadcasted_iota(jnp.int32, (32, 1), 0)
    fresh = (row < mem_count) & (at[FRESH] == 1)
    x[:32, :] = jnp.where(fresh, small[:32, :], x[:32, :].astype(WIDE)).astype(LOW)
    lane = lax.broadcasted_iota(jnp.int32, (1, PAIR), 1)
    scale = jnp.where(lax.broadcasted_iota(jnp.int32, (1, 3 * PAIR), 1) < PAIR, 0.125, 1.0)

    def one_pair(pair, _):
        here = pl.ds(pl.multiple_of(t * part + pair * PAIR, PAIR), PAIR)
        q_bias = small[first_bias : first_bias + 1, here]
        v_bias = small[first_bias + 1 : first_bias + 2, here]
        bias = jnp.concatenate([q_bias, jnp.zeros_like(q_bias), v_bias], axis=1)
        got = (nn(x[...], w[:, lanes(pair, 3 * PAIR)]) + bias).astype(LOW)
        got = (got.astype(WIDE) * scale).astype(LOW)
        qkv[:, lanes(pair, 3 * PAIR)] = got
        keys, values = got[:, PAIR : 2 * PAIR], got[:, 2 * PAIR :]
        for h in range(2):
            mine = (lane < HEAD) if h == 0 else (lane >= HEAD)
            s[...] = nt(jnp.where(mine, got[:, :PAIR], jnp.zeros((), LOW)), keys)

            def body(i, _):
                here = pl.ds(pl.multiple_of(i * CHUNK, CHUNK), CHUNK)
                v = s[here, :] + mask[here, :]
                top = jnp.max(v, axis=-1, keepdims=True)
                e = jnp.exp(v - top)
                total = jnp.sum(e, axis=-1, keepdims=True)
                p[here, :] = (e * (1.0 / total)).astype(LOW)
                spot = lane == 2 * pair + h
                lse[here, :] = jnp.where(spot, top + jnp.log(total), lse[here, :])
                return 0

            lax.fori_loop(0, rows // CHUNK, body, 0, unroll=True)
            out = nn(p[...], values).astype(LOW)
            if h == 0:
                mixed[...] = out
            else:
                mixed[...] = jnp.where(mine, out, mixed[...])
        mix_own[:, lanes(pair, PAIR)] = mixed[pl.ds(pl.multiple_of(t * padded, 16), padded), :]
        mix_sent[:, lanes(pair, PAIR)] = mixed[
            pl.ds(pl.multiple_of((1 - t) * padded, 16), padded), :
        ]
        return 0

    lax.fori_loop(0, part // PAIR, one_pair, 0)


def backward_kernel(
    half_rows, mem_count, starts, at, qkv, own, got, lse, dproj, sums, mask, s, dp, p, ds, dmix
):
    rows, padded = qkv.shape[0], own.shape[0]
    part = own.shape[1]
    t = at[T]
    fill_mask(mask, at, half_rows, mem_count, starts)
    dmix[pl.ds(pl.multiple_of(t * padded, 16), padded), :] = own[...]
    dmix[pl.ds(pl.multiple_of((1 - t) * padded, 16), padded), :] = got[...]
    lane = lax.broadcasted_iota(jnp.int32, (1, PAIR), 1)
    zero = jnp.zeros((), LOW)

    def one_pair(pair, _):
        here = lanes(pair, 3 * PAIR)
        whole = qkv[:, here]
        keys, values = whole[:, PAIR : 2 * PAIR], whole[:, 2 * PAIR :]
        dm_pair = dmix[:, lanes(pair, PAIR)]
        parts = []
        for h in range(2):
            mine = (lane < HEAD) if h == 0 else (lane >= HEAD)
            q = jnp.where(mine, whole[:, :PAIR], zero)
            dm = jnp.where(mine, dm_pair, zero)
            s[...] = nt(q, keys)
            dp[...] = nt(dm, values)

            def body(i, _):
                here = pl.ds(pl.multiple_of(i * CHUNK, CHUNK), CHUNK)
                spot = lane == 2 * pair + h
                stat = jnp.sum(jnp.where(spot, lse[here, :], 0.0), axis=-1, keepdims=True)
                e = jnp.exp(s[here, :] + mask[here, :] - stat)
                d = dp[here, :]
                dot = jnp.sum(e * d, axis=-1, keepdims=True)
                p[here, :] = e.astype(LOW)
                ds[here, :] = (e * (d - dot)).astype(LOW)
                return 0

            lax.fori_loop(0, rows // CHUNK, body, 0, unroll=True)
            parts.append((nn(ds[...], keys) * 0.125, tn(ds[...], q), tn(p[...], dm)))
        dq = jnp.where(lane < HEAD, parts[0][0], parts[1][0])
        dk, dv = parts[0][1] + parts[1][1], parts[0][2] + parts[1][2]
        out = jnp.concatenate([dq, dk, dv], axis=1).astype(LOW)
        dproj[:, here] = out
        sums[:, here] = jnp.sum(out.astype(WIDE), axis=0, keepdims=True)
        return 0

    lax.fori_loop(0, part // PAIR, one_pair, 0)


def projection_back_kernel(
    small_rows, at, layer_in, d_projected, proj_sums, sums_one, sums_two, up_sums, wqkv, d_attn,
    *outs,
):
    d_own, d_sent = outs[:2]
    grads, turn = outs[2:-1], outs[-1]
    padded, part = d_own.shape[0], up_sums.shape[1]
    cols = d_projected.shape[1]
    t = at[T]
    first = t == 0
    half = lambda which: d_projected[pl.ds(pl.multiple_of(which * padded, 16), padded), :]
    weights = wqkv[:, :cols]
    own = nt(half(t), weights)
    other = nt(half(1 - t), weights)
    d_own[...] = d_attn[...] + own
    d_sent[...] = other.astype(LOW)
    turn[...] = jnp.zeros_like(turn)
    (m0, m1), (v0, _), (g0, _), (u0, _) = small_rows
    count = m1 - m0
    memory = jnp.where(first, own[:count] + d_attn[:count, :], other[:count])
    turn[m0:m1, :] = jnp.where(at[FRESH] == 1, memory, 0.0)
    sums = [
        jnp.concatenate(
            [proj_sums[:, (3 * p + k) * PAIR : (3 * p + k + 1) * PAIR] for p in range(part // PAIR)],
            axis=1,
        )
        for k in (0, 2)
    ]
    for value, low in zip(sums + [up_sums[...]], (v0, v0 + 1, u0)):
        high = low + value.shape[0]
        turn[low:high, :part] = jnp.where(first, value, 0.0)
        turn[low:high, part:] = jnp.where(first, 0.0, value)
    turn[v0 + 2 : v0 + 4, :] = sums_one[0:2, :]
    turn[v0 + 4 : v0 + 6, :] = sums_two[0:2, :]
    turn[g0 : g0 + 1, :] = sums_one[2:3, :]
    turn[g0 + 1 : g0 + 2, :] = sums_two[2:3, :]
    small = turn[...].T
    put_gradient(layer_in, d_projected, grads, at[CORE])
    if len(grads) == 1:
        grads[0][:, cols:] = small.astype(LOW)
    else:
        put_blocks(small, grads[0], grads[-1], at[CORE], cols)


def halves_kernel(count, at, *refs):
    parts, (mine, give, out) = refs[:count], refs[count:]
    lines, cols = mine.shape
    fold = out.shape[1] // 2
    total = parts[0][...]
    for part in parts[1:]:
        total = total + part[...].astype(WIDE)
    first = at[T] == 0
    low, high = total[:lines, :cols], total[lines:, :cols]
    mine[...] = jnp.where(first, low, high)
    give[...] = jnp.where(first, high, low).astype(LOW)
    out[:, :fold] = total[:lines, cols:]
    out[:, fold:] = total[lines:, cols:]


def finish_kernel(part, small_rows, at, mine, got, qkv, memory, vectors, gains, up, turn):
    lines = mine.shape[0]
    cols, width = 3 * part, 2 * part
    first = at[T] == 0
    for pair in range(part // PAIR):
        for kind in range(3):
            here = (3 * pair + kind) * PAIR
            a = mine[:, here : here + PAIR]
            b = got[:, here : here + PAIR].astype(WIDE)
            low = kind * width + pair * PAIR
            qkv[:, low : low + PAIR] = jnp.where(first, a, b)
            qkv[:, low + part : low + part + PAIR] = jnp.where(first, b, a)
    turn[...] = jnp.zeros_like(turn)
    turn[:lines, :] = mine[:, cols : cols + PAIR] + got[:, cols : cols + PAIR].astype(WIDE)
    small = turn[...].T
    for target, (low, high) in zip((memory, vectors, gains, up), small_rows):
        target[...] = small[low:high, :lines]


def spread_of(v):
    return jnp.mean(v, axis=-1, keepdims=True)


def first_norm_kernel(bias, gain, at, own, got, wout, layer_in, small, mixed, unit, scale, normed, s):
    padded, part = own.shape
    first = at[T] == 0
    mixed[:, :part] = jnp.where(first, own[...], got[...])
    mixed[:, part:] = jnp.where(first, got[...], own[...])
    s[...] = nn(mixed[...], wout[...])
    for low in range(0, padded, ROWS):
        here = slice(low, low + ROWS)
        rows = layer_in[pl.ds(pl.multiple_of(at[T] * padded + low, ROWS), ROWS), :]
        total = rows.astype(WIDE) + (s[here, :] + small[bias + 2 : bias + 3, :])
        centered = total - spread_of(total)
        factor = lax.rsqrt(spread_of(centered * centered) + NORM_EPSILON)
        value = centered * factor
        unit[here, :] = value
        scale[here, :] = jnp.broadcast_to(factor, (ROWS, PAIR))
        value = value * small[gain : gain + 1, :] + small[bias + 3 : bias + 4, :]
        normed[here, :] = value.astype(LOW)


def add_sums(sums, values):
    sums[...] = jnp.zeros_like(sums)
    for n, value in enumerate(values):
        sums[n : n + 1, :] = jnp.sum(value, axis=0, keepdims=True)


def second_norm_kernel(
    bias, gain, at, unit, small, own, got, d_out, layer_out, d_second, d_ffn, sums
):
    padded, width = unit.shape
    real = d_out.shape[0]
    totals = [jnp.zeros((ROWS, width), WIDE)] * 3
    for low in range(0, padded, ROWS):
        here = slice(low, low + ROWS)
        count = min(ROWS, real - low)
        first = unit[here, :] * small[gain : gain + 1, :] + small[bias + 3 : bias + 4, :]
        ffn = own[here, :] + got[here, :].astype(WIDE) + small[bias + 4 : bias + 5, :]
        total = first + ffn
        centered = total - spread_of(total)
        factor = lax.rsqrt(spread_of(centered * centered) + NORM_EPSILON)
        value = centered * factor
        out = value * small[gain + 1 : gain + 2, :] + small[bias + 5 : bias + 6, :]
        layer_out[low : low + count, :] = out[:count].astype(LOW)
        cotangent = d_out[low : low + count, :].astype(WIDE)
        if count < ROWS:
            cotangent = jnp.concatenate(
                [cotangent, jnp.zeros((ROWS - count, width), WIDE)], axis=0
            )
        d_unit = cotangent * small[gain + 1 : gain + 2, :]
        back = factor * (d_unit - spread_of(d_unit) - value * spread_of(d_unit * value))
        d_second[here, :] = back
        rounded = back.astype(LOW)
        d_ffn[here, :] = rounded
        terms = (rounded.astype(WIDE), cotangent, cotangent * value)
        totals = [a + b for a, b in zip(totals, terms)]
    add_sums(sums, totals)


def first_back_kernel(
    gain, at, d_second, own, got, unit, scale, small, wout, d_attn_in, d_attn, mix_own, mix_sent, sums
):
    padded, width = unit.shape
    part = mix_own.shape[1]
    totals = [jnp.zeros((ROWS, width), WIDE)] * 3
    for low in range(0, padded, ROWS):
        here = slice(low, low + ROWS)
        cotangent = d_second[here, :] + own[here, :] + got[here, :].astype(WIDE)
        value = unit[here, :]
        d_unit = cotangent * small[gain : gain + 1, :]
        back = d_unit - spread_of(d_unit) - value * spread_of(d_unit * value)
        back = scale[here, :1] * back
        d_attn_in[here, :] = back
        rounded = back.astype(LOW)
        d_attn[here, :] = rounded
        terms = (rounded.astype(WIDE), cotangent, cotangent * value)
        totals = [a + b for a, b in zip(totals, terms)]
    add_sums(sums, totals)
    mixed = nt(d_attn[...], wout[...]).astype(LOW)
    first = at[T] == 0
    mix_own[...] = jnp.where(first, mixed[:, :part], mixed[:, part:])
    mix_sent[...] = jnp.where(first, mixed[:, part:], mixed[:, :part])


def rows_kernel(mem_count, at, own, got, out):
    real = out.shape[0]
    row = lax.broadcasted_iota(jnp.int32, (32, 1), 0)
    fresh = (row < mem_count) & (at[FRESH] == 1) & (at[T] == 0)
    out[:32, :] = jnp.where(fresh, 0.0, own[:32, :] + got[:32, :].astype(WIDE))
    out[32:, :] = own[32:real, :] + got[32:real, :].astype(WIDE)


def gelu_parts(pre):
    cdf = 0.5 * (1.0 + lax.erf(pre * 0.7071067811865476))
    density = jnp.exp(-0.5 * pre * pre) * 0.3989422804014327
    return pre * cdf, cdf + pre * density


def shards(
    rows_in,
    d_out,
    starts,
    lengths,
    resets,
    qkv_weight,
    out_weight,
    bias_vec,
    gains,
    mem_init,
    ffn_up,
    up_bias,
    ffn_down,
):
    half_rows, seg_count, width = rows_in.shape
    assert seg_count == 1
    dp_count, t_count = lax.axis_size("dp"), lax.axis_size("tensor")
    assert t_count == 2
    digits = digits_of(dp_count)
    x_digit, core_digit = digits[-2:]
    padded = ceil_to(half_rows, 16)
    rows = 2 * padded
    mem_count = mem_init.shape[0]
    part = HEADS // t_count * HEAD
    cols = 3 * part
    hidden_mine = ffn_up.shape[1]
    feat = bias_vec.shape[1]
    lines = qkv_weight.shape[0]
    spots = up_bias.shape[0] // feat
    doc_count = starts.shape[1]
    counts = (mem_count, bias_vec.shape[0], gains.shape[0], spots)
    edges = [sum(counts[:n]) for n in range(len(counts) + 1)]
    small_rows = tuple(zip(edges[:-1], edges[1:]))
    bias, gain = edges[1], edges[2]
    target = np.arange(part)
    target = (target // feat) * (spots * feat) + target % feat
    target = np.stack([target, np.full(part, feat)], axis=1).astype(np.int32)

    integers = [
        lax.axis_index("tensor"),
        digit_at(x_digit),
        digit_at(core_digit),
        digit_at(digits[-3]),
        lax.axis_index("dp"),
        resets[0],
        lengths[0],
    ]
    at = jnp.concatenate([jnp.stack(integers).astype(jnp.int32), starts[0]])

    kept, sent = call(
        functools.partial(columns_kernel, part, small_rows),
        [low_of(lines, cols + PAIR)] * 2,
        lax.axis_index("tensor").astype(jnp.int32).reshape(1),
        qkv_weight, bias_vec, gains, mem_init, up_bias.reshape(spots, feat),
        scratch=[pltpu.VMEM((PAIR, PAIR), WIDE)],
        room=48 << 20,
    )
    first_cols = cols + PAIR + part
    (first_pair,) = call(
        pair_kernel, [low_of(2 * lines, first_cols)], at, kept, swap_tensor(sent), out_weight
    )
    rows_low = jnp.pad(rows_in[:, 0, :], ((0, padded - half_rows), (0, 0)))
    rows_other = swap_tensor(tie(rows_low, first_pair))
    first_z = spread_outer(first_pair, digits)
    first_z, rows_other = join(first_z, rows_other)
    first_x = rotate(first_z, x_digit, 1)
    up_z = spread_outer(tie(ffn_up, first_z), digits)
    down_in = tie(ffn_down.T, up_z)
    first_z, first_x, up_z = join(first_z, first_x, up_z)
    first_parts = swap_blocks(first_z, first_x, digits)
    wqkv = assemble(at, first_parts, digits, cols + PAIR)
    (out_sent,) = call(
        functools.partial(unfold_kernel, cols + PAIR),
        [low_of(dp_count // 2, lines, width)], at, first_z, first_x,
    )
    out_got = swap_tensor(out_sent)
    up_x = rotate(up_z, x_digit, 1)
    down_z = spread_outer(down_in, digits)

    projected, mix_own, mix_sent, log_total, layer_in, small = call(
        functools.partial(forward_kernel, half_rows, mem_count, doc_count, bias),
        [
            low_of(rows, cols),
            low_of(padded, part),
            low_of(padded, part),
            wide_of(rows, PAIR),
            low_of(rows, width),
            wide_of(edges[-1], width),
        ],
        at, rows_low, rows_other, wqkv,
        scratch=[
            pltpu.VMEM((rows, rows), WIDE),
            pltpu.VMEM((rows, rows), WIDE),
            pltpu.VMEM((rows, rows), LOW),
            pltpu.VMEM((rows, PAIR), LOW),
        ],
    )
    mix_got = swap_tensor(mix_sent)
    out_got = tie(out_got, mix_sent)
    (wout,) = call(
        functools.partial(
            assemble_out_kernel, tuple(size for _, size in digits), cols + PAIR
        ),
        [low_of(dp_count, 2 * lines, width)],
        at, *first_parts, out_got, rotate(out_got, core_digit, 1),
    )
    wout = wout.reshape(width, width)
    mixed, unit, scale, normed_own = call(
        functools.partial(first_norm_kernel, bias, gain),
        [low_of(padded, width), wide_of(padded, width), wide_of(padded, PAIR), low_of(padded, width)],
        at, mix_own, mix_got, wout, layer_in, small,
        scratch=[pltpu.VMEM((padded, width), WIDE)],
    )

    normed_got = swap_tensor(normed_own)
    up_x, up_z, down_z = tie(up_x, mix_sent), tie(up_z, mix_sent), tie(down_z, mix_sent)
    up = assemble(at, swap_blocks(up_z, up_x, digits), digits, hidden_mine)
    (up_b,) = call(
        functools.partial(up_row_kernel, edges[3], spots),
        [wide_of(ROWS, hidden_mine)], at, small, jnp.asarray(target),
    )
    down_x = rotate(down_z, x_digit, 1)
    normed_got, down_x, up_b, up = join(normed_got, down_x, up_b, up)
    down_t = assemble(at, swap_blocks(down_z, down_x, digits), digits, hidden_mine)

    def feed_forward(rows):
        pre_act = nn(rows, up).reshape(-1, *up_b.shape) + up_b
        hidden, slope = (part.reshape(rows.shape[0], -1) for part in gelu_parts(pre_act))
        hidden = hidden.astype(LOW)
        return hidden, slope, nt(hidden, down_t)

    hidden_got, slope_got, ffn_sent = feed_forward(normed_got)
    ffn_sent = ffn_sent.astype(LOW)
    ffn_got = swap_tensor(ffn_sent)
    hidden_own, slope_own, ffn_own = feed_forward(tie(normed_own, ffn_sent))
    layer_out, d_second, d_ffn_own, sums_two = call(
        functools.partial(second_norm_kernel, bias, gain),
        [low_of(half_rows, width), wide_of(padded, width), low_of(padded, width), wide_of(8, width)],
        at, unit, small, ffn_own, ffn_got, d_out.reshape(half_rows, width),
    )

    d_ffn_got = swap_tensor(d_ffn_own)

    def feed_back(rows, slope):
        d_pre = (slope * nn(rows, down_t)).astype(LOW)
        return d_pre, nt(d_pre, up)

    d_pre_own, d_first_own = feed_back(d_ffn_own, slope_own)
    down_own, up_own, sums_own = call(
        own_kernel,
        [wide_of(width, hidden_mine), wide_of(width, hidden_mine), wide_of(1, hidden_mine)],
        at, d_ffn_own, hidden_own, normed_own, d_pre_own,
    )
    d_ffn_got, d_first_own, down_own, up_own = join(d_ffn_got, d_first_own, down_own, up_own)
    d_pre_got, d_first_sent = feed_back(d_ffn_got, slope_got)
    d_first_sent = d_first_sent.astype(LOW)
    d_first_got = swap_tensor(d_first_sent)

    outs = gradient_outs(width, hidden_mine, dp_count)
    down_grads = call(
        rest_kernel, outs, at, down_own, tie(d_ffn_got, d_first_sent), hidden_got
    )
    down_kept, down_sent = halve(at, *swap_cores(down_grads, dp_count, core_digit))
    down_got = rotate(down_sent, x_digit, 1)
    up_sums, *up_grads = call(
        functools.partial(rest_sums_kernel, spots), [wide_of(spots, part)] + outs, at,
        up_own, sums_own, normed_got, tie(d_pre_got, down_sent), jnp.asarray(target),
    )
    up_kept, up_sent = halve(at, *swap_cores(up_grads, dp_count, core_digit))

    d_attn_in, d_attn, d_mix_own, d_mix_sent, sums_one = call(
        functools.partial(first_back_kernel, gain),
        [
            wide_of(padded, width),
            low_of(padded, width),
            low_of(padded, part),
            low_of(padded, part),
            wide_of(8, width),
        ],
        at, d_second, d_first_own, d_first_got, unit, scale, small, wout,
    )
    d_mix_got = swap_tensor(d_mix_sent)
    out_grads = call(
        out_gradient_kernel, gradient_outs(width, width, dp_count, OUT_TILE),
        at, mixed, tie(d_attn, d_mix_sent),
    )
    out_kept, out_parts = swap_cores(out_grads, dp_count, core_digit)
    out_kept, out_sent = call(
        rows_halves_kernel, [low_of(dp_count // 2, lines, width)] * 2, at, out_kept, *out_parts
    )
    down_kept, down_sent = outer_parts(at, down_kept, down_got, digits)
    d_mix_got, out_sent, up_sent, *down_sent = join(d_mix_got, out_sent, up_sent, *down_sent)
    down_got = outer_send(down_sent, digits)
    out_got = swap_tensor(out_sent)
    up_got = rotate(up_sent, x_digit, 1)

    d_projected, proj_sums = call(
        functools.partial(backward_kernel, half_rows, mem_count, doc_count),
        [low_of(rows, cols), wide_of(1, cols)],
        at, projected, d_mix_own, d_mix_got, log_total,
        scratch=[
            pltpu.VMEM((rows, rows), WIDE),
            pltpu.VMEM((rows, rows), WIDE),
            pltpu.VMEM((rows, rows), WIDE),
            pltpu.VMEM((rows, rows), LOW),
            pltpu.VMEM((rows, rows), LOW),
            pltpu.VMEM((rows, part), LOW),
        ],
    )
    up_kept, up_sent = outer_parts(at, up_kept, up_got, digits)
    d_in_own, d_in_sent, *qkv_grads = call(
        functools.partial(projection_back_kernel, small_rows),
        [wide_of(padded, width), low_of(padded, width)]
        + gradient_outs(width, cols + PAIR, dp_count),
        at, layer_in, d_projected, proj_sums, sums_one, sums_two, up_sums, wqkv, d_attn_in,
        scratch=[pltpu.VMEM((PAIR, width), WIDE)],
    )
    out_got, *qkv_grads = join(out_got, *qkv_grads, *down_got)[: 1 + len(qkv_grads)]
    out_kept, out_sent = halve(at, out_kept, [out_got])
    out_got = rotate(out_sent, x_digit, 1)
    qkv_kept, qkv_sent = halve(at, *swap_cores(qkv_grads, dp_count, core_digit))

    qkv_sent, *up_sent = join(qkv_sent, *up_sent)
    qkv_got = rotate(qkv_sent, x_digit, 1)
    up_got = outer_send(up_sent, digits)
    qkv_got, d_in_sent, out_got, *up_got = join(qkv_got, d_in_sent, out_got, *up_got)
    d_in_got = swap_tensor(d_in_sent)
    both_kept, both_sent = outer_parts(
        at, qkv_kept, qkv_got, digits, out_kept, out_got
    )
    both_got = outer_send(both_sent, digits)
    grad_ffn_down = outer_sum(down_kept, down_got, digits)
    grad_ffn_up = outer_sum(up_kept, up_got, digits)
    (grad_rows,) = call(
        functools.partial(rows_kernel, mem_count), [wide_of(half_rows, width)], at, d_in_own, d_in_got
    )
    grad_rows, *both_got = join(grad_rows, *both_got)

    if len(digits) == 3:
        parts = [both_kept[0], *[part[0] for part in both_got]]
    else:
        parts = [outer_sum(both_kept, both_got, digits)]
    mine, give, grad_out_weight = call(
        functools.partial(halves_kernel, len(parts)),
        [wide_of(lines, cols + PAIR), low_of(lines, cols + PAIR), wide_of(lines, width)],
        at, *parts,
    )
    grad_qkv, grad_mem, grad_vec, grad_gains, grad_up_bias = call(
        functools.partial(finish_kernel, part, small_rows),
        [wide_of(lines, 3 * width)] + [wide_of(n, feat) for n in counts],
        at, mine, swap_tensor(give),
        scratch=[pltpu.VMEM((PAIR, PAIR), WIDE)],
    )
    return (
        layer_out.reshape(half_rows, 1, width),
        grad_rows.reshape(half_rows, 1, width),
        grad_qkv,
        grad_out_weight,
        grad_vec,
        grad_gains,
        grad_mem,
        grad_ffn_up,
        grad_up_bias.reshape(up_bias.shape),
        grad_ffn_down.T,
    )


def solution(mesh):
    both = ("dp", "tensor")
    in_specs = (
        P("tensor", "dp", None),
        P("tensor", "dp", None),
        P("dp", None),
        P("dp"),
        P("dp"),
        P(both, None),
        P(both, None),
        P(None, both),
        P(None, both),
        P(None, both),
        P("dp", "tensor"),
        P(both),
        P("tensor", "dp"),
    )
    out_specs = (
        P("tensor", "dp", None),
        P("tensor", "dp", None),
        P(both, None),
        P(both, None),
        P(None, both),
        P(None, both),
        P(None, both),
        P("dp", "tensor"),
        P(both),
        P("tensor", "dp"),
    )
    return jax.shard_map(shards, mesh=mesh, in_specs=in_specs, out_specs=out_specs, check_vma=False)
```

```python
import functools

import jax
import jax.numpy as jnp
import numpy as np
from jax import lax
from jax.experimental import pallas as pl
from jax.experimental.pallas import tpu as pltpu
from jax.sharding import PartitionSpec as P

HEADS = 12
HEAD = 64
NORM_EPSILON = 1e-06
LOW = jnp.bfloat16
WIDE = jnp.float32
CHUNK = 32
FORWARD_BLOCK = 272
BACKWARD_BLOCK = 544
TILE = 384
OUT_TILE = 256
ROWS = 16
PAIR = 2 * HEAD
QUICK = pl.CostEstimate(flops=1, bytes_accessed=1, transcendentals=0)
T, X, CORE, OUTER, DP, FRESH, LENGTH, STARTS = range(8)


def ceil_to(count, unit):
    return -(-count // unit) * unit


def nn(a, b):
    return lax.dot_general(a, b, (((1,), (0,)), ((), ())), preferred_element_type=WIDE)


def nt(a, b):
    return lax.dot_general(a, b, (((1,), (1,)), ((), ())), preferred_element_type=WIDE)


def tn(a, b):
    return lax.dot_general(a, b, (((0,), (0,)), ((), ())), preferred_element_type=WIDE)


def low_of(*shape):
    return jax.ShapeDtypeStruct(shape, LOW)


def wide_of(*shape):
    return jax.ShapeDtypeStruct(shape, WIDE)


def held_bytes(array):
    rows, cols = ((1,) + tuple(array.shape))[-2:]
    lead = int(np.prod(array.shape[:-2])) if len(array.shape) > 2 else 1
    return lead * ceil_to(rows, 16) * ceil_to(cols, 128) * jnp.dtype(array.dtype).itemsize


def call(kernel, outs, at, *arrays, scratch=(), room=0):
    room += sum(held_bytes(array) for array in (*arrays, *outs))
    room += sum(held_bytes(ref) for ref in scratch)
    return pl.pallas_call(
        kernel,
        in_specs=[pl.BlockSpec(memory_space=pltpu.SMEM)]
        + [pl.BlockSpec(memory_space=pltpu.VMEM)] * len(arrays),
        out_specs=[pl.BlockSpec(memory_space=pltpu.VMEM)] * len(outs),
        out_shape=list(outs),
        scratch_shapes=list(scratch),
        compiler_params=pltpu.CompilerParams(vmem_limit_bytes=room + (3 << 20)),
        cost_estimate=QUICK,
    )(at, *arrays)


def digits_of(dp_count):
    assert dp_count % 4 == 0
    sizes = [2, 2]
    left = dp_count // 4
    while left > 1:
        size = next((s for s in (4, 2, 3) if left % s == 0), left)
        sizes.append(size)
        left //= size
    if len(sizes) == 2:
        sizes.append(1)
    digits, stride = [], 1
    for size in sizes:
        digits.append((stride, size))
        stride *= size
    return digits[::-1]


def digit_at(digit):
    stride, size = digit
    return (lax.axis_index("dp") // stride) % size


def rotate(value, digit, step):
    stride, size = digit
    pairs = []
    for at in range(lax.axis_size("dp")):
        mine = (at // stride) % size
        pairs.append((at, at + ((mine + step) % size - mine) * stride))
    return lax.ppermute(value, "dp", pairs)


def swap_tensor(value):
    return lax.ppermute(value, "tensor", [(0, 1), (1, 0)])


def tie(value, *others):
    return lax.optimization_barrier((value,) + others)[0]


join = lambda *values: lax.optimization_barrier(values)


def spread_outer(value, digits):
    for digit in reversed(digits[:-2]):
        got = [value] + [rotate(value, digit, step) for step in range(1, digit[1])]
        value = jnp.stack(got)
    return value.reshape((-1,) + value.shape[-2:])


def placer(sizes, me):
    outer, digits = sizes[:-2], []
    for size in reversed(sizes):
        digits.append(lax.rem(me, size))
        me = lax.div(me, size)
    digits = digits[::-1]

    def place_of(swap_core, swap_x, slot):
        steps = []
        for size in reversed(outer):
            steps.append(slot % size)
            slot //= size
        place = 0
        for size, digit, step in zip(outer, digits, steps[::-1]):
            place = place * size + lax.rem(digit + (size - step), size)
        x, core = digits[-2], digits[-1]
        place = place * 2 + (1 - x if swap_x else x)
        return place * 2 + (1 - core if swap_core else core)

    return place_of


def assemble_kernel(sizes, at, *refs):
    parts, whole = refs[:4], refs[4]
    cols = whole.shape[2]
    place_of = placer(sizes, at[DP])
    for swap_core in range(2):
        for swap_x in range(2):
            source = parts[2 * swap_core + swap_x]
            for slot in range(source.shape[0]):
                whole[place_of(swap_core, swap_x, slot)] = source[slot, :, :cols]


def swap_blocks(mine, x_got, digits):
    core = digits[-1]
    return [mine, x_got, rotate(mine, core, 1), rotate(x_got, core, 1)]


def assemble(at, parts, digits, cols):
    slots, rows, _ = parts[0].shape
    sizes = tuple(size for _, size in digits)
    (whole,) = call(
        functools.partial(assemble_kernel, sizes), [low_of(4 * slots, rows, cols)], at, *parts
    )
    return whole.reshape(4 * slots * rows, cols)


def assemble_out_kernel(sizes, cols, at, *refs):
    parts, gots, whole = refs[:4], refs[4:6], refs[6]
    place_of = placer(sizes, at[DP])
    first = at[T] == 0
    lines = whole.shape[1] // 2
    for swap_core in range(2):
        for swap_x in range(2):
            source, got = parts[2 * swap_core + swap_x], gots[swap_core]
            slots = source.shape[0]
            for slot in range(slots):
                mine = jnp.concatenate(
                    [source[slot, :lines, cols:], source[slot, lines:, cols:]], axis=1
                )
                other = got[swap_x * slots + slot]
                place = place_of(swap_core, swap_x, slot)
                whole[place, :lines] = jnp.where(first, mine, other)
                whole[place, lines:] = jnp.where(first, other, mine)


def columns_kernel(part, small_rows, at, weight, vectors, gains, memory, up, kept, sent, turn):
    lines, width = weight.shape[0], weight.shape[1] // 3
    first = at[T] == 0
    for pair in range(part // PAIR):
        for kind in range(3):
            low = kind * width + pair * PAIR
            a, b = weight[:, low : low + PAIR], weight[:, low + part : low + part + PAIR]
            here = (3 * pair + kind) * PAIR
            kept[:, here : here + PAIR] = jnp.where(first, a, b)
            sent[:, here : here + PAIR] = jnp.where(first, b, a)
    turn[...] = jnp.zeros_like(turn)
    for source, (low, high) in zip((memory, vectors, gains, up), small_rows):
        turn[low:high, :lines] = source[...].astype(WIDE)
    columns = turn[...].T[:lines].astype(LOW)
    kept[:, 3 * part :] = columns
    sent[:, 3 * part :] = columns


def pair_kernel(at, kept, got, out, pair):
    lines, cols = kept.shape
    fold = out.shape[1] // 2
    first = at[T] == 0
    pair[:lines, :cols] = jnp.where(first, kept[...], got[...])
    pair[lines:, :cols] = jnp.where(first, got[...], kept[...])
    pair[:lines, cols:] = out[:, :fold]
    pair[lines:, cols:] = out[:, fold:]


def unfold_kernel(cols, at, mine, x_got, out):
    slots, lines, fold = mine.shape[0], out.shape[1], out.shape[2] // 2
    for n, source in enumerate((mine, x_got)):
        for slot in range(slots):
            out[n * slots + slot, :, :fold] = source[slot, :lines, cols:]
            out[n * slots + slot, :, fold:] = source[slot, lines:, cols:]


def put_blocks(total, kept, sent, core, at):
    groups, rows, _ = kept.shape
    cols = total.shape[1]
    total = total.astype(LOW).reshape(2 * groups, rows, cols)
    second = core == 1
    for group in range(groups):
        even, odd = total[2 * group], total[2 * group + 1]
        kept[group, :, at : at + cols] = jnp.where(second, odd, even)
        sent[group] = jnp.where(second, even, odd)


def put_gradient(a, b, outs, core, own=None, tile=TILE):
    for n, low in enumerate(range(0, b.shape[1], tile)):
        total = tn(a[...], b[:, low : low + tile])
        if own is not None:
            total = total + own[:, low : low + tile]
        if len(outs) == 1:
            outs[0][:, low : low + tile] = total.astype(LOW)
        else:
            put_blocks(total, outs[0], outs[1 + n], core, low)


def gradient_outs(width, cols, dp_count, tile=TILE):
    rows = width // dp_count
    if rows % 16:
        return [low_of(width, cols)]
    tiles = [min(tile, cols - low) for low in range(0, cols, tile)]
    return [low_of(dp_count // 2, rows, n) for n in [cols] + tiles]


def swap_cores(outs, dp_count, digit):
    if len(outs) == 1:
        whole = outs[0].reshape(dp_count // 2, 2, -1, outs[0].shape[1])
        core = digit_at(digit)
        take = lambda which: lax.dynamic_index_in_dim(whole, which, 1, keepdims=False)
        outs = [take(core), take(1 - core)]
    return outs[0], [rotate(part, digit, 1) for part in outs[1:]]


def out_gradient_kernel(at, a, b, *outs):
    put_gradient(a, b, outs, at[CORE], tile=OUT_TILE)


def rows_halves_kernel(at, mine, *refs):
    got, (kept, sent) = refs[:-2], refs[-2:]
    lines = kept.shape[1]
    first = at[T] == 0
    for group in range(mine.shape[0]):
        low = 0
        for part in got:
            high = low + part.shape[2]
            total = mine[group, :, low:high].astype(WIDE) + part[group].astype(WIDE)
            a, b = total[:lines], total[lines:]
            kept[group, :, low:high] = jnp.where(first, a, b).astype(LOW)
            sent[group, :, low:high] = jnp.where(first, b, a).astype(LOW)
            low = high


def own_kernel(at, a_down, b_down, a_up, b_up, down, up, sums):
    tile = 384
    for low in range(0, b_down.shape[1], tile):
        here = slice(low, low + tile)
        down[:, here] = tn(a_down[...], b_down[:, here])
        up[:, here] = tn(a_up[...], b_up[:, here])
    sums[...] = jnp.sum(b_up[...].astype(WIDE), axis=0, keepdims=True)


def rest_kernel(at, own, a, b, *outs):
    put_gradient(a, b, outs, at[CORE], own=own)


def rest_sums_kernel(spots, at, own, own_sums, a, b, target, sums, *outs):
    put_gradient(a, b, outs, at[CORE], own=own)
    total = (own_sums[...] + jnp.sum(b[...].astype(WIDE), axis=0, keepdims=True)).astype(LOW)
    total = jnp.broadcast_to(total, (8, total.shape[1]))
    for spot in range(spots):
        sums[spot : spot + 1, :] = nt(total, one_hot(target, spot, total.shape[1]))[:1]


def one_hot(target, spot, count):
    at = lax.broadcasted_iota(jnp.int32, (target.shape[0], count), 1)
    return (at == target[:, :1] + spot * target[0, 1]).astype(WIDE).astype(LOW)


def up_row_kernel(first_row, spots, at, small, target, row):
    part = target.shape[0]
    total = jnp.zeros((8, row.shape[1]), WIDE)
    for spot in range(spots):
        line = small[first_row + spot : first_row + spot + 1, :]
        line = jnp.where(at[T] == 0, line[:, :part], line[:, part:]).astype(LOW)
        line = jnp.broadcast_to(line, (8, part))
        total = total + nn(line, one_hot(target, spot, row.shape[1]))
    row[...] = jnp.broadcast_to(total[:1], row.shape)


def halve_kernel(at, mine, *refs):
    got, (kept, sent) = refs[:-2], refs[-2:]
    x = at[X]
    for group in range(kept.shape[0]):
        for other, out in ((0, kept), (1, sent)):
            place = 2 * group + (1 - x if other else x)
            low = 0
            for part in got:
                high = low + part.shape[2]
                total = mine[place, :, low:high].astype(WIDE) + part[place].astype(WIDE)
                out[group, :, low:high] = total.astype(LOW)
                low = high


def halve(at, mine, got):
    groups, rows, cols = mine.shape
    return call(halve_kernel, [low_of(groups // 2, rows, cols)] * 2, at, mine, *got)


def parts_kernel(size, at, mine, got, *refs):
    folded, outs = refs[: len(refs) - size], refs[len(refs) - size :]
    me = at[OUTER]
    cols = mine.shape[2]
    for group in range(outs[0].shape[0]):
        for step, out in enumerate(outs):
            place = group * size + lax.rem(me + step, size)
            total = mine[place].astype(WIDE) + got[place].astype(WIDE)
            out[group, :, :cols] = total.astype(out.dtype)
            if folded:
                total = folded[0][place].astype(WIDE) + folded[1][place].astype(WIDE)
                lines, fold = total.shape[0], total.shape[1] // 2
                out[group, :lines, cols:] = total[:, :fold].astype(out.dtype)
                out[group, lines:, cols:] = total[:, fold:].astype(out.dtype)


def outer_parts(at, mine, got, digits, *folded):
    size = digits[-3][1]
    blocks, rows, cols = mine.shape
    if folded:
        cols += folded[0].shape[2] // 2
    shape = (blocks // size, rows, cols)
    outs = [wide_of(*shape)] + [low_of(*shape)] * (size - 1)
    kept, *sent = call(functools.partial(parts_kernel, size), outs, at, mine, got, *folded)
    return kept, sent


def far_kernel(at, mine, got, kept, sent):
    me = at[OUTER]
    pair = lax.bitwise_xor(me, 1)
    for group in range(kept.shape[0] // 2):
        for n, block in enumerate((me, pair)):
            for out, place in ((kept, block), (sent, lax.bitwise_xor(block, 2))):
                spot = 4 * group + place
                total = mine[spot].astype(WIDE) + got[spot].astype(WIDE)
                out[2 * group + n] = total.astype(out.dtype)


def near_kernel(at, mine, got, kept, sent):
    for group in range(kept.shape[0]):
        kept[group] = mine[2 * group] + got[2 * group].astype(WIDE)
        total = mine[2 * group + 1] + got[2 * group + 1].astype(WIDE)
        sent[group] = total.astype(LOW)


def far_parts(at, mine, got, digits):
    assert digits[-3][1] == 4
    blocks, rows, cols = mine.shape
    return call(
        far_kernel, [wide_of(blocks // 2, rows, cols), low_of(blocks // 2, rows, cols)], at, mine, got
    )


def near_parts(at, mine, got):
    blocks, rows, cols = mine.shape
    return call(
        near_kernel, [wide_of(blocks // 2, rows, cols), low_of(blocks // 2, rows, cols)], at, mine, got
    )


def swap_near(value, digit):
    stride, _ = digit
    pairs = []
    for at in range(lax.axis_size("dp")):
        pairs.append((at, at + stride if (at // stride) % 2 == 0 else at - stride))
    return lax.ppermute(value, "dp", pairs)


def outer_send(sent, digits):
    return [rotate(part, digits[-3], step + 1) for step, part in enumerate(sent)]


def outer_sum(kept, got, digits):
    for part in got:
        kept = kept + part.astype(WIDE)
    for digit in reversed(digits[:-3]):
        size = digit[1]
        kept = kept.reshape((-1, size) + kept.shape[1:])
        at = digit_at(digit)
        take = lambda step: lax.dynamic_index_in_dim(kept, (at + step) % size, 1, keepdims=False)
        total = take(0)
        for step in range(1, size):
            total = total + rotate(take(step).astype(LOW), digit, step).astype(WIDE)
        kept = total
    return kept[0]


def fill_mask(mask, at, half_rows, mem_count, starts):
    rows = mask.shape[0]
    padded = rows // 2

    def places(shape, axis):
        spot = lax.broadcasted_iota(jnp.int32, shape, axis)
        second = spot >= padded
        within = jnp.where(second, spot - padded, spot)
        pos = within + jnp.where(second, half_rows, 0) - mem_count
        doc = jnp.zeros(shape, jnp.int32)
        for i in range(starts):
            doc = doc + (at[STARTS + i] <= pos).astype(jnp.int32)
        return within < half_rows, pos, doc

    _, q_pos, q_doc = places((rows, 1), 0)
    real, k_pos, k_doc = places((1, rows), 1)
    key_ok = real & (k_pos < at[LENGTH])
    for low in range(0, rows, CHUNK):
        qp, qd = q_pos[low : low + CHUNK], q_doc[low : low + CHUNK]
        same = (qd == k_doc) | (qp < 0) | (k_pos < 0)
        mask[low : low + CHUNK, :] = jnp.where(same & key_ok, 0.0, -1e9)


def heads_apart(pair):
    lane = lax.broadcasted_iota(jnp.int32, (1, PAIR), 1)
    zero = jnp.zeros((), LOW)
    return jnp.concatenate(
        [jnp.where(lane < HEAD, pair, zero), jnp.where(lane < HEAD, zero, pair)], axis=0
    )


def lanes(pair, count):
    return pl.ds(pl.multiple_of(pair * count, PAIR), count)


def forward_kernel(
    half_rows, mem_count, starts, first_bias,
    at, own, other, w, qkv, mix_own, mix_sent, lse, x, small, mask, s, mixed,
):
    rows, padded = x.shape[0], own.shape[0]
    t = at[T]
    part = mix_own.shape[1]
    fill_mask(mask, at, half_rows, mem_count, starts)
    lse[...] = jnp.zeros_like(lse)
    small[...] = w[:, 3 * part :].astype(WIDE).T[: small.shape[0]]
    x[pl.ds(pl.multiple_of(t * padded, 16), padded), :] = own[...]
    x[pl.ds(pl.multiple_of((1 - t) * padded, 16), padded), :] = other[...]
    row = lax.broadcasted_iota(jnp.int32, (32, 1), 0)
    fresh = (row < mem_count) & (at[FRESH] == 1)
    x[:32, :] = jnp.where(fresh, small[:32, :], x[:32, :].astype(WIDE)).astype(LOW)
    lane = lax.broadcasted_iota(jnp.int32, (1, PAIR), 1)
    scale = jnp.where(lax.broadcasted_iota(jnp.int32, (1, 3 * PAIR), 1) < PAIR, 0.125, 1.0)

    def one_pair(pair, _):
        here = pl.ds(pl.multiple_of(t * part + pair * PAIR, PAIR), PAIR)
        q_bias = small[first_bias : first_bias + 1, here]
        v_bias = small[first_bias + 1 : first_bias + 2, here]
        bias = jnp.concatenate([q_bias, jnp.zeros_like(q_bias), v_bias], axis=1)
        got = (nn(x[...], w[:, lanes(pair, 3 * PAIR)]) + bias).astype(LOW)
        got = (got.astype(WIDE) * scale).astype(LOW)
        qkv[:, lanes(pair, 3 * PAIR)] = got
        keys, values = got[:, PAIR : 2 * PAIR], got[:, 2 * PAIR :]
        q = heads_apart(got[:, :PAIR])
        for low in range(0, 2 * rows, FORWARD_BLOCK):
            here, there = slice(low, low + FORWARD_BLOCK), slice(low % rows, low % rows + FORWARD_BLOCK)
            v = nt(q[here], keys) + mask[there, :]
            top = jnp.max(v, axis=-1, keepdims=True)
            e = jnp.exp(v - top)
            total = jnp.sum(e, axis=-1, keepdims=True)
            out = nn((e * (1.0 / total)).astype(LOW), values)
            spot = lane == 2 * pair + low // rows
            lse[there, :] = jnp.where(spot, top + jnp.log(total), lse[there, :])
            if low < rows:
                s[there, :] = out
            else:
                mixed[there, :] = jnp.where(lane < HEAD, s[there, :], out).astype(LOW)
        mix_own[:, lanes(pair, PAIR)] = mixed[pl.ds(pl.multiple_of(t * padded, 16), padded), :]
        mix_sent[:, lanes(pair, PAIR)] = mixed[
            pl.ds(pl.multiple_of((1 - t) * padded, 16), padded), :
        ]
        return 0

    lax.fori_loop(0, part // PAIR, one_pair, 0)


def backward_kernel(
    half_rows, mem_count, starts, at, qkv, own, got, lse, dproj, sums, mask, s, p, ds, dmix
):
    rows, padded = qkv.shape[0], own.shape[0]
    part = own.shape[1]
    t = at[T]
    fill_mask(mask, at, half_rows, mem_count, starts)
    dmix[pl.ds(pl.multiple_of(t * padded, 16), padded), :] = own[...]
    dmix[pl.ds(pl.multiple_of((1 - t) * padded, 16), padded), :] = got[...]
    lane = lax.broadcasted_iota(jnp.int32, (1, PAIR), 1)
    zero = jnp.zeros((), LOW)

    def one_pair(pair, _):
        here = lanes(pair, 3 * PAIR)
        whole = qkv[:, here]
        keys, values = whole[:, PAIR : 2 * PAIR], whole[:, 2 * PAIR :]
        dm_pair = dmix[:, lanes(pair, PAIR)]
        q, dm = heads_apart(whole[:, :PAIR]), heads_apart(dm_pair)
        for low in range(0, 2 * rows, BACKWARD_BLOCK):
            block, there = slice(low, low + BACKWARD_BLOCK), slice(low % rows, low % rows + BACKWARD_BLOCK)
            spot = lane == 2 * pair + low // rows
            stat = jnp.sum(jnp.where(spot, lse[there, :], 0.0), axis=-1, keepdims=True)
            e = jnp.exp(nt(q[block], keys) + mask[there, :] - stat)
            d = nt(dm[block], values)
            dot = jnp.sum(e * d, axis=-1, keepdims=True)
            p[block, :] = e.astype(LOW)
            d = (e * (d - dot)).astype(LOW)
            ds[block, :] = d
            s[block, :] = nn(d, keys)
        dq = jnp.where(lane < HEAD, s[:rows, :], s[rows:, :]) * 0.125
        dk, dv = tn(ds[...], q), tn(p[...], dm)
        out = jnp.concatenate([dq, dk, dv], axis=1).astype(LOW)
        dproj[:, here] = out
        sums[:, here] = jnp.sum(out.astype(WIDE), axis=0, keepdims=True)
        return 0

    lax.fori_loop(0, part // PAIR, one_pair, 0)


def half_rows_of(ref, which, padded):
    return ref[pl.ds(pl.multiple_of(which * padded, 16), padded), :]


def projection_gradient_kernel(
    small_rows, at, layer_in, d_projected, proj_sums, sums_one, two0, two1, up_sums, wqkv, d_attn,
    *refs,
):
    grads, turn = refs[:-1], refs[-1]
    part = up_sums.shape[1]
    cols = d_projected.shape[1]
    first = at[T] == 0
    turn[...] = jnp.zeros_like(turn)
    (m0, m1), (v0, _), (g0, _), (u0, _) = small_rows
    count = m1 - m0
    memory = nt(d_projected[:32, :], wqkv[:, :cols])[:count]
    memory = memory + jnp.where(first, d_attn[:count, :], 0.0)
    turn[m0:m1, :] = jnp.where(at[FRESH] == 1, memory, 0.0)
    sums = [
        jnp.concatenate(
            [proj_sums[:, (3 * p + k) * PAIR : (3 * p + k + 1) * PAIR] for p in range(part // PAIR)],
            axis=1,
        )
        for k in (0, 2)
    ]
    for value, low in zip(sums + [up_sums[...]], (v0, v0 + 1, u0)):
        high = low + value.shape[0]
        turn[low:high, :part] = jnp.where(first, value, 0.0)
        turn[low:high, part:] = jnp.where(first, 0.0, value)
    sums_two = two0[...] + two1[...]
    turn[v0 + 2 : v0 + 4, :] = sums_one[0:2, :]
    turn[v0 + 4 : v0 + 6, :] = sums_two[0:2, :]
    turn[g0 : g0 + 1, :] = sums_one[2:3, :]
    turn[g0 + 1 : g0 + 2, :] = sums_two[2:3, :]
    small = turn[...].T
    put_gradient(layer_in, d_projected, grads, at[CORE])
    if len(grads) == 1:
        grads[0][:, cols:] = small.astype(LOW)
    else:
        put_blocks(small, grads[0], grads[-1], at[CORE], cols)


def projection_back_kernel(at, d_projected, wqkv, d_attn, d_own, d_sent):
    padded, cols = d_own.shape[0], d_projected.shape[1]
    t = at[T]
    d_own[...] = d_attn[...] + nt(half_rows_of(d_projected, t, padded), wqkv[:, :cols])
    d_sent[...] = nt(half_rows_of(d_projected, 1 - t, padded), wqkv[:, :cols]).astype(LOW)


def halves_kernel(count, at, *refs):
    parts, (mine, give, out) = refs[:count], refs[count:]
    lines, cols = mine.shape
    fold = out.shape[1] // 2
    total = parts[0][...]
    for part in parts[1:]:
        total = total + part[...].astype(WIDE)
    first = at[T] == 0
    low, high = total[:lines, :cols], total[lines:, :cols]
    mine[...] = jnp.where(first, low, high)
    give[...] = jnp.where(first, high, low).astype(LOW)
    out[:, :fold] = total[:lines, cols:]
    out[:, fold:] = total[lines:, cols:]


def finish_kernel(part, small_rows, at, mine, got, qkv, memory, vectors, gains, up, turn):
    lines = mine.shape[0]
    cols, width = 3 * part, 2 * part
    first = at[T] == 0
    for pair in range(part // PAIR):
        for kind in range(3):
            here = (3 * pair + kind) * PAIR
            a = mine[:, here : here + PAIR]
            b = got[:, here : here + PAIR].astype(WIDE)
            low = kind * width + pair * PAIR
            qkv[:, low : low + PAIR] = jnp.where(first, a, b)
            qkv[:, low + part : low + part + PAIR] = jnp.where(first, b, a)
    turn[...] = jnp.zeros_like(turn)
    turn[:lines, :] = mine[:, cols : cols + PAIR] + got[:, cols : cols + PAIR].astype(WIDE)
    small = turn[...].T
    for target, (low, high) in zip((memory, vectors, gains, up), small_rows):
        target[...] = small[low:high, :lines]


def spread_of(v):
    return jnp.mean(v, axis=-1, keepdims=True)


def first_norm_kernel(bias, gain, at, own, got, wout, layer_in, small, mixed, unit, scale, normed, s):
    padded, part = own.shape
    first = at[T] == 0
    mixed[:, :part] = jnp.where(first, own[...], got[...])
    mixed[:, part:] = jnp.where(first, got[...], own[...])
    s[...] = nn(mixed[...], wout[...])
    for low in range(0, padded, ROWS):
        here = slice(low, low + ROWS)
        rows = layer_in[pl.ds(pl.multiple_of(at[T] * padded + low, ROWS), ROWS), :]
        total = rows.astype(WIDE) + (s[here, :] + small[bias + 2 : bias + 3, :])
        centered = total - spread_of(total)
        factor = lax.rsqrt(spread_of(centered * centered) + NORM_EPSILON)
        value = centered * factor
        unit[here, :] = value
        scale[here, :] = jnp.broadcast_to(factor, (ROWS, PAIR))
        value = value * small[gain : gain + 1, :] + small[bias + 3 : bias + 4, :]
        normed[here, :] = value.astype(LOW)


def add_sums(sums, values):
    sums[...] = jnp.zeros_like(sums)
    for n, value in enumerate(values):
        sums[n : n + 1, :] = jnp.sum(value, axis=0, keepdims=True)


def second_norm_kernel(
    bias, gain, start, at, unit, small, own, got, d_out, _, layer_out, d_second, d_ffn, sums
):
    width = unit.shape[1]
    real = d_out.shape[0] - start
    totals = [jnp.zeros((ROWS, width), WIDE)] * 3
    for low in range(0, got.shape[0], ROWS):
        here, there = slice(low, low + ROWS), slice(start + low, start + low + ROWS)
        count = min(ROWS, real - low)
        first = unit[there, :] * small[gain : gain + 1, :] + small[bias + 3 : bias + 4, :]
        ffn = own[there, :] + got[here, :].astype(WIDE) + small[bias + 4 : bias + 5, :]
        total = first + ffn
        centered = total - spread_of(total)
        factor = lax.rsqrt(spread_of(centered * centered) + NORM_EPSILON)
        value = centered * factor
        out = value * small[gain + 1 : gain + 2, :] + small[bias + 5 : bias + 6, :]
        layer_out[low : low + count, :] = out[:count].astype(LOW)
        cotangent = d_out[start + low : start + low + count, :].astype(WIDE)
        if count < ROWS:
            cotangent = jnp.concatenate(
                [cotangent, jnp.zeros((ROWS - count, width), WIDE)], axis=0
            )
        d_unit = cotangent * small[gain + 1 : gain + 2, :]
        back = factor * (d_unit - spread_of(d_unit) - value * spread_of(d_unit * value))
        d_second[here, :] = back
        rounded = back.astype(LOW)
        d_ffn[here, :] = rounded
        terms = (rounded.astype(WIDE), cotangent, cotangent * value)
        totals = [a + b for a, b in zip(totals, terms)]
    add_sums(sums, totals)


def first_back_kernel(
    gain, at, second0, second1, own, got, unit, scale, small, wout, d_attn_in, d_attn, mix_own, mix_sent, sums
):
    padded, width = unit.shape
    part = mix_own.shape[1]
    totals = [jnp.zeros((ROWS, width), WIDE)] * 3
    for low in range(0, padded, ROWS):
        here = slice(low, low + ROWS)
        cut = second0.shape[0]
        second = second0[here, :] if low < cut else second1[low - cut : low - cut + ROWS, :]
        cotangent = second + own[here, :] + got[here, :].astype(WIDE)
        value = unit[here, :]
        d_unit = cotangent * small[gain : gain + 1, :]
        back = d_unit - spread_of(d_unit) - value * spread_of(d_unit * value)
        back = scale[here, :1] * back
        d_attn_in[here, :] = back
        rounded = back.astype(LOW)
        d_attn[here, :] = rounded
        terms = (rounded.astype(WIDE), cotangent, cotangent * value)
        totals = [a + b for a, b in zip(totals, terms)]
    add_sums(sums, totals)
    mixed = nt(d_attn[...], wout[...]).astype(LOW)
    first = at[T] == 0
    mix_own[...] = jnp.where(first, mixed[:, :part], mixed[:, part:])
    mix_sent[...] = jnp.where(first, mixed[:, part:], mixed[:, :part])


def rows_kernel(mem_count, at, own, got, out):
    real = out.shape[0]
    row = lax.broadcasted_iota(jnp.int32, (32, 1), 0)
    fresh = (row < mem_count) & (at[FRESH] == 1) & (at[T] == 0)
    out[:32, :] = jnp.where(fresh, 0.0, own[:32, :] + got[:32, :].astype(WIDE))
    out[32:, :] = own[32:real, :] + got[32:real, :].astype(WIDE)


def gelu_parts(pre):
    cdf = 0.5 * (1.0 + lax.erf(pre * 0.7071067811865476))
    density = jnp.exp(-0.5 * pre * pre) * 0.3989422804014327
    return pre * cdf, cdf + pre * density


def shards(
    rows_in,
    d_out,
    starts,
    lengths,
    resets,
    qkv_weight,
    out_weight,
    bias_vec,
    gains,
    mem_init,
    ffn_up,
    up_bias,
    ffn_down,
):
    half_rows, seg_count, width = rows_in.shape
    assert seg_count == 1
    dp_count, t_count = lax.axis_size("dp"), lax.axis_size("tensor")
    assert t_count == 2
    digits = digits_of(dp_count)
    x_digit, core_digit = digits[-2:]
    padded = ceil_to(half_rows, 16)
    rows = 2 * padded
    mem_count = mem_init.shape[0]
    part = HEADS // t_count * HEAD
    cols = 3 * part
    hidden_mine = ffn_up.shape[1]
    feat = bias_vec.shape[1]
    lines = qkv_weight.shape[0]
    spots = up_bias.shape[0] // feat
    doc_count = starts.shape[1]
    counts = (mem_count, bias_vec.shape[0], gains.shape[0], spots)
    edges = [sum(counts[:n]) for n in range(len(counts) + 1)]
    small_rows = tuple(zip(edges[:-1], edges[1:]))
    bias, gain = edges[1], edges[2]
    target = np.arange(part)
    target = (target // feat) * (spots * feat) + target % feat
    target = np.stack([target, np.full(part, feat)], axis=1).astype(np.int32)

    integers = [
        lax.axis_index("tensor"),
        digit_at(x_digit),
        digit_at(core_digit),
        digit_at(digits[-3]),
        lax.axis_index("dp"),
        resets[0],
        lengths[0],
    ]
    at = jnp.concatenate([jnp.stack(integers).astype(jnp.int32), starts[0]])

    kept, sent = call(
        functools.partial(columns_kernel, part, small_rows),
        [low_of(lines, cols + PAIR)] * 2,
        lax.axis_index("tensor").astype(jnp.int32).reshape(1),
        qkv_weight, bias_vec, gains, mem_init, up_bias.reshape(spots, feat),
        scratch=[pltpu.VMEM((PAIR, PAIR), WIDE)],
        room=48 << 20,
    )
    first_cols = cols + PAIR + part
    (first_pair,) = call(
        pair_kernel, [low_of(2 * lines, first_cols)], at, kept, swap_tensor(sent), out_weight
    )
    rows_low = jnp.pad(rows_in[:, 0, :], ((0, padded - half_rows), (0, 0)))
    rows_other = swap_tensor(tie(rows_low, first_pair))
    first_z = spread_outer(first_pair, digits)
    first_z, rows_other = join(first_z, rows_other)
    first_x = rotate(first_z, x_digit, 1)
    up_z = spread_outer(tie(ffn_up, first_z), digits)
    down_in = tie(ffn_down.T, up_z)
    first_z, first_x, up_z = join(first_z, first_x, up_z)
    first_parts = swap_blocks(first_z, first_x, digits)
    wqkv = assemble(at, first_parts, digits, cols + PAIR)
    (out_sent,) = call(
        functools.partial(unfold_kernel, cols + PAIR),
        [low_of(dp_count // 2, lines, width)], at, first_z, first_x,
    )
    out_got = swap_tensor(out_sent)
    up_x = rotate(up_z, x_digit, 1)
    down_z = spread_outer(down_in, digits)

    projected, mix_own, mix_sent, log_total, layer_in, small = call(
        functools.partial(forward_kernel, half_rows, mem_count, doc_count, bias),
        [
            low_of(rows, cols),
            low_of(padded, part),
            low_of(padded, part),
            wide_of(rows, PAIR),
            low_of(rows, width),
            wide_of(edges[-1], width),
        ],
        at, rows_low, rows_other, wqkv,
        scratch=[
            pltpu.VMEM((rows, rows), WIDE),
            pltpu.VMEM((rows, PAIR), WIDE),
            pltpu.VMEM((rows, PAIR), LOW),
        ],
    )
    mix_got = swap_tensor(mix_sent)
    out_got = tie(out_got, mix_sent)
    (wout,) = call(
        functools.partial(
            assemble_out_kernel, tuple(size for _, size in digits), cols + PAIR
        ),
        [low_of(dp_count, 2 * lines, width)],
        at, *first_parts, out_got, rotate(out_got, core_digit, 1),
    )
    wout = wout.reshape(width, width)
    mixed, unit, scale, normed_own = call(
        functools.partial(first_norm_kernel, bias, gain),
        [low_of(padded, width), wide_of(padded, width), wide_of(padded, PAIR), low_of(padded, width)],
        at, mix_own, mix_got, wout, layer_in, small,
        scratch=[pltpu.VMEM((padded, width), WIDE)],
    )

    normed_got = swap_tensor(normed_own)
    up_x, up_z, down_z = tie(up_x, mix_sent), tie(up_z, mix_sent), tie(down_z, mix_sent)
    up = assemble(at, swap_blocks(up_z, up_x, digits), digits, hidden_mine)
    (up_b,) = call(
        functools.partial(up_row_kernel, edges[3], spots),
        [wide_of(ROWS, hidden_mine)], at, small, jnp.asarray(target),
    )
    down_x = rotate(down_z, x_digit, 1)
    normed_got, down_x, up_b, up = join(normed_got, down_x, up_b, up)
    down_t = assemble(at, swap_blocks(down_z, down_x, digits), digits, hidden_mine)

    def feed_forward(rows):
        pre_act = nn(rows, up).reshape(-1, *up_b.shape) + up_b
        hidden, slope = (part.reshape(rows.shape[0], -1) for part in gelu_parts(pre_act))
        hidden = hidden.astype(LOW)
        return hidden, slope, nt(hidden, down_t)

    cut = ceil_to(padded // 2, ROWS)
    pieces = ((0, cut), (cut, padded))
    hidden_got, slope_got, ffn_sent = feed_forward(normed_got)
    ffn_sent = ffn_sent.astype(LOW)
    ffn_got = [swap_tensor(ffn_sent[low:high]) for low, high in pieces]
    hidden_own, slope_own, ffn_own = feed_forward(tie(normed_own, ffn_sent))
    d_out_rows = d_out.reshape(half_rows, width)
    second, ahead = [], small
    for (low, high), got in zip(pieces, ffn_got):
        if second:
            ahead = rotate(second[-1][2][:ROWS, :PAIR], core_digit, 1)
        outs = [
            low_of(min(high, half_rows) - low, width),
            wide_of(high - low, width),
            low_of(high - low, width),
            wide_of(8, width),
        ]
        kernel = functools.partial(second_norm_kernel, bias, gain, low)
        second.append(call(kernel, outs, at, unit, small, ffn_own, got, d_out_rows, ahead))
    layer_out, d_second, d_ffn_sent, sums_two = zip(*second)

    d_ffn_got = jnp.concatenate([swap_tensor(piece) for piece in d_ffn_sent], axis=0)
    d_ffn_own = jnp.concatenate(d_ffn_sent, axis=0)

    def feed_back(rows, slope):
        d_pre = (slope * nn(rows, down_t)).astype(LOW)
        return d_pre, nt(d_pre, up)

    d_pre_own, d_first_own = feed_back(d_ffn_own, slope_own)
    down_own, up_own, sums_own = call(
        own_kernel,
        [wide_of(width, hidden_mine), wide_of(width, hidden_mine), wide_of(1, hidden_mine)],
        at, d_ffn_own, hidden_own, normed_own, d_pre_own,
    )
    d_ffn_got, d_first_own, down_own, up_own = join(d_ffn_got, d_first_own, down_own, up_own)
    d_pre_got, d_first_sent = feed_back(d_ffn_got, slope_got)
    d_first_sent = d_first_sent.astype(LOW)
    d_first_got = swap_tensor(d_first_sent)

    outs = gradient_outs(width, hidden_mine, dp_count)
    down_grads = call(
        rest_kernel, outs, at, down_own, tie(d_ffn_got, d_first_sent), hidden_got
    )
    down_kept, down_sent = halve(at, *swap_cores(down_grads, dp_count, core_digit))
    down_got = rotate(down_sent, x_digit, 1)
    up_sums, *up_grads = call(
        functools.partial(rest_sums_kernel, spots), [wide_of(spots, part)] + outs, at,
        up_own, sums_own, normed_got, tie(d_pre_got, down_sent), jnp.asarray(target),
    )
    up_kept, up_sent = halve(at, *swap_cores(up_grads, dp_count, core_digit))

    d_attn_in, d_attn, d_mix_own, d_mix_sent, sums_one = call(
        functools.partial(first_back_kernel, gain),
        [
            wide_of(padded, width),
            low_of(padded, width),
            low_of(padded, part),
            low_of(padded, part),
            wide_of(8, width),
        ],
        at, *d_second, d_first_own, d_first_got, unit, scale, small, wout,
    )
    d_mix_got = swap_tensor(d_mix_sent)
    out_grads = call(
        out_gradient_kernel, gradient_outs(width, width, dp_count, OUT_TILE),
        at, mixed, tie(d_attn, d_mix_sent),
    )
    out_kept, out_parts = swap_cores(out_grads, dp_count, core_digit)
    out_kept, out_sent = call(
        rows_halves_kernel, [low_of(dp_count // 2, lines, width)] * 2, at, out_kept, *out_parts
    )
    down_kept, down_sent = far_parts(at, down_kept, down_got, digits)
    d_mix_got, out_sent, up_sent, down_sent = join(d_mix_got, out_sent, up_sent, down_sent)
    down_got = rotate(down_sent, digits[-3], 2)
    out_got = swap_tensor(out_sent)
    up_got = rotate(up_sent, x_digit, 1)

    d_projected, proj_sums = call(
        functools.partial(backward_kernel, half_rows, mem_count, doc_count),
        [low_of(rows, cols), wide_of(1, cols)],
        at, projected, d_mix_own, d_mix_got, log_total,
        scratch=[
            pltpu.VMEM((rows, rows), WIDE),
            pltpu.VMEM((2 * rows, PAIR), WIDE),
            pltpu.VMEM((2 * rows, rows), LOW),
            pltpu.VMEM((2 * rows, rows), LOW),
            pltpu.VMEM((rows, part), LOW),
        ],
    )
    up_kept, up_sent = far_parts(at, up_kept, up_got, digits)
    qkv_grads = call(
        functools.partial(projection_gradient_kernel, small_rows),
        gradient_outs(width, cols + PAIR, dp_count),
        at, layer_in, d_projected, proj_sums, sums_one, *sums_two, up_sums, wqkv, d_attn_in,
        scratch=[pltpu.VMEM((PAIR, width), WIDE)],
    )
    out_got, down_got, *qkv_grads = join(out_got, down_got, *qkv_grads)
    down_kept, down_sent = near_parts(at, down_kept, down_got)
    out_kept, out_sent = halve(at, out_kept, [out_got])
    out_got = rotate(out_sent, x_digit, 1)
    qkv_kept, qkv_parts = swap_cores(qkv_grads, dp_count, core_digit)
    up_sent, *qkv_parts = join(up_sent, *qkv_parts)
    qkv_kept, qkv_sent = halve(at, qkv_kept, qkv_parts)

    qkv_got = rotate(qkv_sent, x_digit, 1)
    up_got = rotate(up_sent, digits[-3], 2)
    down_got = swap_near(down_sent, digits[-3])
    d_in_own, d_in_sent = call(
        projection_back_kernel, [wide_of(padded, width), low_of(padded, width)],
        at, tie(d_projected, qkv_sent), wqkv, d_attn_in,
    )
    up_kept, up_sent = near_parts(at, up_kept, up_got)
    qkv_got, d_in_sent, out_got, up_sent, down_got = join(
        qkv_got, d_in_sent, out_got, up_sent, down_got
    )
    up_got = swap_near(up_sent, digits[-3])
    d_in_got = swap_tensor(d_in_sent)
    both_kept, both_sent = outer_parts(
        at, qkv_kept, qkv_got, digits, out_kept, out_got
    )
    both_got = outer_send(both_sent, digits)
    grad_ffn_down = outer_sum(down_kept, [down_got], digits)
    grad_ffn_up = outer_sum(up_kept, [up_got], digits)
    (grad_rows,) = call(
        functools.partial(rows_kernel, mem_count), [wide_of(half_rows, width)], at, d_in_own, d_in_got
    )
    grad_rows, *both_got = join(grad_rows, *both_got)

    if len(digits) == 3:
        parts = [both_kept[0], *[part[0] for part in both_got]]
    else:
        parts = [outer_sum(both_kept, both_got, digits)]
    mine, give, grad_out_weight = call(
        functools.partial(halves_kernel, len(parts)),
        [wide_of(lines, cols + PAIR), low_of(lines, cols + PAIR), wide_of(lines, width)],
        at, *parts,
    )
    grad_qkv, grad_mem, grad_vec, grad_gains, grad_up_bias = call(
        functools.partial(finish_kernel, part, small_rows),
        [wide_of(lines, 3 * width)] + [wide_of(n, feat) for n in counts],
        at, mine, swap_tensor(give),
        scratch=[pltpu.VMEM((PAIR, PAIR), WIDE)],
    )
    return (
        jnp.concatenate(layer_out, axis=0).reshape(half_rows, 1, width),
        grad_rows.reshape(half_rows, 1, width),
        grad_qkv,
        grad_out_weight,
        grad_vec,
        grad_gains,
        grad_mem,
        grad_ffn_up,
        grad_up_bias.reshape(up_bias.shape),
        grad_ffn_down.T,
    )


def solution(mesh):
    both = ("dp", "tensor")
    in_specs = (
        P("tensor", "dp", None),
        P("tensor", "dp", None),
        P("dp", None),
        P("dp"),
        P("dp"),
        P(both, None),
        P(both, None),
        P(None, both),
        P(None, both),
        P(None, both),
        P("dp", "tensor"),
        P(both),
        P("tensor", "dp"),
    )
    out_specs = (
        P("tensor", "dp", None),
        P("tensor", "dp", None),
        P(both, None),
        P(both, None),
        P(None, both),
        P(None, both),
        P(None, both),
        P("dp", "tensor"),
        P(both),
        P("tensor", "dp"),
    )
    return jax.shard_map(shards, mesh=mesh, in_specs=in_specs, out_specs=out_specs, check_vma=False)
```

```python
import functools

import jax
import jax.numpy as jnp
import numpy as np
from jax import lax
from jax.experimental import pallas as pl
from jax.experimental.pallas import tpu as pltpu
from jax.sharding import PartitionSpec as P

HEADS = 12
HEAD = 64
NORM_EPSILON = 1e-06
LOW = jnp.bfloat16
WIDE = jnp.float32
CHUNK = 32
FORWARD_BLOCK = 272
BACKWARD_BLOCK = 544
TILE = 384
OUT_TILE = 256
ROWS = 16
PAIR = 2 * HEAD
UP_AT = 32
QUICK = pl.CostEstimate(flops=1, bytes_accessed=1, transcendentals=0)
T, X, CORE, OUTER, DP, FRESH, LENGTH, STARTS = range(8)


def ceil_to(count, unit):
    return -(-count // unit) * unit


def nn(a, b):
    return lax.dot_general(a, b, (((1,), (0,)), ((), ())), preferred_element_type=WIDE)


def nt(a, b):
    return lax.dot_general(a, b, (((1,), (1,)), ((), ())), preferred_element_type=WIDE)


def tn(a, b):
    return lax.dot_general(a, b, (((0,), (0,)), ((), ())), preferred_element_type=WIDE)


def low_of(*shape):
    return jax.ShapeDtypeStruct(shape, LOW)


def wide_of(*shape):
    return jax.ShapeDtypeStruct(shape, WIDE)


def held_bytes(array):
    rows, cols = ((1,) + tuple(array.shape))[-2:]
    lead = int(np.prod(array.shape[:-2])) if len(array.shape) > 2 else 1
    return lead * ceil_to(rows, 16) * ceil_to(cols, 128) * jnp.dtype(array.dtype).itemsize


def call(kernel, outs, at, *arrays, scratch=(), room=0):
    room += sum(held_bytes(array) for array in (*arrays, *outs))
    room += sum(held_bytes(ref) for ref in scratch)
    return pl.pallas_call(
        kernel,
        in_specs=[pl.BlockSpec(memory_space=pltpu.SMEM)]
        + [pl.BlockSpec(memory_space=pltpu.VMEM)] * len(arrays),
        out_specs=[pl.BlockSpec(memory_space=pltpu.VMEM)] * len(outs),
        out_shape=list(outs),
        scratch_shapes=list(scratch),
        compiler_params=pltpu.CompilerParams(vmem_limit_bytes=room + (3 << 20)),
        cost_estimate=QUICK,
    )(at, *arrays)


def digits_of(dp_count):
    assert dp_count % 4 == 0
    sizes = [2, 2]
    left = dp_count // 4
    while left > 1:
        size = next((s for s in (4, 2, 3) if left % s == 0), left)
        sizes.append(size)
        left //= size
    if len(sizes) == 2:
        sizes.append(1)
    digits, stride = [], 1
    for size in sizes:
        digits.append((stride, size))
        stride *= size
    return digits[::-1]


def digit_at(digit):
    stride, size = digit
    return (lax.axis_index("dp") // stride) % size


def rotate(value, digit, step):
    stride, size = digit
    pairs = []
    for at in range(lax.axis_size("dp")):
        mine = (at // stride) % size
        pairs.append((at, at + ((mine + step) % size - mine) * stride))
    return lax.ppermute(value, "dp", pairs)


def swap_tensor(value):
    return lax.ppermute(value, "tensor", [(0, 1), (1, 0)])


def swap_both(value, digit):
    stride, _ = digit
    pairs = []
    for at in range(lax.axis_size("dp")):
        other = at + stride if (at // stride) % 2 == 0 else at - stride
        pairs += [(2 * at + side, 2 * other + 1 - side) for side in range(2)]
    return lax.ppermute(value, ("dp", "tensor"), pairs)


def tie(value, *others):
    return lax.optimization_barrier((value,) + others)[0]


join = lambda *values: lax.optimization_barrier(values)


def spread_outer(value, digits):
    for digit in reversed(digits[:-2]):
        got = [value] + [rotate(value, digit, step) for step in range(1, digit[1])]
        value = jnp.stack(got)
    return value.reshape((-1,) + value.shape[-2:])


def swap_near(value, digit):
    stride, _ = digit
    pairs = []
    for at in range(lax.axis_size("dp")):
        pairs.append((at, at + stride if (at // stride) % 2 == 0 else at - stride))
    return lax.ppermute(value, "dp", pairs)


def spread_near(value, digits):
    assert digits[-3][1] == 4
    return jnp.stack([value, swap_near(value, digits[-3])])


def spread_far(pair, digits):
    value = jnp.concatenate([pair, rotate(pair, digits[-3], 2)], axis=0)
    for digit in reversed(digits[:-3]):
        value = jnp.stack([value] + [rotate(value, digit, step) for step in range(1, digit[1])])
    return value.reshape((-1,) + value.shape[-2:])


def placer(sizes, me, paired):
    outer, digits = sizes[:-2], []
    for size in reversed(sizes):
        digits.append(lax.rem(me, size))
        me = lax.div(me, size)
    digits = digits[::-1]

    def place_of(swap_core, swap_x, slot):
        steps = []
        for size in reversed(outer):
            steps.append(slot % size)
            slot //= size
        place = 0
        for n, (size, digit, step) in enumerate(zip(outer, digits, steps[::-1])):
            if paired and n == len(outer) - 1:
                at = lax.bitwise_xor(digit, step)
            else:
                at = lax.rem(digit + (size - step), size)
            place = place * size + at
        x, core = digits[-2], digits[-1]
        place = place * 2 + (1 - x if swap_x else x)
        return place * 2 + (1 - core if swap_core else core)

    return place_of


def assemble_kernel(sizes, paired, at, *refs):
    parts, whole = refs[:4], refs[4]
    cols = whole.shape[2]
    place_of = placer(sizes, at[DP], paired)
    for swap_core in range(2):
        for swap_x in range(2):
            source = parts[2 * swap_core + swap_x]
            for slot in range(source.shape[0]):
                whole[place_of(swap_core, swap_x, slot)] = source[slot, :, :cols]


def swap_blocks(mine, x_got, digits):
    core = digits[-1]
    return [mine, x_got, rotate(mine, core, 1), rotate(x_got, core, 1)]


def assemble(at, parts, digits, cols, paired=False):
    slots, rows, _ = parts[0].shape
    sizes = tuple(size for _, size in digits)
    (whole,) = call(
        functools.partial(assemble_kernel, sizes, paired),
        [low_of(4 * slots, rows, cols)],
        at,
        *parts,
    )
    return whole.reshape(4 * slots * rows, cols)


def assemble_first_kernel(sizes, at, *refs):
    parts, whole = refs[:4], refs[4]
    lines, cols = whole.shape[1] // 2, whole.shape[2]
    place_of = placer(sizes, at[DP], False)
    first = at[T] == 0
    for swap_core in range(2):
        for swap_x in range(2):
            source = parts[2 * swap_core + swap_x]
            far = source.shape[2] - cols
            for slot in range(source.shape[0]):
                place = place_of(swap_core, swap_x, slot)
                a, b = source[slot, :, :cols], source[slot, :, far:]
                whole[place, :lines] = jnp.where(first, a, b)
                whole[place, lines:] = jnp.where(first, b, a)


def assemble_out_kernel(sizes, cols, at, *refs):
    parts, gots, whole = refs[:4], refs[4:6], refs[6]
    place_of = placer(sizes, at[DP], False)
    first = at[T] == 0
    lines, width = whole.shape[1] // 2, whole.shape[2]
    for swap_core in range(2):
        for swap_x in range(2):
            source, got = parts[2 * swap_core + swap_x], gots[swap_core]
            slots = source.shape[0]
            for slot in range(slots):
                mine, other = source[slot, :, cols : cols + width], got[swap_x * slots + slot]
                place = place_of(swap_core, swap_x, slot)
                whole[place, :lines] = jnp.where(first, mine, other)
                whole[place, lines:] = jnp.where(first, other, mine)


def columns_kernel(small_rows, at, weight, vectors, gains, memory, up, out, packed, turn):
    lines, width = weight.shape
    packed[:, :width] = weight[...]
    turn[...] = jnp.zeros_like(turn)
    for source, (low, high) in zip((memory, vectors, gains), small_rows):
        turn[low:high, :lines] = source[...].astype(WIDE)
    columns = turn[...].T[:lines]
    turn[:lines, :] = columns
    turn[0:1, UP_AT : UP_AT + up.shape[1]] = up[...].astype(WIDE)
    packed[:, width : width + PAIR] = turn[:lines, :].astype(LOW)
    packed[:, width + PAIR :] = out[...]


def halves_of_heads_kernel(part, at, packed, mine, other):
    width = 6 * part
    first = at[T] == 0
    for slot in range(packed.shape[0]):
        for pair in range(part // PAIR):
            for kind in range(3):
                low = 2 * kind * part + pair * PAIR
                a = packed[slot, :, low : low + PAIR]
                b = packed[slot, :, low + part : low + part + PAIR]
                here = (3 * pair + kind) * PAIR
                mine[slot, :, here : here + PAIR] = jnp.where(first, a, b)
                other[slot, :, here : here + PAIR] = jnp.where(first, b, a)
        mine[slot, :, 3 * part :] = packed[slot, :, width:]
        other[slot, :, 3 * part :] = packed[slot, :, width : width + PAIR]


def beside_kernel(cols, at, mine, x_got, out):
    slots = mine.shape[0]
    for n, source in enumerate((mine, x_got)):
        for slot in range(slots):
            out[n * slots + slot] = source[slot, :, cols : cols + out.shape[2]]


def put_blocks(total, kept, sent, core, at):
    groups, rows, _ = kept.shape
    cols = total.shape[1]
    total = total.astype(LOW).reshape(2 * groups, rows, cols)
    second = core == 1
    for group in range(groups):
        even, odd = total[2 * group], total[2 * group + 1]
        kept[group, :, at : at + cols] = jnp.where(second, odd, even)
        sent[group] = jnp.where(second, even, odd)


def put_gradient(a, b, outs, core, own=None, tile=TILE):
    for n, low in enumerate(range(0, b.shape[1], tile)):
        total = tn(a[...], b[:, low : low + tile])
        if own is not None:
            total = total + own[:, low : low + tile]
        if len(outs) == 1:
            outs[0][:, low : low + tile] = total.astype(LOW)
        else:
            put_blocks(total, outs[0], outs[1 + n], core, low)


def gradient_outs(width, cols, dp_count, tile=TILE):
    rows = width // dp_count
    if rows % 16:
        return [low_of(width, cols)]
    tiles = [min(tile, cols - low) for low in range(0, cols, tile)]
    return [low_of(dp_count // 2, rows, n) for n in [cols] + tiles]


def swap_cores(outs, dp_count, digit):
    if len(outs) == 1:
        whole = outs[0].reshape(dp_count // 2, 2, -1, outs[0].shape[1])
        core = digit_at(digit)
        take = lambda which: lax.dynamic_index_in_dim(whole, which, 1, keepdims=False)
        outs = [take(core), take(1 - core)]
    return outs[0], [rotate(part, digit, 1) for part in outs[1:]]


def out_gradient_kernel(at, a, b, *outs):
    put_gradient(a, b, outs, at[CORE], tile=OUT_TILE)


def rows_halves_kernel(at, mine, *refs):
    got, (kept, sent) = refs[:-2], refs[-2:]
    lines = kept.shape[1]
    first = at[T] == 0
    for group in range(mine.shape[0]):
        low = 0
        for part in got:
            high = low + part.shape[2]
            total = mine[group, :, low:high].astype(WIDE) + part[group].astype(WIDE)
            a, b = total[:lines], total[lines:]
            kept[group, :, low:high] = jnp.where(first, a, b).astype(LOW)
            sent[group, :, low:high] = jnp.where(first, b, a).astype(LOW)
            low = high


def own_kernel(at, a_down, b_down, a_up, b_up, down, up, sums):
    tile = 384
    for low in range(0, b_down.shape[1], tile):
        here = slice(low, low + tile)
        down[:, here] = tn(a_down[...], b_down[:, here])
        up[:, here] = tn(a_up[...], b_up[:, here])
    sums[...] = jnp.sum(b_up[...].astype(WIDE), axis=0, keepdims=True)


def rest_kernel(at, own, a, b, *outs):
    put_gradient(a, b, outs, at[CORE], own=own)


def rest_sums_kernel(at, own, own_sums, a, b, sums, *outs):
    put_gradient(a, b, outs, at[CORE], own=own)
    sums[...] = own_sums[...] + jnp.sum(b[...].astype(WIDE), axis=0, keepdims=True)


def up_row_kernel(lines, at, w, row, line):
    half, each = w.shape[0] // 2, row.shape[1] * lines * 2 // w.shape[0]
    low = w.shape[1] - PAIR
    for n in range(half // lines):
        a = w[n * lines : n * lines + 1, low:].astype(WIDE)
        b = w[half + n * lines : half + n * lines + 1, low:].astype(WIDE)
        value = jnp.where(at[T] == 0, a, b)[:, UP_AT : UP_AT + each]
        line[:, n * each : (n + 1) * each] = value
    row[...] = jnp.broadcast_to(line[...], row.shape)


def halve_kernel(at, mine, *refs):
    got, (kept, sent) = refs[:-2], refs[-2:]
    x = at[X]
    for group in range(kept.shape[0]):
        for other, out in ((0, kept), (1, sent)):
            place = 2 * group + (1 - x if other else x)
            low = 0
            for part in got:
                high = low + part.shape[2]
                total = mine[place, :, low:high].astype(WIDE) + part[place].astype(WIDE)
                out[group, :, low:high] = total.astype(LOW)
                low = high


def halve(at, mine, got):
    groups, rows, cols = mine.shape
    return call(halve_kernel, [low_of(groups // 2, rows, cols)] * 2, at, mine, *got)


def quarter_kernel(at, mine, *refs):
    got, (out_mine, out_got, keep, to_x, to_y, to_both) = refs[:-6], refs[-6:]
    lines, cols = to_y.shape[1:]
    first = at[T] == 0
    for group in range(keep.shape[0]):
        own, other = 2 * group + at[X], 2 * group + 1 - at[X]
        for place, same, across in ((own, keep, to_y), (other, to_x, to_both)):
            low = 0
            for part in got:
                high = low + part.shape[2]
                total = mine[place, :, low:high].astype(WIDE) + part[place].astype(WIDE)
                a, b = total[:lines], total[lines:]
                same[group, :, low:high] = jnp.where(first, a, b).astype(LOW)
                across[group, :, low:high] = jnp.where(first, b, a).astype(LOW)
                low = high
            total = out_mine[place].astype(WIDE) + out_got[place].astype(WIDE)
            same[group, :, cols:] = total.astype(LOW)


def parts_kernel(size, at, mine, x_got, y_got, both_got, *outs):
    me = at[OUTER]
    cols = mine.shape[2]
    for group in range(outs[0].shape[0]):
        for step, out in enumerate(outs):
            place = group * size + lax.rem(me + step, size)
            total = mine[place].astype(WIDE) + x_got[place].astype(WIDE)
            out[group, :, :cols] = total.astype(out.dtype)
            total = y_got[place].astype(WIDE) + both_got[place].astype(WIDE)
            out[group, :, cols:] = total.astype(out.dtype)


def outer_parts(at, digits, *parts):
    size = digits[-3][1]
    blocks, rows, cols = parts[0].shape
    shape = (blocks // size, rows, cols + parts[2].shape[2])
    outs = [wide_of(*shape)] + [low_of(*shape)] * (size - 1)
    kept, *sent = call(functools.partial(parts_kernel, size), outs, at, *parts)
    return kept, sent


def far_kernel(at, mine, got, kept, sent):
    me = at[OUTER]
    pair = lax.bitwise_xor(me, 1)
    for group in range(kept.shape[0] // 2):
        for n, block in enumerate((me, pair)):
            for out, place in ((kept, block), (sent, lax.bitwise_xor(block, 2))):
                spot = 4 * group + place
                total = mine[spot].astype(WIDE) + got[spot].astype(WIDE)
                out[2 * group + n] = total.astype(out.dtype)


def near_kernel(at, mine, got, kept, sent):
    for group in range(kept.shape[0]):
        kept[group] = mine[2 * group] + got[2 * group].astype(WIDE)
        total = mine[2 * group + 1] + got[2 * group + 1].astype(WIDE)
        sent[group] = total.astype(LOW)


def far_parts(at, mine, got, digits):
    assert digits[-3][1] == 4
    blocks, rows, cols = mine.shape
    return call(
        far_kernel, [wide_of(blocks // 2, rows, cols), low_of(blocks // 2, rows, cols)], at, mine, got
    )


def near_parts(at, mine, got):
    blocks, rows, cols = mine.shape
    return call(
        near_kernel, [wide_of(blocks // 2, rows, cols), low_of(blocks // 2, rows, cols)], at, mine, got
    )


def outer_send(sent, digits):
    return [rotate(part, digits[-3], step + 1) for step, part in enumerate(sent)]


def outer_sum(kept, got, digits):
    for part in got:
        kept = kept + part.astype(WIDE)
    for digit in reversed(digits[:-3]):
        size = digit[1]
        kept = kept.reshape((-1, size) + kept.shape[1:])
        at = digit_at(digit)
        take = lambda step: lax.dynamic_index_in_dim(kept, (at + step) % size, 1, keepdims=False)
        total = take(0)
        for step in range(1, size):
            total = total + rotate(take(step).astype(LOW), digit, step).astype(WIDE)
        kept = total
    return kept[0]


def fill_mask(mask, at, half_rows, mem_count, starts):
    rows = mask.shape[0]
    padded = rows // 2

    def places(shape, axis):
        spot = lax.broadcasted_iota(jnp.int32, shape, axis)
        second = spot >= padded
        within = jnp.where(second, spot - padded, spot)
        pos = within + jnp.where(second, half_rows, 0) - mem_count
        doc = jnp.zeros(shape, jnp.int32)
        for i in range(starts):
            doc = doc + (at[STARTS + i] <= pos).astype(jnp.int32)
        return within < half_rows, pos, doc

    _, q_pos, q_doc = places((rows, 1), 0)
    real, k_pos, k_doc = places((1, rows), 1)
    key_ok = real & (k_pos < at[LENGTH])
    for low in range(0, rows, CHUNK):
        qp, qd = q_pos[low : low + CHUNK], q_doc[low : low + CHUNK]
        same = (qd == k_doc) | (qp < 0) | (k_pos < 0)
        mask[low : low + CHUNK, :] = jnp.where(same & key_ok, 0.0, -1e9)


def heads_apart(pair):
    lane = lax.broadcasted_iota(jnp.int32, (1, PAIR), 1)
    zero = jnp.zeros((), LOW)
    return jnp.concatenate(
        [jnp.where(lane < HEAD, pair, zero), jnp.where(lane < HEAD, zero, pair)], axis=0
    )


def lanes(pair, count):
    return pl.ds(pl.multiple_of(pair * count, PAIR), count)


def forward_kernel(
    half_rows, mem_count, starts, first_bias,
    at, own, other, w, qkv, mix_own, mix_sent, lse, x, small, mask, s, mixed,
):
    rows, padded = x.shape[0], own.shape[0]
    t = at[T]
    part = mix_own.shape[1]
    fill_mask(mask, at, half_rows, mem_count, starts)
    lse[...] = jnp.zeros_like(lse)
    small[...] = w[:, 3 * part :].astype(WIDE).T[: small.shape[0]]
    x[pl.ds(pl.multiple_of(t * padded, 16), padded), :] = own[...]
    x[pl.ds(pl.multiple_of((1 - t) * padded, 16), padded), :] = other[...]
    row = lax.broadcasted_iota(jnp.int32, (32, 1), 0)
    fresh = (row < mem_count) & (at[FRESH] == 1)
    x[:32, :] = jnp.where(fresh, small[:32, :], x[:32, :].astype(WIDE)).astype(LOW)
    lane = lax.broadcasted_iota(jnp.int32, (1, PAIR), 1)
    scale = jnp.where(lax.broadcasted_iota(jnp.int32, (1, 3 * PAIR), 1) < PAIR, 0.125, 1.0)

    def one_pair(pair, _):
        here = pl.ds(pl.multiple_of(t * part + pair * PAIR, PAIR), PAIR)
        q_bias = small[first_bias : first_bias + 1, here]
        v_bias = small[first_bias + 1 : first_bias + 2, here]
        bias = jnp.concatenate([q_bias, jnp.zeros_like(q_bias), v_bias], axis=1)
        got = (nn(x[...], w[:, lanes(pair, 3 * PAIR)]) + bias).astype(LOW)
        got = (got.astype(WIDE) * scale).astype(LOW)
        qkv[:, lanes(pair, 3 * PAIR)] = got
        keys, values = got[:, PAIR : 2 * PAIR], got[:, 2 * PAIR :]
        q = heads_apart(got[:, :PAIR])
        for low in range(0, 2 * rows, FORWARD_BLOCK):
            here, there = slice(low, low + FORWARD_BLOCK), slice(low % rows, low % rows + FORWARD_BLOCK)
            v = nt(q[here], keys) + mask[there, :]
            top = jnp.max(v, axis=-1, keepdims=True)
            e = jnp.exp(v - top)
            total = jnp.sum(e, axis=-1, keepdims=True)
            out = nn((e * (1.0 / total)).astype(LOW), values)
            spot = lane == 2 * pair + low // rows
            lse[there, :] = jnp.where(spot, top + jnp.log(total), lse[there, :])
            if low < rows:
                s[there, :] = out
            else:
                mixed[there, :] = jnp.where(lane < HEAD, s[there, :], out).astype(LOW)
        mix_own[:, lanes(pair, PAIR)] = mixed[pl.ds(pl.multiple_of(t * padded, 16), padded), :]
        mix_sent[:, lanes(pair, PAIR)] = mixed[
            pl.ds(pl.multiple_of((1 - t) * padded, 16), padded), :
        ]
        return 0

    lax.fori_loop(0, part // PAIR, one_pair, 0)


def backward_kernel(
    half_rows, mem_count, starts, at, qkv, own, got, lse, dproj, sums, mask, s, p, ds, dmix
):
    rows, padded = qkv.shape[0], own.shape[0]
    part = own.shape[1]
    t = at[T]
    fill_mask(mask, at, half_rows, mem_count, starts)
    dmix[pl.ds(pl.multiple_of(t * padded, 16), padded), :] = own[...]
    dmix[pl.ds(pl.multiple_of((1 - t) * padded, 16), padded), :] = got[...]
    lane = lax.broadcasted_iota(jnp.int32, (1, PAIR), 1)
    zero = jnp.zeros((), LOW)

    def one_pair(pair, _):
        here = lanes(pair, 3 * PAIR)
        whole = qkv[:, here]
        keys, values = whole[:, PAIR : 2 * PAIR], whole[:, 2 * PAIR :]
        dm_pair = dmix[:, lanes(pair, PAIR)]
        q, dm = heads_apart(whole[:, :PAIR]), heads_apart(dm_pair)
        for low in range(0, 2 * rows, BACKWARD_BLOCK):
            block, there = slice(low, low + BACKWARD_BLOCK), slice(low % rows, low % rows + BACKWARD_BLOCK)
            spot = lane == 2 * pair + low // rows
            stat = jnp.sum(jnp.where(spot, lse[there, :], 0.0), axis=-1, keepdims=True)
            e = jnp.exp(nt(q[block], keys) + mask[there, :] - stat)
            d = nt(dm[block], values)
            dot = jnp.sum(e * d, axis=-1, keepdims=True)
            p[block, :] = e.astype(LOW)
            d = (e * (d - dot)).astype(LOW)
            ds[block, :] = d
            s[block, :] = nn(d, keys)
        dq = jnp.where(lane < HEAD, s[:rows, :], s[rows:, :]) * 0.125
        dk, dv = tn(ds[...], q), tn(p[...], dm)
        out = jnp.concatenate([dq, dk, dv], axis=1).astype(LOW)
        dproj[:, here] = out
        sums[:, here] = jnp.sum(out.astype(WIDE), axis=0, keepdims=True)
        return 0

    lax.fori_loop(0, part // PAIR, one_pair, 0)


def half_rows_of(ref, which, padded):
    return ref[pl.ds(pl.multiple_of(which * padded, 16), padded), :]


def projection_gradient_kernel(
    small_rows, lines, at, layer_in, d_projected, proj_sums, sums_one, two0, two1, up_sums, wqkv, d_attn,
    *refs,
):
    grads, (turn, rows) = refs[:-2], refs[-2:]
    cols = d_projected.shape[1]
    part = cols // 3
    first = at[T] == 0
    turn[...] = jnp.zeros_like(turn)
    (m0, m1), (v0, _), (g0, _) = small_rows
    count = m1 - m0
    memory = nt(d_projected[:32, :], wqkv[:, :cols])[:count]
    memory = memory + jnp.where(first, d_attn[:count, :], 0.0)
    turn[m0:m1, :] = jnp.where(at[FRESH] == 1, memory, 0.0)
    sums = [
        jnp.concatenate(
            [proj_sums[:, (3 * p + k) * PAIR : (3 * p + k + 1) * PAIR] for p in range(part // PAIR)],
            axis=1,
        )
        for k in (0, 2)
    ]
    for low, value in enumerate(sums, v0):
        turn[low : low + 1, :part] = jnp.where(first, value, 0.0)
        turn[low : low + 1, part:] = jnp.where(first, 0.0, value)
    sums_two = two0[...] + two1[...]
    turn[v0 + 2 : v0 + 4, :] = sums_one[0:2, :]
    turn[v0 + 4 : v0 + 6, :] = sums_two[0:2, :]
    turn[g0 : g0 + 1, :] = sums_one[2:3, :]
    turn[g0 + 1 : g0 + 2, :] = sums_two[2:3, :]
    rows[...] = turn[...].T
    half = rows.shape[0] // 2
    each = up_sums.shape[1] * lines // half
    for n in range(half // lines):
        value = up_sums[:, n * each : (n + 1) * each]
        for side, low in ((0, n * lines), (1, half + n * lines)):
            rows[low : low + 1, UP_AT : UP_AT + each] = jnp.where(at[T] == side, value, 0.0)
    small = rows[...]
    put_gradient(layer_in, d_projected, grads, at[CORE])
    if len(grads) == 1:
        grads[0][:, cols:] = small.astype(LOW)
    else:
        put_blocks(small, grads[0], grads[-1], at[CORE], cols)


def projection_back_kernel(at, d_projected, wqkv, d_attn, d_own, d_sent):
    padded, cols = d_own.shape[0], d_projected.shape[1]
    t = at[T]
    d_own[...] = d_attn[...] + nt(half_rows_of(d_projected, t, padded), wqkv[:, :cols])
    d_sent[...] = nt(half_rows_of(d_projected, 1 - t, padded), wqkv[:, :cols]).astype(LOW)


def finish_kernel(
    part, small_rows, count, at, *refs
):
    parts, (qkv, out, memory, vectors, gains, up, turn) = refs[:count], refs[count:]
    total = parts[0][...]
    for value in parts[1:]:
        total = total + value[...].astype(WIDE)
    lines = total.shape[0]
    cols, width = 3 * part, 2 * part
    mine, got = total[:, : cols + PAIR], total[:, cols + PAIR + width :]
    first = at[T] == 0
    for pair in range(part // PAIR):
        for kind in range(3):
            here = (3 * pair + kind) * PAIR
            a, b = mine[:, here : here + PAIR], got[:, here : here + PAIR]
            low = kind * width + pair * PAIR
            qkv[:, low : low + PAIR] = jnp.where(first, a, b)
            qkv[:, low + part : low + part + PAIR] = jnp.where(first, b, a)
    out[...] = total[:, cols + PAIR : cols + PAIR + width]
    turn[...] = jnp.zeros_like(turn)
    turn[:lines, :] = mine[:, cols:] + got[:, cols:]
    up[...] = turn[0:1, UP_AT : UP_AT + up.shape[1]]
    small = turn[...].T
    for target, (low, high) in zip((memory, vectors, gains), small_rows):
        target[...] = small[low:high, :lines]


def spread_of(v):
    return jnp.mean(v, axis=-1, keepdims=True)


def first_norm_kernel(bias, gain, at, own, got, wout, layer_in, small, mixed, unit, scale, normed, s):
    padded, part = own.shape
    first = at[T] == 0
    mixed[:, :part] = jnp.where(first, own[...], got[...])
    mixed[:, part:] = jnp.where(first, got[...], own[...])
    s[...] = nn(mixed[...], wout[...])
    for low in range(0, padded, ROWS):
        here = slice(low, low + ROWS)
        rows = layer_in[pl.ds(pl.multiple_of(at[T] * padded + low, ROWS), ROWS), :]
        total = rows.astype(WIDE) + (s[here, :] + small[bias + 2 : bias + 3, :])
        centered = total - spread_of(total)
        factor = lax.rsqrt(spread_of(centered * centered) + NORM_EPSILON)
        value = centered * factor
        unit[here, :] = value
        scale[here, :] = jnp.broadcast_to(factor, (ROWS, PAIR))
        value = value * small[gain : gain + 1, :] + small[bias + 3 : bias + 4, :]
        normed[here, :] = value.astype(LOW)


def add_sums(sums, values):
    sums[...] = jnp.zeros_like(sums)
    for n, value in enumerate(values):
        sums[n : n + 1, :] = jnp.sum(value, axis=0, keepdims=True)


def second_norm_kernel(
    bias, gain, start, at, unit, small, own, got, d_out, _, layer_out, d_second, d_ffn, sums
):
    width = unit.shape[1]
    real = d_out.shape[0] - start
    totals = [jnp.zeros((ROWS, width), WIDE)] * 3
    for low in range(0, got.shape[0], ROWS):
        here, there = slice(low, low + ROWS), slice(start + low, start + low + ROWS)
        count = min(ROWS, real - low)
        first = unit[there, :] * small[gain : gain + 1, :] + small[bias + 3 : bias + 4, :]
        ffn = own[there, :] + got[here, :].astype(WIDE) + small[bias + 4 : bias + 5, :]
        total = first + ffn
        centered = total - spread_of(total)
        factor = lax.rsqrt(spread_of(centered * centered) + NORM_EPSILON)
        value = centered * factor
        out = value * small[gain + 1 : gain + 2, :] + small[bias + 5 : bias + 6, :]
        layer_out[low : low + count, :] = out[:count].astype(LOW)
        cotangent = d_out[start + low : start + low + count, :].astype(WIDE)
        if count < ROWS:
            cotangent = jnp.concatenate(
                [cotangent, jnp.zeros((ROWS - count, width), WIDE)], axis=0
            )
        d_unit = cotangent * small[gain + 1 : gain + 2, :]
        back = factor * (d_unit - spread_of(d_unit) - value * spread_of(d_unit * value))
        d_second[here, :] = back
        rounded = back.astype(LOW)
        d_ffn[here, :] = rounded
        terms = (rounded.astype(WIDE), cotangent, cotangent * value)
        totals = [a + b for a, b in zip(totals, terms)]
    add_sums(sums, totals)


def first_back_kernel(
    gain, at, second0, second1, own, got, unit, scale, small, wout, d_attn_in, d_attn, mix_own, mix_sent, sums
):
    padded, width = unit.shape
    part = mix_own.shape[1]
    totals = [jnp.zeros((ROWS, width), WIDE)] * 3
    for low in range(0, padded, ROWS):
        here = slice(low, low + ROWS)
        cut = second0.shape[0]
        second = second0[here, :] if low < cut else second1[low - cut : low - cut + ROWS, :]
        cotangent = second + own[here, :] + got[here, :].astype(WIDE)
        value = unit[here, :]
        d_unit = cotangent * small[gain : gain + 1, :]
        back = d_unit - spread_of(d_unit) - value * spread_of(d_unit * value)
        back = scale[here, :1] * back
        d_attn_in[here, :] = back
        rounded = back.astype(LOW)
        d_attn[here, :] = rounded
        terms = (rounded.astype(WIDE), cotangent, cotangent * value)
        totals = [a + b for a, b in zip(totals, terms)]
    add_sums(sums, totals)
    mixed = nt(d_attn[...], wout[...]).astype(LOW)
    first = at[T] == 0
    mix_own[...] = jnp.where(first, mixed[:, :part], mixed[:, part:])
    mix_sent[...] = jnp.where(first, mixed[:, part:], mixed[:, :part])


def rows_kernel(mem_count, at, own, got, out):
    real = out.shape[0]
    row = lax.broadcasted_iota(jnp.int32, (32, 1), 0)
    fresh = (row < mem_count) & (at[FRESH] == 1) & (at[T] == 0)
    out[:32, :] = jnp.where(fresh, 0.0, own[:32, :] + got[:32, :].astype(WIDE))
    out[32:, :] = own[32:real, :] + got[32:real, :].astype(WIDE)


def gelu_parts(pre):
    cdf = 0.5 * (1.0 + lax.erf(pre * 0.7071067811865476))
    density = jnp.exp(-0.5 * pre * pre) * 0.3989422804014327
    return pre * cdf, cdf + pre * density


def shards(
    rows_in,
    d_out,
    starts,
    lengths,
    resets,
    qkv_weight,
    out_weight,
    bias_vec,
    gains,
    mem_init,
    ffn_up,
    up_bias,
    ffn_down,
):
    half_rows, seg_count, width = rows_in.shape
    assert seg_count == 1
    dp_count, t_count = lax.axis_size("dp"), lax.axis_size("tensor")
    assert t_count == 2
    digits = digits_of(dp_count)
    x_digit, core_digit = digits[-2:]
    padded = ceil_to(half_rows, 16)
    rows = 2 * padded
    mem_count = mem_init.shape[0]
    part = HEADS // t_count * HEAD
    cols = 3 * part
    hidden_mine = ffn_up.shape[1]
    feat = bias_vec.shape[1]
    lines = qkv_weight.shape[0]
    doc_count = starts.shape[1]
    counts = (mem_count, bias_vec.shape[0], gains.shape[0])
    edges = [sum(counts[:n]) for n in range(len(counts) + 1)]
    small_rows = tuple(zip(edges[:-1], edges[1:]))
    bias, gain = edges[1], edges[2]
    integers = [
        lax.axis_index("tensor"),
        digit_at(x_digit),
        digit_at(core_digit),
        digit_at(digits[-3]),
        lax.axis_index("dp"),
        resets[0],
        lengths[0],
    ]
    at = jnp.concatenate([jnp.stack(integers).astype(jnp.int32), starts[0]])

    side = lax.axis_index("tensor").astype(jnp.int32).reshape(1)
    (packed,) = call(
        functools.partial(columns_kernel, small_rows),
        [low_of(lines, 3 * width + PAIR + width)],
        side, qkv_weight, bias_vec, gains, mem_init, up_bias.reshape(1, -1), out_weight,
        scratch=[pltpu.VMEM((PAIR, PAIR), WIDE)],
        room=57 << 20,
    )
    rows_low = jnp.pad(tie(rows_in, packed)[:, 0, :], ((0, padded - half_rows), (0, 0)))
    rows_other = swap_tensor(rows_low)
    up_pair = spread_near(tie(ffn_up, packed), digits)
    first_z = spread_outer(packed, digits)
    first_z, rows_other, up_pair = join(first_z, rows_other, up_pair)
    slots = first_z.shape[0]
    mine, other = call(
        functools.partial(halves_of_heads_kernel, part),
        [low_of(slots, lines, cols + PAIR + width), low_of(slots, lines, cols + PAIR)],
        at, first_z,
    )
    first_parts = [mine, swap_tensor(other), rotate(mine, x_digit, 1), swap_both(other, x_digit)]
    up_z = spread_far(up_pair, digits)
    down_pair = spread_near(tie(ffn_down.T, mine), digits)
    *first_parts, up_z, down_pair = join(*first_parts, up_z, down_pair)
    first_parts = [jnp.concatenate(first_parts[n : n + 2], axis=2) for n in (0, 2)]
    core_parts = [rotate(value, core_digit, 1) for value in first_parts]
    sizes = tuple(size for _, size in digits)
    (wqkv,) = call(
        functools.partial(assemble_first_kernel, sizes),
        [low_of(dp_count, 2 * lines, cols + PAIR)],
        at, *first_parts, *core_parts,
    )
    wqkv = wqkv.reshape(width, cols + PAIR)
    (out_sent,) = call(
        functools.partial(beside_kernel, cols + PAIR),
        [low_of(dp_count // 2, lines, width)], at, *first_parts,
    )
    out_got = swap_tensor(out_sent)
    up_x = rotate(up_z, x_digit, 1)
    down_z = spread_far(down_pair, digits)

    projected, mix_own, mix_sent, log_total, layer_in, small = call(
        functools.partial(forward_kernel, half_rows, mem_count, doc_count, bias),
        [
            low_of(rows, cols),
            low_of(padded, part),
            low_of(padded, part),
            wide_of(rows, PAIR),
            low_of(rows, width),
            wide_of(ceil_to(edges[-1], 32), width),
        ],
        at, rows_low, rows_other, wqkv,
        scratch=[
            pltpu.VMEM((rows, rows), WIDE),
            pltpu.VMEM((rows, PAIR), WIDE),
            pltpu.VMEM((rows, PAIR), LOW),
        ],
    )
    mix_got = swap_tensor(mix_sent)
    out_got = tie(out_got, mix_sent)
    (wout,) = call(
        functools.partial(assemble_out_kernel, sizes, cols + PAIR),
        [low_of(dp_count, 2 * lines, width)],
        at, *first_parts, *core_parts, out_got, rotate(out_got, core_digit, 1),
    )
    wout = wout.reshape(width, width)
    mixed, unit, scale, normed_own = call(
        functools.partial(first_norm_kernel, bias, gain),
        [low_of(padded, width), wide_of(padded, width), wide_of(padded, PAIR), low_of(padded, width)],
        at, mix_own, mix_got, wout, layer_in, small,
        scratch=[pltpu.VMEM((padded, width), WIDE)],
    )

    normed_got = swap_tensor(normed_own)
    up_x, up_z, down_z = tie(up_x, mix_sent), tie(up_z, mix_sent), tie(down_z, mix_sent)
    up = assemble(at, swap_blocks(up_z, up_x, digits), digits, hidden_mine, paired=True)
    (up_b,) = call(
        functools.partial(up_row_kernel, lines), [wide_of(ROWS, hidden_mine)], at, wqkv,
        scratch=[pltpu.VMEM((1, hidden_mine), WIDE)],
    )
    down_x = rotate(down_z, x_digit, 1)
    normed_got, down_x, up_b, up = join(normed_got, down_x, up_b, up)
    down_t = assemble(at, swap_blocks(down_z, down_x, digits), digits, hidden_mine, paired=True)

    def feed_forward(rows):
        pre_act = nn(rows, up).reshape(-1, *up_b.shape) + up_b
        hidden, slope = (part.reshape(rows.shape[0], -1) for part in gelu_parts(pre_act))
        hidden = hidden.astype(LOW)
        return hidden, slope, nt(hidden, down_t)

    cut = ceil_to(padded // 2, ROWS)
    pieces = ((0, cut), (cut, padded))
    hidden_got, slope_got, ffn_sent = feed_forward(normed_got)
    ffn_sent = ffn_sent.astype(LOW)
    ffn_got = [swap_tensor(ffn_sent[low:high]) for low, high in pieces]
    hidden_own, slope_own, ffn_own = feed_forward(tie(normed_own, ffn_sent))
    d_out_rows = d_out.reshape(half_rows, width)
    second, ahead = [], small
    for (low, high), got in zip(pieces, ffn_got):
        if second:
            ahead = rotate(second[-1][2][:ROWS, :PAIR], core_digit, 1)
        outs = [
            low_of(min(high, half_rows) - low, width),
            wide_of(high - low, width),
            low_of(high - low, width),
            wide_of(8, width),
        ]
        kernel = functools.partial(second_norm_kernel, bias, gain, low)
        second.append(call(kernel, outs, at, unit, small, ffn_own, got, d_out_rows, ahead))
    layer_out, d_second, d_ffn_sent, sums_two = zip(*second)

    d_ffn_got = jnp.concatenate([swap_tensor(piece) for piece in d_ffn_sent], axis=0)
    d_ffn_own = jnp.concatenate(d_ffn_sent, axis=0)

    def feed_back(rows, slope):
        d_pre = (slope * nn(rows, down_t)).astype(LOW)
        return d_pre, nt(d_pre, up)

    d_pre_own, d_first_own = feed_back(d_ffn_own, slope_own)
    down_own, up_own, sums_own = call(
        own_kernel,
        [wide_of(width, hidden_mine), wide_of(width, hidden_mine), wide_of(1, hidden_mine)],
        at, d_ffn_own, hidden_own, normed_own, d_pre_own,
    )
    d_ffn_got, d_first_own, down_own, up_own = join(d_ffn_got, d_first_own, down_own, up_own)
    d_pre_got, d_first_sent = feed_back(d_ffn_got, slope_got)
    d_first_sent = d_first_sent.astype(LOW)
    d_first_got = swap_tensor(d_first_sent)

    outs = gradient_outs(width, hidden_mine, dp_count)
    down_grads = call(
        rest_kernel, outs, at, down_own, tie(d_ffn_got, d_first_sent), hidden_got
    )
    down_kept, down_sent = halve(at, *swap_cores(down_grads, dp_count, core_digit))
    down_got = rotate(down_sent, x_digit, 1)
    up_sums, *up_grads = call(
        rest_sums_kernel, [wide_of(1, hidden_mine)] + outs,
        at, up_own, sums_own, normed_got, tie(d_pre_got, down_sent),
    )
    up_kept, up_sent = halve(at, *swap_cores(up_grads, dp_count, core_digit))

    d_attn_in, d_attn, d_mix_own, d_mix_sent, sums_one = call(
        functools.partial(first_back_kernel, gain),
        [
            wide_of(padded, width),
            low_of(padded, width),
            low_of(padded, part),
            low_of(padded, part),
            wide_of(8, width),
        ],
        at, *d_second, d_first_own, d_first_got, unit, scale, small, wout,
    )
    d_mix_got = swap_tensor(d_mix_sent)
    out_grads = call(
        out_gradient_kernel, gradient_outs(width, width, dp_count, OUT_TILE),
        at, mixed, tie(d_attn, d_mix_sent),
    )
    out_kept, out_parts = swap_cores(out_grads, dp_count, core_digit)
    out_kept, out_sent = call(
        rows_halves_kernel, [low_of(dp_count // 2, lines, width)] * 2, at, out_kept, *out_parts
    )
    down_kept, down_sent = far_parts(at, down_kept, down_got, digits)
    d_mix_got, out_sent, up_sent, down_sent = join(d_mix_got, out_sent, up_sent, down_sent)
    down_got = rotate(down_sent, digits[-3], 2)
    out_got = swap_tensor(out_sent)
    up_got = rotate(up_sent, x_digit, 1)

    d_projected, proj_sums = call(
        functools.partial(backward_kernel, half_rows, mem_count, doc_count),
        [low_of(rows, cols), wide_of(1, cols)],
        at, projected, d_mix_own, d_mix_got, log_total,
        scratch=[
            pltpu.VMEM((rows, rows), WIDE),
            pltpu.VMEM((2 * rows, PAIR), WIDE),
            pltpu.VMEM((2 * rows, rows), LOW),
            pltpu.VMEM((2 * rows, rows), LOW),
            pltpu.VMEM((rows, part), LOW),
        ],
    )
    up_kept, up_sent = far_parts(at, up_kept, up_got, digits)
    qkv_grads = call(
        functools.partial(projection_gradient_kernel, small_rows, lines),
        gradient_outs(width, cols + PAIR, dp_count),
        at, layer_in, d_projected, proj_sums, sums_one, *sums_two, up_sums, wqkv, d_attn_in,
        scratch=[pltpu.VMEM((PAIR, width), WIDE), pltpu.VMEM((width, PAIR), WIDE)],
    )
    out_got, down_got, *qkv_grads = join(out_got, down_got, *qkv_grads)
    down_kept, down_sent = near_parts(at, down_kept, down_got)
    qkv_kept, qkv_parts = swap_cores(qkv_grads, dp_count, core_digit)
    up_sent, *qkv_parts = join(up_sent, *qkv_parts)
    slots = dp_count // 4
    mine, to_x, to_y, to_both = call(
        quarter_kernel,
        [low_of(slots, lines, cols + PAIR + width)] * 2 + [low_of(slots, lines, cols + PAIR)] * 2,
        at, qkv_kept, *qkv_parts, out_kept, out_got,
    )

    both_got = [rotate(to_x, x_digit, 1), swap_tensor(to_y), swap_both(to_both, x_digit)]
    up_got = rotate(up_sent, digits[-3], 2)
    down_got = swap_near(down_sent, digits[-3])
    d_in_own, d_in_sent = call(
        projection_back_kernel, [wide_of(padded, width), low_of(padded, width)],
        at, tie(d_projected, to_x), wqkv, d_attn_in,
    )
    up_kept, up_sent = near_parts(at, up_kept, up_got)
    *both_got, d_in_sent, up_sent, down_got = join(*both_got, d_in_sent, up_sent, down_got)
    up_got = swap_near(up_sent, digits[-3])
    d_in_got = swap_tensor(d_in_sent)
    both_kept, both_sent = outer_parts(at, digits, mine, *both_got)
    both_got = outer_send(both_sent, digits)
    grad_ffn_down = outer_sum(down_kept, [down_got], digits)
    grad_ffn_up = outer_sum(up_kept, [up_got], digits)
    (grad_rows,) = call(
        functools.partial(rows_kernel, mem_count), [wide_of(half_rows, width)], at, d_in_own, d_in_got
    )
    grad_rows, *both_got = join(grad_rows, *both_got)

    if len(digits) == 3:
        parts = [both_kept[0], *[part[0] for part in both_got]]
    else:
        parts = [outer_sum(both_kept, both_got, digits)]
    grad_qkv, grad_out_weight, grad_mem, grad_vec, grad_gains, grad_up_bias = call(
        functools.partial(finish_kernel, part, small_rows, len(parts)),
        [wide_of(lines, 3 * width), wide_of(lines, width)]
        + [wide_of(n, feat) for n in counts]
        + [wide_of(1, up_bias.shape[0])],
        at, *parts,
        scratch=[pltpu.VMEM((PAIR, PAIR), WIDE)],
    )
    return (
        jnp.concatenate(layer_out, axis=0).reshape(half_rows, 1, width),
        grad_rows.reshape(half_rows, 1, width),
        grad_qkv,
        grad_out_weight,
        grad_vec,
        grad_gains,
        grad_mem,
        grad_ffn_up,
        grad_up_bias.reshape(up_bias.shape),
        grad_ffn_down.T,
    )


def solution(mesh):
    both = ("dp", "tensor")
    in_specs = (
        P("tensor", "dp", None),
        P("tensor", "dp", None),
        P("dp", None),
        P("dp"),
        P("dp"),
        P(both, None),
        P(both, None),
        P(None, both),
        P(None, both),
        P(None, both),
        P("dp", "tensor"),
        P(both),
        P("tensor", "dp"),
    )
    out_specs = (
        P("tensor", "dp", None),
        P("tensor", "dp", None),
        P(both, None),
        P(both, None),
        P(None, both),
        P(None, both),
        P(None, both),
        P("dp", "tensor"),
        P(both),
        P("tensor", "dp"),
    )
    return jax.shard_map(shards, mesh=mesh, in_specs=in_specs, out_specs=out_specs, check_vma=False)
```

```python
import functools

import jax
import jax.numpy as jnp
import numpy as np
from jax import lax
from jax.experimental import pallas as pl
from jax.experimental.pallas import tpu as pltpu
from jax.sharding import PartitionSpec as P

HEADS = 12
HEAD = 64
NORM_EPSILON = 1e-06
LOW = jnp.bfloat16
WIDE = jnp.float32
CHUNK = 32
FORWARD_BLOCK = 272
BACKWARD_BLOCK = 544
TILE = 384
OUT_TILE = 256
ROWS = 16
PAIR = 2 * HEAD
UP_AT = 32
QUICK = pl.CostEstimate(flops=1, bytes_accessed=1, transcendentals=0)
T, X, CORE, OUTER, DP, FRESH, LENGTH, STARTS = range(8)


def ceil_to(count, unit):
    return -(-count // unit) * unit


def nn(a, b):
    return lax.dot_general(a, b, (((1,), (0,)), ((), ())), preferred_element_type=WIDE)


def nt(a, b):
    return lax.dot_general(a, b, (((1,), (1,)), ((), ())), preferred_element_type=WIDE)


def tn(a, b):
    return lax.dot_general(a, b, (((0,), (0,)), ((), ())), preferred_element_type=WIDE)


def low_of(*shape):
    return jax.ShapeDtypeStruct(shape, LOW)


def wide_of(*shape):
    return jax.ShapeDtypeStruct(shape, WIDE)


def held_bytes(array):
    rows, cols = ((1,) + tuple(array.shape))[-2:]
    lead = int(np.prod(array.shape[:-2])) if len(array.shape) > 2 else 1
    return lead * ceil_to(rows, 16) * ceil_to(cols, 128) * jnp.dtype(array.dtype).itemsize


def call(kernel, outs, at, *arrays, scratch=(), room=0):
    room += sum(held_bytes(array) for array in (*arrays, *outs))
    room += sum(held_bytes(ref) for ref in scratch)
    return pl.pallas_call(
        kernel,
        in_specs=[pl.BlockSpec(memory_space=pltpu.SMEM)]
        + [pl.BlockSpec(memory_space=pltpu.VMEM)] * len(arrays),
        out_specs=[pl.BlockSpec(memory_space=pltpu.VMEM)] * len(outs),
        out_shape=list(outs),
        scratch_shapes=list(scratch),
        compiler_params=pltpu.CompilerParams(vmem_limit_bytes=room + (9 << 20)),
        cost_estimate=QUICK,
    )(at, *arrays)


def digits_of(dp_count):
    assert dp_count % 4 == 0
    sizes = [2, 2]
    left = dp_count // 4
    while left > 1:
        size = next((s for s in (4, 2, 3) if left % s == 0), left)
        sizes.append(size)
        left //= size
    if len(sizes) == 2:
        sizes.append(1)
    digits, stride = [], 1
    for size in sizes:
        digits.append((stride, size))
        stride *= size
    return digits[::-1]


def digit_at(digit):
    stride, size = digit
    return (lax.axis_index("dp") // stride) % size


def rotate(value, digit, step):
    stride, size = digit
    pairs = []
    for at in range(lax.axis_size("dp")):
        mine = (at // stride) % size
        pairs.append((at, at + ((mine + step) % size - mine) * stride))
    return lax.ppermute(value, "dp", pairs)


def swap_tensor(value):
    return lax.ppermute(value, "tensor", [(0, 1), (1, 0)])


def swap_both(value, digit):
    stride, _ = digit
    pairs = []
    for at in range(lax.axis_size("dp")):
        other = at + stride if (at // stride) % 2 == 0 else at - stride
        pairs += [(2 * at + side, 2 * other + 1 - side) for side in range(2)]
    return lax.ppermute(value, ("dp", "tensor"), pairs)


def tie(value, *others):
    return lax.optimization_barrier((value,) + others)[0]


join = lambda *values: lax.optimization_barrier(values)


def spread_outer(value, digits):
    for digit in reversed(digits[:-2]):
        got = [value] + [rotate(value, digit, step) for step in range(1, digit[1])]
        value = jnp.stack(got)
    return value.reshape((-1,) + value.shape[-2:])


def swap_near(value, digit):
    stride, _ = digit
    pairs = []
    for at in range(lax.axis_size("dp")):
        pairs.append((at, at + stride if (at // stride) % 2 == 0 else at - stride))
    return lax.ppermute(value, "dp", pairs)


def spread_near(value, digits):
    assert digits[-3][1] == 4
    return jnp.stack([value, swap_near(value, digits[-3])])


def spread_far(pair, digits):
    value = jnp.concatenate([pair, rotate(pair, digits[-3], 2)], axis=0)
    for digit in reversed(digits[:-3]):
        value = jnp.stack([value] + [rotate(value, digit, step) for step in range(1, digit[1])])
    return value.reshape((-1,) + value.shape[-2:])


def spread_far_pieces(pair, digits):
    pieces = [pair, rotate(pair, digits[-3], 2)]
    for digit in reversed(digits[:-3]):
        for n, value in enumerate(pieces):
            value = jnp.stack([value] + [rotate(value, digit, step) for step in range(1, digit[1])])
            pieces[n] = value.reshape((-1,) + value.shape[-2:])
    return pieces


def placer(sizes, me, paired):
    outer, digits = sizes[:-2], []
    for size in reversed(sizes):
        digits.append(lax.rem(me, size))
        me = lax.div(me, size)
    digits = digits[::-1]

    def place_of(swap_core, swap_x, slot):
        steps = []
        for size in reversed(outer):
            steps.append(slot % size)
            slot //= size
        place = 0
        for n, (size, digit, step) in enumerate(zip(outer, digits, steps[::-1])):
            if paired and n == len(outer) - 1:
                at = lax.bitwise_xor(digit, step)
            else:
                at = lax.rem(digit + (size - step), size)
            place = place * size + at
        x, core = digits[-2], digits[-1]
        place = place * 2 + (1 - x if swap_x else x)
        return place * 2 + (1 - core if swap_core else core)

    return place_of


def assemble_kernel(sizes, paired, at, *refs):
    *parts, whole = refs
    cols = whole.shape[2]
    pieces = len(parts) // 4
    place_of = placer(sizes, at[DP], paired)
    for swap_core in range(2):
        for swap_x in range(2):
            for piece in range(pieces):
                source = parts[pieces * (2 * swap_core + swap_x) + piece]
                for block in range(source.shape[0]):
                    slot = 2 * (pieces * (block // 2) + piece) + block % 2
                    whole[place_of(swap_core, swap_x, slot)] = source[block, :, :cols]


def swap_blocks(mine, x_got, digits):
    core = digits[-1]
    return [mine, x_got, rotate(mine, core, 1), rotate(x_got, core, 1)]


def swap_pieces(mine, x_got, digits):
    core = digits[-1]
    return [*mine, *x_got] + [rotate(piece, core, 1) for piece in (*mine, *x_got)]


def assemble(at, parts, digits, cols, paired=False):
    rows = parts[0].shape[1]
    blocks = sum(part.shape[0] for part in parts)
    sizes = tuple(size for _, size in digits)
    (whole,) = call(
        functools.partial(assemble_kernel, sizes, paired),
        [low_of(blocks, rows, cols)],
        at,
        *parts,
    )
    return whole.reshape(blocks * rows, cols)


def assemble_first_kernel(sizes, at, *refs):
    parts, whole = refs[:4], refs[4]
    lines, cols = whole.shape[1] // 2, whole.shape[2]
    place_of = placer(sizes, at[DP], False)
    first = at[T] == 0
    for swap_core in range(2):
        for swap_x in range(2):
            source = parts[2 * swap_core + swap_x]
            far = source.shape[2] - cols
            for slot in range(source.shape[0]):
                place = place_of(swap_core, swap_x, slot)
                a, b = source[slot, :, :cols], source[slot, :, far:]
                whole[place, :lines] = jnp.where(first, a, b)
                whole[place, lines:] = jnp.where(first, b, a)


def assemble_out_kernel(sizes, cols, at, *refs):
    parts, gots, whole = refs[:4], refs[4:6], refs[6]
    place_of = placer(sizes, at[DP], False)
    first = at[T] == 0
    lines, width = whole.shape[1] // 2, whole.shape[2]
    for swap_core in range(2):
        for swap_x in range(2):
            source, got = parts[2 * swap_core + swap_x], gots[swap_core]
            slots = source.shape[0]
            for slot in range(slots):
                mine, other = source[slot, :, cols : cols + width], got[swap_x * slots + slot]
                place = place_of(swap_core, swap_x, slot)
                whole[place, :lines] = jnp.where(first, mine, other)
                whole[place, lines:] = jnp.where(first, other, mine)


def columns_kernel(small_rows, at, weight, vectors, gains, memory, up, out, packed, turn):
    lines, width = weight.shape
    packed[:, :width] = weight[...]
    turn[...] = jnp.zeros_like(turn)
    for source, (low, high) in zip((memory, vectors, gains), small_rows):
        turn[low:high, :lines] = source[...].astype(WIDE)
    columns = turn[...].T[:lines]
    turn[:lines, :] = columns
    turn[0:1, UP_AT : UP_AT + up.shape[1]] = up[...].astype(WIDE)
    packed[:, width : width + PAIR] = turn[:lines, :].astype(LOW)
    packed[:, width + PAIR :] = out[...]


def halves_of_heads_kernel(part, at, packed, mine, other):
    width = 6 * part
    first = at[T] == 0
    for slot in range(packed.shape[0]):
        for pair in range(part // PAIR):
            for kind in range(3):
                low = 2 * kind * part + pair * PAIR
                a = packed[slot, :, low : low + PAIR]
                b = packed[slot, :, low + part : low + part + PAIR]
                here = (3 * pair + kind) * PAIR
                mine[slot, :, here : here + PAIR] = jnp.where(first, a, b)
                other[slot, :, here : here + PAIR] = jnp.where(first, b, a)
        mine[slot, :, 3 * part :] = packed[slot, :, width:]
        other[slot, :, 3 * part :] = packed[slot, :, width : width + PAIR]


def beside_kernel(cols, at, mine, x_got, out):
    slots = mine.shape[0]
    for n, source in enumerate((mine, x_got)):
        for slot in range(slots):
            out[n * slots + slot] = source[slot, :, cols : cols + out.shape[2]]


def put_blocks(total, kept, sent, core, at):
    groups, rows, _ = kept.shape
    cols = total.shape[1]
    total = total.astype(LOW).reshape(2 * groups, rows, cols)
    second = core == 1
    for group in range(groups):
        even, odd = total[2 * group], total[2 * group + 1]
        kept[group, :, at : at + cols] = jnp.where(second, odd, even)
        sent[group] = jnp.where(second, even, odd)


def put_gradient(a, b, outs, core, own=None, tile=TILE):
    whole = tn(a[...], b[...])
    for n, low in enumerate(range(0, b.shape[1], tile)):
        total = whole[:, low : low + tile]
        if own is not None:
            total = total + own[:, low : low + tile]
        if len(outs) == 1:
            outs[0][:, low : low + tile] = total.astype(LOW)
        else:
            put_blocks(total, outs[0], outs[1 + n], core, low)


def gradient_outs(width, cols, dp_count, tile=TILE):
    rows = width // dp_count
    if rows % 16:
        return [low_of(width, cols)]
    tiles = [min(tile, cols - low) for low in range(0, cols, tile)]
    return [low_of(dp_count // 2, rows, n) for n in [cols] + tiles]


def swap_cores(outs, dp_count, digit):
    if len(outs) == 1:
        whole = outs[0].reshape(dp_count // 2, 2, -1, outs[0].shape[1])
        core = digit_at(digit)
        take = lambda which: lax.dynamic_index_in_dim(whole, which, 1, keepdims=False)
        outs = [take(core), take(1 - core)]
    return outs[0], [rotate(part, digit, 1) for part in outs[1:]]


def out_gradient_kernel(at, a, b, *outs):
    put_gradient(a, b, outs, at[CORE], tile=OUT_TILE)


def rows_halves_kernel(at, mine, *refs):
    got, (kept, sent) = refs[:-2], refs[-2:]
    lines = kept.shape[1]
    first = at[T] == 0
    for group in range(mine.shape[0]):
        low = 0
        for part in got:
            high = low + part.shape[2]
            total = mine[group, :, low:high].astype(WIDE) + part[group].astype(WIDE)
            a, b = total[:lines], total[lines:]
            kept[group, :, low:high] = jnp.where(first, a, b).astype(LOW)
            sent[group, :, low:high] = jnp.where(first, b, a).astype(LOW)
            low = high


def own_forward_kernel(at, normed, up, up_b, down_t, _, hidden, slope, out):
    pre_act = nn(normed[...], up[...]).reshape(-1, *up_b.shape) + up_b[...]
    active, slopes = (value.reshape(hidden.shape) for value in gelu_parts(pre_act))
    hidden[...] = active.astype(LOW)
    slope[...] = slopes
    out[...] = nt(hidden[...], down_t[...])


def own_kernel(at, a_down, b_down, a_up, b_up, down, up, sums):
    tile = 384
    for low in range(0, b_down.shape[1], tile):
        here = slice(low, low + tile)
        down[:, here] = tn(a_down[...], b_down[:, here])
        up[:, here] = tn(a_up[...], b_up[:, here])
    sums[...] = jnp.sum(b_up[...].astype(WIDE), axis=0, keepdims=True)


def rest_kernel(at, own, a, b, *outs):
    put_gradient(a, b, outs, at[CORE], own=own)


def rest_sums_kernel(at, own, own_sums, a, b, sums, *outs):
    put_gradient(a, b, outs, at[CORE], own=own)
    sums[...] = own_sums[...] + jnp.sum(b[...].astype(WIDE), axis=0, keepdims=True)


def up_row_kernel(lines, at, w, row, line):
    half, each = w.shape[0] // 2, row.shape[1] * lines * 2 // w.shape[0]
    low = w.shape[1] - PAIR
    for n in range(half // lines):
        a = w[n * lines : n * lines + 1, low:].astype(WIDE)
        b = w[half + n * lines : half + n * lines + 1, low:].astype(WIDE)
        value = jnp.where(at[T] == 0, a, b)[:, UP_AT : UP_AT + each]
        line[:, n * each : (n + 1) * each] = value
    row[...] = jnp.broadcast_to(line[...], row.shape)


def halve_kernel(at, mine, *refs):
    got, (kept, sent) = refs[:-2], refs[-2:]
    x = at[X]
    for group in range(kept.shape[0]):
        for other, out in ((0, kept), (1, sent)):
            place = 2 * group + (1 - x if other else x)
            low = 0
            for part in got:
                high = low + part.shape[2]
                total = mine[place, :, low:high].astype(WIDE) + part[place].astype(WIDE)
                out[group, :, low:high] = total.astype(LOW)
                low = high


def halve(at, mine, got):
    groups, rows, cols = mine.shape
    return call(halve_kernel, [low_of(groups // 2, rows, cols)] * 2, at, mine, *got)


def quarter_kernel(at, mine, *refs):
    got, (out_mine, out_got, keep, to_x, to_y, to_both) = refs[:-6], refs[-6:]
    lines, cols = to_y.shape[1:]
    first = at[T] == 0
    for group in range(keep.shape[0]):
        own, other = 2 * group + at[X], 2 * group + 1 - at[X]
        for place, same, across in ((own, keep, to_y), (other, to_x, to_both)):
            low = 0
            for part in got:
                high = low + part.shape[2]
                total = mine[place, :, low:high].astype(WIDE) + part[place].astype(WIDE)
                a, b = total[:lines], total[lines:]
                same[group, :, low:high] = jnp.where(first, a, b).astype(LOW)
                across[group, :, low:high] = jnp.where(first, b, a).astype(LOW)
                low = high
            total = out_mine[place].astype(WIDE) + out_got[place].astype(WIDE)
            same[group, :, cols:] = total.astype(LOW)


def parts_kernel(size, at, mine, x_got, y_got, both_got, *outs):
    me = at[OUTER]
    cols = mine.shape[2]
    for group in range(outs[0].shape[0]):
        for step, out in enumerate(outs):
            place = group * size + lax.rem(me + step, size)
            total = mine[place].astype(WIDE) + x_got[place].astype(WIDE)
            out[group, :, :cols] = total.astype(out.dtype)
            total = y_got[place].astype(WIDE) + both_got[place].astype(WIDE)
            out[group, :, cols:] = total.astype(out.dtype)


def outer_parts(at, digits, *parts):
    size = digits[-3][1]
    blocks, rows, cols = parts[0].shape
    shape = (blocks // size, rows, cols + parts[2].shape[2])
    outs = [wide_of(*shape)] + [low_of(*shape)] * (size - 1)
    kept, *sent = call(functools.partial(parts_kernel, size), outs, at, *parts)
    return kept, sent


def far_kernel(at, mine, got, kept, sent):
    me = at[OUTER]
    pair = lax.bitwise_xor(me, 1)
    for group in range(kept.shape[0] // 2):
        for n, block in enumerate((me, pair)):
            for out, place in ((kept, block), (sent, lax.bitwise_xor(block, 2))):
                spot = 4 * group + place
                total = mine[spot].astype(WIDE) + got[spot].astype(WIDE)
                out[2 * group + n] = total.astype(out.dtype)


def near_kernel(at, mine, got, *refs):
    kept, sent = refs[-2:]
    for group in range(kept.shape[0]):
        kept[group] = mine[2 * group] + got[2 * group].astype(WIDE)
        total = mine[2 * group + 1] + got[2 * group + 1].astype(WIDE)
        sent[group] = total.astype(LOW)


def far_parts(at, mine, got, digits):
    assert digits[-3][1] == 4
    blocks, rows, cols = mine.shape
    return call(
        far_kernel, [wide_of(blocks // 2, rows, cols), low_of(blocks // 2, rows, cols)], at, mine, got
    )


def near_parts(at, mine, got, *ahead):
    blocks, rows, cols = mine.shape
    outs = [wide_of(blocks // 2, rows, cols), low_of(blocks // 2, rows, cols)]
    return call(near_kernel, outs, at, mine, got, *ahead)


def outer_send(sent, digits):
    return [rotate(part, digits[-3], step + 1) for step, part in enumerate(sent)]


def outer_sum(kept, got, digits):
    for part in got:
        kept = kept + part.astype(WIDE)
    for digit in reversed(digits[:-3]):
        size = digit[1]
        kept = kept.reshape((-1, size) + kept.shape[1:])
        at = digit_at(digit)
        take = lambda step: lax.dynamic_index_in_dim(kept, (at + step) % size, 1, keepdims=False)
        total = take(0)
        for step in range(1, size):
            total = total + rotate(take(step).astype(LOW), digit, step).astype(WIDE)
        kept = total
    return kept[0]


def fill_mask(mask, at, half_rows, mem_count, starts):
    rows = mask.shape[0]
    padded = rows // 2

    def places(shape, axis):
        spot = lax.broadcasted_iota(jnp.int32, shape, axis)
        second = spot >= padded
        within = jnp.where(second, spot - padded, spot)
        pos = within + jnp.where(second, half_rows, 0) - mem_count
        doc = jnp.zeros(shape, jnp.int32)
        for i in range(starts):
            doc = doc + (at[STARTS + i] <= pos).astype(jnp.int32)
        return within < half_rows, pos, doc

    _, q_pos, q_doc = places((rows, 1), 0)
    real, k_pos, k_doc = places((1, rows), 1)
    key_ok = real & (k_pos < at[LENGTH])
    for low in range(0, rows, CHUNK):
        qp, qd = q_pos[low : low + CHUNK], q_doc[low : low + CHUNK]
        same = (qd == k_doc) | (qp < 0) | (k_pos < 0)
        mask[low : low + CHUNK, :] = jnp.where(same & key_ok, 0.0, -1e9)


def heads_apart(pair):
    lane = lax.broadcasted_iota(jnp.int32, (1, PAIR), 1)
    zero = jnp.zeros((), LOW)
    return jnp.concatenate(
        [jnp.where(lane < HEAD, pair, zero), jnp.where(lane < HEAD, zero, pair)], axis=0
    )


def lanes(pair, count):
    return pl.ds(pl.multiple_of(pair * count, PAIR), count)


def forward_kernel(
    half_rows, mem_count, starts, first_bias,
    at, own, other, w, qkv, mix_own, mix_sent, lse, x, small, mask, s, mixed,
):
    rows, padded = x.shape[0], own.shape[0]
    t = at[T]
    part = mix_own.shape[1]
    fill_mask(mask, at, half_rows, mem_count, starts)
    lse[...] = jnp.zeros_like(lse)
    small[...] = w[:, 3 * part :].astype(WIDE).T[: small.shape[0]]
    x[pl.ds(pl.multiple_of(t * padded, 16), padded), :] = own[...]
    x[pl.ds(pl.multiple_of((1 - t) * padded, 16), padded), :] = other[...]
    row = lax.broadcasted_iota(jnp.int32, (32, 1), 0)
    fresh = (row < mem_count) & (at[FRESH] == 1)
    x[:32, :] = jnp.where(fresh, small[:32, :], x[:32, :].astype(WIDE)).astype(LOW)
    lane = lax.broadcasted_iota(jnp.int32, (1, PAIR), 1)
    scale = jnp.where(lax.broadcasted_iota(jnp.int32, (1, 3 * PAIR), 1) < PAIR, 0.125, 1.0)

    def one_pair(pair, _):
        here = pl.ds(pl.multiple_of(t * part + pair * PAIR, PAIR), PAIR)
        q_bias = small[first_bias : first_bias + 1, here]
        v_bias = small[first_bias + 1 : first_bias + 2, here]
        bias = jnp.concatenate([q_bias, jnp.zeros_like(q_bias), v_bias], axis=1)
        got = (nn(x[...], w[:, lanes(pair, 3 * PAIR)]) + bias).astype(LOW)
        got = (got.astype(WIDE) * scale).astype(LOW)
        qkv[:, lanes(pair, 3 * PAIR)] = got
        keys, values = got[:, PAIR : 2 * PAIR], got[:, 2 * PAIR :]
        q = heads_apart(got[:, :PAIR])
        for low in range(0, 2 * rows, FORWARD_BLOCK):
            here, there = slice(low, low + FORWARD_BLOCK), slice(low % rows, low % rows + FORWARD_BLOCK)
            v = nt(q[here], keys) + mask[there, :]
            top = jnp.max(v, axis=-1, keepdims=True)
            e = jnp.exp(v - top)
            total = jnp.sum(e, axis=-1, keepdims=True)
            out = nn((e * (1.0 / total)).astype(LOW), values)
            spot = lane == 2 * pair + low // rows
            lse[there, :] = jnp.where(spot, top + jnp.log(total), lse[there, :])
            if low < rows:
                s[there, :] = out
            else:
                mixed[there, :] = jnp.where(lane < HEAD, s[there, :], out).astype(LOW)
        mix_own[:, lanes(pair, PAIR)] = mixed[pl.ds(pl.multiple_of(t * padded, 16), padded), :]
        mix_sent[:, lanes(pair, PAIR)] = mixed[
            pl.ds(pl.multiple_of((1 - t) * padded, 16), padded), :
        ]
        return 0

    lax.fori_loop(0, part // PAIR, one_pair, 0)


def backward_kernel(
    half_rows, mem_count, starts, at, qkv, own, got, lse, dproj, sums, mask, s, p, ds, dmix
):
    rows, padded = qkv.shape[0], own.shape[0]
    part = own.shape[1]
    t = at[T]
    fill_mask(mask, at, half_rows, mem_count, starts)
    dmix[pl.ds(pl.multiple_of(t * padded, 16), padded), :] = own[...]
    dmix[pl.ds(pl.multiple_of((1 - t) * padded, 16), padded), :] = got[...]
    lane = lax.broadcasted_iota(jnp.int32, (1, PAIR), 1)
    zero = jnp.zeros((), LOW)

    def one_pair(pair, _):
        here = lanes(pair, 3 * PAIR)
        whole = qkv[:, here]
        keys, values = whole[:, PAIR : 2 * PAIR], whole[:, 2 * PAIR :]
        dm_pair = dmix[:, lanes(pair, PAIR)]
        q, dm = heads_apart(whole[:, :PAIR]), heads_apart(dm_pair)
        for low in range(0, 2 * rows, BACKWARD_BLOCK):
            block, there = slice(low, low + BACKWARD_BLOCK), slice(low % rows, low % rows + BACKWARD_BLOCK)
            spot = lane == 2 * pair + low // rows
            stat = jnp.sum(jnp.where(spot, lse[there, :], 0.0), axis=-1, keepdims=True)
            e = jnp.exp(nt(q[block], keys) + mask[there, :] - stat)
            d = nt(dm[block], values)
            dot = jnp.sum(e * d, axis=-1, keepdims=True)
            p[block, :] = e.astype(LOW)
            d = (e * (d - dot)).astype(LOW)
            ds[block, :] = d
            s[block, :] = nn(d, keys)
        dq = jnp.where(lane < HEAD, s[:rows, :], s[rows:, :]) * 0.125
        dk, dv = tn(ds[...], q), tn(p[...], dm)
        out = jnp.concatenate([dq, dk, dv], axis=1).astype(LOW)
        dproj[:, here] = out
        sums[:, here] = jnp.sum(out.astype(WIDE), axis=0, keepdims=True)
        return 0

    lax.fori_loop(0, part // PAIR, one_pair, 0)


def half_rows_of(ref, which, padded):
    return ref[pl.ds(pl.multiple_of(which * padded, 16), padded), :]


def projection_gradient_kernel(
    small_rows, lines, at, layer_in, d_projected, proj_sums, sums_one, two0, two1, up_sums, wqkv, d_attn,
    *refs,
):
    grads, (turn, rows) = refs[:-2], refs[-2:]
    cols = d_projected.shape[1]
    part = cols // 3
    first = at[T] == 0
    turn[...] = jnp.zeros_like(turn)
    (m0, m1), (v0, _), (g0, _) = small_rows
    count = m1 - m0
    memory = nt(d_projected[:32, :], wqkv[:, :cols])[:count]
    memory = memory + jnp.where(first, d_attn[:count, :], 0.0)
    turn[m0:m1, :] = jnp.where(at[FRESH] == 1, memory, 0.0)
    sums = [
        jnp.concatenate(
            [proj_sums[:, (3 * p + k) * PAIR : (3 * p + k + 1) * PAIR] for p in range(part // PAIR)],
            axis=1,
        )
        for k in (0, 2)
    ]
    for low, value in enumerate(sums, v0):
        turn[low : low + 1, :part] = jnp.where(first, value, 0.0)
        turn[low : low + 1, part:] = jnp.where(first, 0.0, value)
    sums_two = two0[...] + two1[...]
    turn[v0 + 2 : v0 + 4, :] = sums_one[0:2, :]
    turn[v0 + 4 : v0 + 6, :] = sums_two[0:2, :]
    turn[g0 : g0 + 1, :] = sums_one[2:3, :]
    turn[g0 + 1 : g0 + 2, :] = sums_two[2:3, :]
    rows[...] = turn[...].T
    half = rows.shape[0] // 2
    each = up_sums.shape[1] * lines // half
    for n in range(half // lines):
        value = up_sums[:, n * each : (n + 1) * each]
        for side, low in ((0, n * lines), (1, half + n * lines)):
            rows[low : low + 1, UP_AT : UP_AT + each] = jnp.where(at[T] == side, value, 0.0)
    small = rows[...]
    put_gradient(layer_in, d_projected, grads, at[CORE])
    if len(grads) == 1:
        grads[0][:, cols:] = small.astype(LOW)
    else:
        put_blocks(small, grads[0], grads[-1], at[CORE], cols)


def projection_back_kernel(at, d_projected, wqkv, d_attn, d_own, d_sent):
    padded, cols = d_own.shape[0], d_projected.shape[1]
    t = at[T]
    d_own[...] = d_attn[...] + nt(half_rows_of(d_projected, t, padded), wqkv[:, :cols])
    d_sent[...] = nt(half_rows_of(d_projected, 1 - t, padded), wqkv[:, :cols]).astype(LOW)


def finish_kernel(
    part, small_rows, count, at, *refs
):
    parts, (qkv, out, memory, vectors, gains, up, turn) = refs[:count], refs[count:]
    total = parts[0][...]
    for value in parts[1:]:
        total = total + value[...].astype(WIDE)
    lines = total.shape[0]
    cols, width = 3 * part, 2 * part
    mine, got = total[:, : cols + PAIR], total[:, cols + PAIR + width :]
    first = at[T] == 0
    for pair in range(part // PAIR):
        for kind in range(3):
            here = (3 * pair + kind) * PAIR
            a, b = mine[:, here : here + PAIR], got[:, here : here + PAIR]
            low = kind * width + pair * PAIR
            qkv[:, low : low + PAIR] = jnp.where(first, a, b)
            qkv[:, low + part : low + part + PAIR] = jnp.where(first, b, a)
    out[...] = total[:, cols + PAIR : cols + PAIR + width]
    turn[...] = jnp.zeros_like(turn)
    turn[:lines, :] = mine[:, cols:] + got[:, cols:]
    up[...] = turn[0:1, UP_AT : UP_AT + up.shape[1]]
    small = turn[...].T
    for target, (low, high) in zip((memory, vectors, gains), small_rows):
        target[...] = small[low:high, :lines]


def spread_of(v):
    return jnp.mean(v, axis=-1, keepdims=True)


def first_norm_kernel(bias, gain, at, own, got, wout, layer_in, small, mixed, unit, scale, normed, s):
    padded, part = own.shape
    first = at[T] == 0
    mixed[:, :part] = jnp.where(first, own[...], got[...])
    mixed[:, part:] = jnp.where(first, got[...], own[...])
    s[...] = nn(mixed[...], wout[...])
    for low in range(0, padded, ROWS):
        here = slice(low, low + ROWS)
        rows = layer_in[pl.ds(pl.multiple_of(at[T] * padded + low, ROWS), ROWS), :]
        total = rows.astype(WIDE) + (s[here, :] + small[bias + 2 : bias + 3, :])
        centered = total - spread_of(total)
        factor = lax.rsqrt(spread_of(centered * centered) + NORM_EPSILON)
        value = centered * factor
        unit[here, :] = value
        scale[here, :] = jnp.broadcast_to(factor, (ROWS, PAIR))
        value = value * small[gain : gain + 1, :] + small[bias + 3 : bias + 4, :]
        normed[here, :] = value.astype(LOW)


def add_sums(sums, values):
    sums[...] = jnp.zeros_like(sums)
    for n, value in enumerate(values):
        sums[n : n + 1, :] = jnp.sum(value, axis=0, keepdims=True)


def second_norm_kernel(
    bias, gain, start, at, unit, small, own, got, d_out, _, layer_out, d_second, d_ffn, sums
):
    width = unit.shape[1]
    real = d_out.shape[0] - start
    totals = [jnp.zeros((ROWS, width), WIDE)] * 3
    for low in range(0, got.shape[0], ROWS):
        here, there = slice(low, low + ROWS), slice(start + low, start + low + ROWS)
        count = min(ROWS, real - low)
        first = unit[there, :] * small[gain : gain + 1, :] + small[bias + 3 : bias + 4, :]
        ffn = own[there, :] + got[here, :].astype(WIDE) + small[bias + 4 : bias + 5, :]
        total = first + ffn
        centered = total - spread_of(total)
        factor = lax.rsqrt(spread_of(centered * centered) + NORM_EPSILON)
        value = centered * factor
        out = value * small[gain + 1 : gain + 2, :] + small[bias + 5 : bias + 6, :]
        layer_out[low : low + count, :] = out[:count].astype(LOW)
        cotangent = d_out[start + low : start + low + count, :].astype(WIDE)
        if count < ROWS:
            cotangent = jnp.concatenate(
                [cotangent, jnp.zeros((ROWS - count, width), WIDE)], axis=0
            )
        d_unit = cotangent * small[gain + 1 : gain + 2, :]
        back = factor * (d_unit - spread_of(d_unit) - value * spread_of(d_unit * value))
        d_second[here, :] = back
        rounded = back.astype(LOW)
        d_ffn[here, :] = rounded
        terms = (rounded.astype(WIDE), cotangent, cotangent * value)
        totals = [a + b for a, b in zip(totals, terms)]
    add_sums(sums, totals)


def first_back_kernel(
    gain, at, second0, second1, own, got, unit, scale, small, wout, d_attn_in, d_attn, mix_own, mix_sent, sums
):
    padded, width = unit.shape
    part = mix_own.shape[1]
    totals = [jnp.zeros((ROWS, width), WIDE)] * 3
    for low in range(0, padded, ROWS):
        here = slice(low, low + ROWS)
        cut = second0.shape[0]
        second = second0[here, :] if low < cut else second1[low - cut : low - cut + ROWS, :]
        cotangent = second + own[here, :] + got[here, :].astype(WIDE)
        value = unit[here, :]
        d_unit = cotangent * small[gain : gain + 1, :]
        back = d_unit - spread_of(d_unit) - value * spread_of(d_unit * value)
        back = scale[here, :1] * back
        d_attn_in[here, :] = back
        rounded = back.astype(LOW)
        d_attn[here, :] = rounded
        terms = (rounded.astype(WIDE), cotangent, cotangent * value)
        totals = [a + b for a, b in zip(totals, terms)]
    add_sums(sums, totals)
    mixed = nt(d_attn[...], wout[...]).astype(LOW)
    first = at[T] == 0
    mix_own[...] = jnp.where(first, mixed[:, :part], mixed[:, part:])
    mix_sent[...] = jnp.where(first, mixed[:, part:], mixed[:, :part])


def rows_kernel(mem_count, at, own, got, out):
    real = out.shape[0]
    row = lax.broadcasted_iota(jnp.int32, (32, 1), 0)
    fresh = (row < mem_count) & (at[FRESH] == 1) & (at[T] == 0)
    out[:32, 0, :] = jnp.where(fresh, 0.0, own[:32, :] + got[:32, :].astype(WIDE))
    out[32:, 0, :] = own[32:real, :] + got[32:real, :].astype(WIDE)


def gelu_parts(pre):
    cdf = 0.5 * (1.0 + lax.erf(pre * 0.7071067811865476))
    density = jnp.exp(-0.5 * pre * pre) * 0.3989422804014327
    return pre * cdf, cdf + pre * density


def shards(
    rows_in,
    d_out,
    starts,
    lengths,
    resets,
    qkv_weight,
    out_weight,
    bias_vec,
    gains,
    mem_init,
    ffn_up,
    up_bias,
    ffn_down,
):
    half_rows, seg_count, width = rows_in.shape
    assert seg_count == 1
    dp_count, t_count = lax.axis_size("dp"), lax.axis_size("tensor")
    assert t_count == 2
    digits = digits_of(dp_count)
    x_digit, core_digit = digits[-2:]
    padded = ceil_to(half_rows, 16)
    rows = 2 * padded
    mem_count = mem_init.shape[0]
    part = HEADS // t_count * HEAD
    cols = 3 * part
    hidden_mine = ffn_up.shape[1]
    feat = bias_vec.shape[1]
    lines = qkv_weight.shape[0]
    doc_count = starts.shape[1]
    counts = (mem_count, bias_vec.shape[0], gains.shape[0])
    edges = [sum(counts[:n]) for n in range(len(counts) + 1)]
    small_rows = tuple(zip(edges[:-1], edges[1:]))
    bias, gain = edges[1], edges[2]
    integers = [
        lax.axis_index("tensor"),
        digit_at(x_digit),
        digit_at(core_digit),
        digit_at(digits[-3]),
        lax.axis_index("dp"),
        resets[0],
        lengths[0],
    ]
    at = jnp.concatenate([jnp.stack(integers).astype(jnp.int32), starts[0]])

    side = lax.axis_index("tensor").astype(jnp.int32).reshape(1)
    (packed,) = call(
        functools.partial(columns_kernel, small_rows),
        [low_of(lines, 3 * width + PAIR + width)],
        side, qkv_weight, bias_vec, gains, mem_init, up_bias.reshape(1, -1), out_weight,
        scratch=[pltpu.VMEM((PAIR, PAIR), WIDE)],
        room=57 << 20,
    )
    rows_low = jnp.pad(tie(rows_in, packed)[:, 0, :], ((0, padded - half_rows), (0, 0)))
    rows_other = swap_tensor(rows_low)
    up_pair = spread_near(tie(ffn_up, packed), digits)
    first_z = spread_outer(packed, digits)
    first_z, rows_other, up_pair = join(first_z, rows_other, up_pair)
    slots = first_z.shape[0]
    mine, other = call(
        functools.partial(halves_of_heads_kernel, part),
        [low_of(slots, lines, cols + PAIR + width), low_of(slots, lines, cols + PAIR)],
        at, first_z,
    )
    first_parts = [mine, swap_tensor(other), rotate(mine, x_digit, 1), swap_both(other, x_digit)]
    up_z = spread_far(up_pair, digits)
    down_pair = spread_near(tie(ffn_down.T, mine), digits)
    up_z, down_in = join(up_z, down_pair)
    *first_parts, up_z = join(*first_parts, up_z)
    first_parts = [jnp.concatenate(first_parts[n : n + 2], axis=2) for n in (0, 2)]
    core_parts = [rotate(value, core_digit, 1) for value in first_parts]
    sizes = tuple(size for _, size in digits)
    (wqkv,) = call(
        functools.partial(assemble_first_kernel, sizes),
        [low_of(dp_count, 2 * lines, cols + PAIR)],
        at, *first_parts, *core_parts,
    )
    wqkv = wqkv.reshape(width, cols + PAIR)
    (out_sent,) = call(
        functools.partial(beside_kernel, cols + PAIR),
        [low_of(dp_count // 2, lines, width)], at, *first_parts,
    )
    out_got = swap_tensor(out_sent)
    up_x = rotate(up_z, x_digit, 1)
    down_pieces = spread_far_pieces(down_in, digits)
    down_x = [rotate(down_pieces[0], x_digit, 1)]

    projected, mix_own, mix_sent, log_total, layer_in, small = call(
        functools.partial(forward_kernel, half_rows, mem_count, doc_count, bias),
        [
            low_of(rows, cols),
            low_of(padded, part),
            low_of(padded, part),
            wide_of(rows, PAIR),
            low_of(rows, width),
            wide_of(ceil_to(edges[-1], 32), width),
        ],
        at, rows_low, rows_other, wqkv,
        scratch=[
            pltpu.VMEM((rows, rows), WIDE),
            pltpu.VMEM((rows, PAIR), WIDE),
            pltpu.VMEM((rows, PAIR), LOW),
        ],
    )
    mix_got = swap_tensor(mix_sent)
    out_got = tie(out_got, mix_sent)
    (wout,) = call(
        functools.partial(assemble_out_kernel, sizes, cols + PAIR),
        [low_of(dp_count, 2 * lines, width)],
        at, *first_parts, *core_parts, out_got, rotate(out_got, core_digit, 1),
    )
    wout = wout.reshape(width, width)
    mix_got, *down_pieces = join(mix_got, *down_pieces)
    mixed, unit, scale, normed_own = call(
        functools.partial(first_norm_kernel, bias, gain),
        [low_of(padded, width), wide_of(padded, width), wide_of(padded, PAIR), low_of(padded, width)],
        at, mix_own, mix_got, wout, layer_in, small,
        scratch=[pltpu.VMEM((padded, width), WIDE)],
    )

    normed_got = swap_tensor(normed_own)
    up_x, up_z = tie(up_x, mix_sent), tie(up_z, mix_sent)
    down_pieces = [tie(piece, mix_sent) for piece in down_pieces]
    down_x = [tie(down_x[0], mix_sent)]
    up = assemble(at, swap_blocks(up_z, up_x, digits), digits, hidden_mine, paired=True)
    (up_b,) = call(
        functools.partial(up_row_kernel, lines), [wide_of(ROWS, hidden_mine)], at, wqkv,
        scratch=[pltpu.VMEM((1, hidden_mine), WIDE)],
    )
    down_pieces[1], down_x[0] = join(down_pieces[1], down_x[0])
    down_x.append(rotate(down_pieces[1], x_digit, 1))
    normed_got, up_b, up = join(normed_got, up_b, up)
    down_t = assemble(at, swap_pieces(down_pieces, down_x, digits), digits, hidden_mine, paired=True)

    def feed_forward(rows):
        pre_act = nn(rows, up).reshape(-1, *up_b.shape) + up_b
        hidden, slope = (part.reshape(rows.shape[0], -1) for part in gelu_parts(pre_act))
        hidden = hidden.astype(LOW)
        return hidden, slope, nt(hidden, down_t)

    cut = ceil_to(padded // 2, ROWS)
    pieces = ((0, cut), (cut, padded))
    hidden_got, slope_got, ffn_sent = feed_forward(normed_got)
    ffn_sent = ffn_sent.astype(LOW)
    (_, first_cut), (_, end) = pieces
    ffn_got = [swap_tensor(ffn_sent[:first_cut])]
    hidden_own, slope_own, ffn_own = call(
        own_forward_kernel,
        [low_of(padded, hidden_mine), wide_of(padded, hidden_mine), wide_of(padded, width)],
        at, normed_own, up, up_b, down_t, rotate(ffn_sent[:ROWS, :PAIR], core_digit, 1),
    )
    ffn_got.append(swap_tensor(tie(ffn_sent, ffn_own)[first_cut:end]))
    d_out_rows = d_out.reshape(half_rows, width)
    second, ahead = [], small
    for (low, high), got in zip(pieces, ffn_got):
        if second:
            ahead = rotate(second[-1][2][:ROWS, :PAIR], core_digit, 1)
        outs = [
            low_of(min(high, half_rows) - low, width),
            wide_of(high - low, width),
            low_of(high - low, width),
            wide_of(8, width),
        ]
        kernel = functools.partial(second_norm_kernel, bias, gain, low)
        second.append(call(kernel, outs, at, unit, small, ffn_own, got, d_out_rows, ahead))
    layer_out, d_second, d_ffn_sent, sums_two = zip(*second)

    d_ffn_got = jnp.concatenate([swap_tensor(piece) for piece in d_ffn_sent], axis=0)
    d_ffn_own = jnp.concatenate(d_ffn_sent, axis=0)

    def feed_back(rows, slope):
        d_pre = (slope * nn(rows, down_t)).astype(LOW)
        return d_pre, nt(d_pre, up)

    d_pre_own, d_first_own = feed_back(d_ffn_own, slope_own)
    down_own, up_own, sums_own = call(
        own_kernel,
        [wide_of(width, hidden_mine), wide_of(width, hidden_mine), wide_of(1, hidden_mine)],
        at, d_ffn_own, hidden_own, normed_own, d_pre_own,
    )
    d_ffn_got, d_first_own, down_own, up_own = join(d_ffn_got, d_first_own, down_own, up_own)
    d_pre_got, d_first_sent = feed_back(d_ffn_got, slope_got)
    d_first_sent = d_first_sent.astype(LOW)
    d_first_got = swap_tensor(d_first_sent)

    outs = gradient_outs(width, hidden_mine, dp_count)
    down_grads = call(
        rest_kernel, outs, at, down_own, tie(d_ffn_got, d_first_sent), hidden_got
    )
    down_kept, down_sent = halve(at, *swap_cores(down_grads, dp_count, core_digit))
    down_got = rotate(down_sent, x_digit, 1)
    up_sums, *up_grads = call(
        rest_sums_kernel, [wide_of(1, hidden_mine)] + outs,
        at, up_own, sums_own, normed_got, tie(d_pre_got, down_sent),
    )
    up_kept, up_sent = halve(at, *swap_cores(up_grads, dp_count, core_digit))

    d_attn_in, d_attn, d_mix_own, d_mix_sent, sums_one = call(
        functools.partial(first_back_kernel, gain),
        [
            wide_of(padded, width),
            low_of(padded, width),
            low_of(padded, part),
            low_of(padded, part),
            wide_of(8, width),
        ],
        at, *d_second, d_first_own, d_first_got, unit, scale, small, wout,
    )
    d_mix_got = swap_tensor(d_mix_sent)
    out_grads = call(
        out_gradient_kernel, gradient_outs(width, width, dp_count, OUT_TILE),
        at, mixed, tie(d_attn, d_mix_sent),
    )
    out_kept, out_parts = swap_cores(out_grads, dp_count, core_digit)
    out_kept, out_sent = call(
        rows_halves_kernel, [low_of(dp_count // 2, lines, width)] * 2, at, out_kept, *out_parts
    )
    down_kept, down_sent = far_parts(at, down_kept, down_got, digits)
    d_mix_got, out_sent, up_sent, down_sent = join(d_mix_got, out_sent, up_sent, down_sent)
    down_got = rotate(down_sent, digits[-3], 2)
    out_got = swap_tensor(out_sent)
    up_got = rotate(up_sent, x_digit, 1)

    d_projected, proj_sums = call(
        functools.partial(backward_kernel, half_rows, mem_count, doc_count),
        [low_of(rows, cols), wide_of(1, cols)],
        at, projected, d_mix_own, d_mix_got, log_total,
        scratch=[
            pltpu.VMEM((rows, rows), WIDE),
            pltpu.VMEM((2 * rows, PAIR), WIDE),
            pltpu.VMEM((2 * rows, rows), LOW),
            pltpu.VMEM((2 * rows, rows), LOW),
            pltpu.VMEM((rows, part), LOW),
        ],
    )
    up_kept, up_sent = far_parts(at, up_kept, up_got, digits)
    qkv_grads = call(
        functools.partial(projection_gradient_kernel, small_rows, lines),
        gradient_outs(width, cols + PAIR, dp_count),
        at, layer_in, d_projected, proj_sums, sums_one, *sums_two, up_sums, wqkv, d_attn_in,
        scratch=[pltpu.VMEM((PAIR, width), WIDE), pltpu.VMEM((width, PAIR), WIDE)],
    )
    out_got, down_got, *qkv_grads = join(out_got, down_got, *qkv_grads)
    down_kept, down_sent = near_parts(at, down_kept, down_got)
    qkv_kept, qkv_parts = swap_cores(qkv_grads, dp_count, core_digit)
    up_sent, *qkv_parts = join(up_sent, *qkv_parts)
    slots = dp_count // 4
    mine, to_x, to_y, to_both = call(
        quarter_kernel,
        [low_of(slots, lines, cols + PAIR + width)] * 2 + [low_of(slots, lines, cols + PAIR)] * 2,
        at, qkv_kept, *qkv_parts, out_kept, out_got,
    )

    both_got = [rotate(to_x, x_digit, 1), swap_tensor(to_y), swap_both(to_both, x_digit)]
    up_got = rotate(up_sent, digits[-3], 2)
    down_got = swap_near(down_sent, digits[-3])
    d_in_own, d_in_sent = call(
        projection_back_kernel, [wide_of(padded, width), low_of(padded, width)],
        at, tie(d_projected, to_x), wqkv, d_attn_in,
    )
    d_in_got = swap_tensor(d_in_sent)
    ahead = rotate(tie(d_in_sent, up_got)[:ROWS, :PAIR], core_digit, 1)
    up_kept, up_sent = near_parts(at, up_kept, up_got, ahead)
    *both_got, up_sent, down_got = join(*both_got, up_sent, down_got)
    up_got = swap_near(up_sent, digits[-3])
    both_kept, both_sent = outer_parts(at, digits, mine, *both_got)
    both_got = outer_send(both_sent, digits)
    grad_ffn_down = outer_sum(down_kept, [down_got], digits)
    grad_ffn_up = outer_sum(up_kept, [up_got], digits)
    (grad_rows,) = call(
        functools.partial(rows_kernel, mem_count), [wide_of(half_rows, 1, width)], at, d_in_own, d_in_got
    )
    grad_rows, *both_got = join(grad_rows, *both_got)

    if len(digits) == 3:
        parts = [both_kept[0], *[part[0] for part in both_got]]
    else:
        parts = [outer_sum(both_kept, both_got, digits)]
    grad_qkv, grad_out_weight, grad_mem, grad_vec, grad_gains, grad_up_bias = call(
        functools.partial(finish_kernel, part, small_rows, len(parts)),
        [wide_of(lines, 3 * width), wide_of(lines, width)]
        + [wide_of(n, feat) for n in counts]
        + [wide_of(1, up_bias.shape[0])],
        at, *parts,
        scratch=[pltpu.VMEM((PAIR, PAIR), WIDE)],
    )
    return (
        jnp.concatenate(layer_out, axis=0).reshape(half_rows, 1, width),
        grad_rows,
        grad_qkv,
        grad_out_weight,
        grad_vec,
        grad_gains,
        grad_mem,
        grad_ffn_up,
        grad_up_bias.reshape(up_bias.shape),
        grad_ffn_down.T,
    )


def solution(mesh):
    both = ("dp", "tensor")
    in_specs = (
        P("tensor", "dp", None),
        P("tensor", "dp", None),
        P("dp", None),
        P("dp"),
        P("dp"),
        P(both, None),
        P(both, None),
        P(None, both),
        P(None, both),
        P(None, both),
        P("dp", "tensor"),
        P(both),
        P("tensor", "dp"),
    )
    out_specs = (
        P("tensor", "dp", None),
        P("tensor", "dp", None),
        P(both, None),
        P(both, None),
        P(None, both),
        P(None, both),
        P(None, both),
        P("dp", "tensor"),
        P(both),
        P("tensor", "dp"),
    )
    return jax.shard_map(shards, mesh=mesh, in_specs=in_specs, out_specs=out_specs, check_vma=False)
```

```python
import functools

import jax
import jax.numpy as jnp
import numpy as np
from jax import lax
from jax.experimental import pallas as pl
from jax.experimental.pallas import tpu as pltpu
from jax.sharding import PartitionSpec as P

HEADS = 12
HEAD = 64
NORM_EPSILON = 1e-06
LOW = jnp.bfloat16
WIDE = jnp.float32
CHUNK = 32
FORWARD_BLOCK = 272
BACKWARD_BLOCK = 544
TILE = 384
OUT_TILE = 256
ROWS = 16
PAIR = 2 * HEAD
UP_AT = 32
QUICK = pl.CostEstimate(flops=1, bytes_accessed=1, transcendentals=0)
T, X, CORE, OUTER, DP, FRESH, LENGTH, STARTS = range(8)


def ceil_to(count, unit):
    return -(-count // unit) * unit


def nn(a, b):
    return lax.dot_general(a, b, (((1,), (0,)), ((), ())), preferred_element_type=WIDE)


def nt(a, b):
    return lax.dot_general(a, b, (((1,), (1,)), ((), ())), preferred_element_type=WIDE)


def tn(a, b):
    return lax.dot_general(a, b, (((0,), (0,)), ((), ())), preferred_element_type=WIDE)


def low_of(*shape):
    return jax.ShapeDtypeStruct(shape, LOW)


def wide_of(*shape):
    return jax.ShapeDtypeStruct(shape, WIDE)


def held_bytes(array):
    rows, cols = ((1,) + tuple(array.shape))[-2:]
    lead = int(np.prod(array.shape[:-2])) if len(array.shape) > 2 else 1
    return lead * ceil_to(rows, 16) * ceil_to(cols, 128) * jnp.dtype(array.dtype).itemsize


def call(kernel, outs, at, *arrays, scratch=(), room=0):
    room += sum(held_bytes(array) for array in (*arrays, *outs))
    room += sum(held_bytes(ref) for ref in scratch)
    return pl.pallas_call(
        kernel,
        in_specs=[pl.BlockSpec(memory_space=pltpu.SMEM)]
        + [pl.BlockSpec(memory_space=pltpu.VMEM)] * len(arrays),
        out_specs=[pl.BlockSpec(memory_space=pltpu.VMEM)] * len(outs),
        out_shape=list(outs),
        scratch_shapes=list(scratch),
        compiler_params=pltpu.CompilerParams(vmem_limit_bytes=room + (9 << 20)),
        cost_estimate=QUICK,
    )(at, *arrays)


def digits_of(dp_count):
    assert dp_count % 4 == 0
    sizes = [2, 2]
    left = dp_count // 4
    while left > 1:
        size = next((s for s in (4, 2, 3) if left % s == 0), left)
        sizes.append(size)
        left //= size
    if len(sizes) == 2:
        sizes.append(1)
    digits, stride = [], 1
    for size in sizes:
        digits.append((stride, size))
        stride *= size
    return digits[::-1]


def digit_at(digit):
    stride, size = digit
    return (lax.axis_index("dp") // stride) % size


def rotate(value, digit, step):
    stride, size = digit
    pairs = []
    for at in range(lax.axis_size("dp")):
        mine = (at // stride) % size
        pairs.append((at, at + ((mine + step) % size - mine) * stride))
    return lax.ppermute(value, "dp", pairs)


def swap_tensor(value):
    return lax.ppermute(value, "tensor", [(0, 1), (1, 0)])


def swap_both(value, digit):
    stride, _ = digit
    pairs = []
    for at in range(lax.axis_size("dp")):
        other = at + stride if (at // stride) % 2 == 0 else at - stride
        pairs += [(2 * at + side, 2 * other + 1 - side) for side in range(2)]
    return lax.ppermute(value, ("dp", "tensor"), pairs)


def tie(value, *others):
    return lax.optimization_barrier((value,) + others)[0]


join = lambda *values: lax.optimization_barrier(values)


def spread_outer(value, digits):
    for digit in reversed(digits[:-2]):
        got = [value] + [rotate(value, digit, step) for step in range(1, digit[1])]
        value = jnp.stack(got)
    return value.reshape((-1,) + value.shape[-2:])


def swap_near(value, digit):
    stride, _ = digit
    pairs = []
    for at in range(lax.axis_size("dp")):
        pairs.append((at, at + stride if (at // stride) % 2 == 0 else at - stride))
    return lax.ppermute(value, "dp", pairs)


def spread_near(value, digits):
    assert digits[-3][1] == 4
    return jnp.stack([value, swap_near(value, digits[-3])])


def spread_far(pair, digits):
    value = jnp.concatenate([pair, rotate(pair, digits[-3], 2)], axis=0)
    for digit in reversed(digits[:-3]):
        value = jnp.stack([value] + [rotate(value, digit, step) for step in range(1, digit[1])])
    return value.reshape((-1,) + value.shape[-2:])


def spread_far_pieces(pair, digits):
    pieces = [pair, rotate(pair, digits[-3], 2)]
    for digit in reversed(digits[:-3]):
        for n, value in enumerate(pieces):
            value = jnp.stack([value] + [rotate(value, digit, step) for step in range(1, digit[1])])
            pieces[n] = value.reshape((-1,) + value.shape[-2:])
    return pieces


def placer(sizes, me, paired):
    outer, digits = sizes[:-2], []
    for size in reversed(sizes):
        digits.append(lax.rem(me, size))
        me = lax.div(me, size)
    digits = digits[::-1]

    def place_of(swap_core, swap_x, slot):
        steps = []
        for size in reversed(outer):
            steps.append(slot % size)
            slot //= size
        place = 0
        for n, (size, digit, step) in enumerate(zip(outer, digits, steps[::-1])):
            if paired and n == len(outer) - 1:
                at = lax.bitwise_xor(digit, step)
            else:
                at = lax.rem(digit + (size - step), size)
            place = place * size + at
        x, core = digits[-2], digits[-1]
        place = place * 2 + (1 - x if swap_x else x)
        return place * 2 + (1 - core if swap_core else core)

    return place_of


def assemble_kernel(sizes, paired, at, *refs):
    *parts, whole = refs
    cols = whole.shape[2]
    pieces = len(parts) // 4
    place_of = placer(sizes, at[DP], paired)
    for swap_core in range(2):
        for swap_x in range(2):
            for piece in range(pieces):
                source = parts[pieces * (2 * swap_core + swap_x) + piece]
                for block in range(source.shape[0]):
                    slot = 2 * (pieces * (block // 2) + piece) + block % 2
                    whole[place_of(swap_core, swap_x, slot)] = source[block, :, :cols]


def swap_blocks(mine, x_got, digits):
    core = digits[-1]
    return [mine, x_got, rotate(mine, core, 1), rotate(x_got, core, 1)]


def swap_pieces(mine, x_got, digits):
    core = digits[-1]
    return [*mine, *x_got] + [rotate(piece, core, 1) for piece in (*mine, *x_got)]


def assemble(at, parts, digits, cols, paired=False):
    rows = parts[0].shape[1]
    blocks = sum(part.shape[0] for part in parts)
    sizes = tuple(size for _, size in digits)
    (whole,) = call(
        functools.partial(assemble_kernel, sizes, paired),
        [low_of(blocks, rows, cols)],
        at,
        *parts,
    )
    return whole.reshape(blocks * rows, cols)


def assemble_first_kernel(sizes, at, *refs):
    parts, whole = refs[:4], refs[4]
    lines, cols = whole.shape[1] // 2, whole.shape[2]
    place_of = placer(sizes, at[DP], False)
    first = at[T] == 0
    for swap_core in range(2):
        for swap_x in range(2):
            source = parts[2 * swap_core + swap_x]
            far = source.shape[2] - cols
            for slot in range(source.shape[0]):
                place = place_of(swap_core, swap_x, slot)
                a, b = source[slot, :, :cols], source[slot, :, far:]
                whole[place, :lines] = jnp.where(first, a, b)
                whole[place, lines:] = jnp.where(first, b, a)


def assemble_out_kernel(sizes, cols, at, *refs):
    parts, gots, whole = refs[:4], refs[4:6], refs[6]
    place_of = placer(sizes, at[DP], False)
    first = at[T] == 0
    lines, width = whole.shape[1] // 2, whole.shape[2]
    for swap_core in range(2):
        for swap_x in range(2):
            source, got = parts[2 * swap_core + swap_x], gots[swap_core]
            slots = source.shape[0]
            for slot in range(slots):
                mine, other = source[slot, :, cols : cols + width], got[swap_x * slots + slot]
                place = place_of(swap_core, swap_x, slot)
                whole[place, :lines] = jnp.where(first, mine, other)
                whole[place, lines:] = jnp.where(first, other, mine)


def columns_kernel(small_rows, at, weight, vectors, gains, memory, up, out, packed, turn):
    lines, width = weight.shape
    packed[:, :width] = weight[...]
    turn[...] = jnp.zeros_like(turn)
    for source, (low, high) in zip((memory, vectors, gains), small_rows):
        turn[low:high, :lines] = source[...].astype(WIDE)
    columns = turn[...].T[:lines]
    turn[:lines, :] = columns
    turn[0:1, UP_AT : UP_AT + up.shape[1]] = up[...].astype(WIDE)
    packed[:, width : width + PAIR] = turn[:lines, :].astype(LOW)
    packed[:, width + PAIR :] = out[...]


def halves_of_heads_kernel(part, at, packed, mine, other):
    width = 6 * part
    first = at[T] == 0
    for slot in range(packed.shape[0]):
        for pair in range(part // PAIR):
            for kind in range(3):
                low = 2 * kind * part + pair * PAIR
                a = packed[slot, :, low : low + PAIR]
                b = packed[slot, :, low + part : low + part + PAIR]
                here = (3 * pair + kind) * PAIR
                mine[slot, :, here : here + PAIR] = jnp.where(first, a, b)
                other[slot, :, here : here + PAIR] = jnp.where(first, b, a)
        mine[slot, :, 3 * part :] = packed[slot, :, width:]
        other[slot, :, 3 * part :] = packed[slot, :, width : width + PAIR]


def beside_kernel(cols, at, mine, x_got, out):
    slots = mine.shape[0]
    for n, source in enumerate((mine, x_got)):
        for slot in range(slots):
            out[n * slots + slot] = source[slot, :, cols : cols + out.shape[2]]


def put_blocks(total, kept, sent, core, at):
    groups, rows, _ = kept.shape
    cols = total.shape[1]
    total = total.astype(LOW).reshape(2 * groups, rows, cols)
    second = core == 1
    for group in range(groups):
        even, odd = total[2 * group], total[2 * group + 1]
        kept[group, :, at : at + cols] = jnp.where(second, odd, even)
        sent[group] = jnp.where(second, even, odd)


def put_gradient(a, b, outs, core, own=None, tile=TILE):
    whole = tn(a[...], b[...])
    for n, low in enumerate(range(0, b.shape[1], tile)):
        total = whole[:, low : low + tile]
        if own is not None:
            total = total + own[:, low : low + tile]
        if len(outs) == 1:
            outs[0][:, low : low + tile] = total.astype(LOW)
        else:
            put_blocks(total, outs[0], outs[1 + n], core, low)


def gradient_outs(width, cols, dp_count, tile=TILE):
    rows = width // dp_count
    if rows % 16:
        return [low_of(width, cols)]
    tiles = [min(tile, cols - low) for low in range(0, cols, tile)]
    return [low_of(dp_count // 2, rows, n) for n in [cols] + tiles]


def swap_cores(outs, dp_count, digit):
    if len(outs) == 1:
        whole = outs[0].reshape(dp_count // 2, 2, -1, outs[0].shape[1])
        core = digit_at(digit)
        take = lambda which: lax.dynamic_index_in_dim(whole, which, 1, keepdims=False)
        outs = [take(core), take(1 - core)]
    return outs[0], [rotate(part, digit, 1) for part in outs[1:]]


def out_gradient_kernel(at, a, b, *outs):
    put_gradient(a, b, outs, at[CORE], tile=OUT_TILE)


def rows_halves_kernel(at, mine, *refs):
    got, (kept, sent) = refs[:-2], refs[-2:]
    lines = kept.shape[1]
    first = at[T] == 0
    for group in range(mine.shape[0]):
        low = 0
        for part in got:
            high = low + part.shape[2]
            total = mine[group, :, low:high].astype(WIDE) + part[group].astype(WIDE)
            a, b = total[:lines], total[lines:]
            kept[group, :, low:high] = jnp.where(first, a, b).astype(LOW)
            sent[group, :, low:high] = jnp.where(first, b, a).astype(LOW)
            low = high


def own_forward_kernel(at, normed, up, up_b, down_t, _, hidden, slope, out):
    pre_act = nn(normed[...], up[...]).reshape(-1, *up_b.shape) + up_b[...]
    active, slopes = (value.reshape(hidden.shape) for value in gelu_parts(pre_act))
    hidden[...] = active.astype(LOW)
    slope[...] = slopes
    out[...] = nt(hidden[...], down_t[...])


def own_kernel(at, a_down, b_down, a_up, b_up, down, up, sums):
    tile = 384
    for low in range(0, b_down.shape[1], tile):
        here = slice(low, low + tile)
        down[:, here] = tn(a_down[...], b_down[:, here])
        up[:, here] = tn(a_up[...], b_up[:, here])
    sums[...] = jnp.sum(b_up[...].astype(WIDE), axis=0, keepdims=True)


def rest_kernel(at, own, a, b, *outs):
    put_gradient(a, b, outs, at[CORE], own=own)


def rest_sums_kernel(at, own, own_sums, a, b, sums, *outs):
    put_gradient(a, b, outs, at[CORE], own=own)
    sums[...] = own_sums[...] + jnp.sum(b[...].astype(WIDE), axis=0, keepdims=True)


def up_row_kernel(lines, at, w, row, line):
    half, each = w.shape[0] // 2, row.shape[1] * lines * 2 // w.shape[0]
    low = w.shape[1] - PAIR
    for n in range(half // lines):
        a = w[n * lines : n * lines + 1, low:].astype(WIDE)
        b = w[half + n * lines : half + n * lines + 1, low:].astype(WIDE)
        value = jnp.where(at[T] == 0, a, b)[:, UP_AT : UP_AT + each]
        line[:, n * each : (n + 1) * each] = value
    row[...] = jnp.broadcast_to(line[...], row.shape)


def halve_kernel(at, mine, *refs):
    got, (kept, sent) = refs[:-2], refs[-2:]
    x = at[X]
    for group in range(kept.shape[0]):
        for other, out in ((0, kept), (1, sent)):
            place = 2 * group + (1 - x if other else x)
            low = 0
            for part in got:
                high = low + part.shape[2]
                total = mine[place, :, low:high].astype(WIDE) + part[place].astype(WIDE)
                out[group, :, low:high] = total.astype(LOW)
                low = high


def halve(at, mine, got):
    groups, rows, cols = mine.shape
    return call(halve_kernel, [low_of(groups // 2, rows, cols)] * 2, at, mine, *got)


def quarter_kernel(at, mine, *refs):
    got, (out_mine, out_got, keep, to_x, to_y, to_both) = refs[:-6], refs[-6:]
    lines, cols = to_y.shape[1:]
    first = at[T] == 0
    for group in range(keep.shape[0]):
        own, other = 2 * group + at[X], 2 * group + 1 - at[X]
        for place, same, across in ((own, keep, to_y), (other, to_x, to_both)):
            low = 0
            for part in got:
                high = low + part.shape[2]
                total = mine[place, :, low:high].astype(WIDE) + part[place].astype(WIDE)
                a, b = total[:lines], total[lines:]
                same[group, :, low:high] = jnp.where(first, a, b).astype(LOW)
                across[group, :, low:high] = jnp.where(first, b, a).astype(LOW)
                low = high
            total = out_mine[place].astype(WIDE) + out_got[place].astype(WIDE)
            same[group, :, cols:] = total.astype(LOW)


def parts_kernel(size, at, mine, x_got, y_got, both_got, *outs):
    me = at[OUTER]
    cols = mine.shape[2]
    for group in range(outs[0].shape[0]):
        for step, out in enumerate(outs):
            place = group * size + lax.rem(me + step, size)
            total = mine[place].astype(WIDE) + x_got[place].astype(WIDE)
            out[group, :, :cols] = total.astype(out.dtype)
            total = y_got[place].astype(WIDE) + both_got[place].astype(WIDE)
            out[group, :, cols:] = total.astype(out.dtype)


def outer_parts(at, digits, *parts):
    size = digits[-3][1]
    blocks, rows, cols = parts[0].shape
    shape = (blocks // size, rows, cols + parts[2].shape[2])
    outs = [wide_of(*shape)] + [low_of(*shape)] * (size - 1)
    kept, *sent = call(functools.partial(parts_kernel, size), outs, at, *parts)
    return kept, sent


def far_kernel(at, mine, got, kept, sent):
    me = at[OUTER]
    pair = lax.bitwise_xor(me, 1)
    for group in range(kept.shape[0] // 2):
        for n, block in enumerate((me, pair)):
            for out, place in ((kept, block), (sent, lax.bitwise_xor(block, 2))):
                spot = 4 * group + place
                total = mine[spot].astype(WIDE) + got[spot].astype(WIDE)
                out[2 * group + n] = total.astype(out.dtype)


def near_kernel(at, mine, got, *refs):
    kept, sent = refs[-2:]
    for group in range(kept.shape[0]):
        kept[group] = mine[2 * group] + got[2 * group].astype(WIDE)
        total = mine[2 * group + 1] + got[2 * group + 1].astype(WIDE)
        sent[group] = total.astype(LOW)


def far_parts(at, mine, got, digits):
    assert digits[-3][1] == 4
    blocks, rows, cols = mine.shape
    return call(
        far_kernel, [wide_of(blocks // 2, rows, cols), low_of(blocks // 2, rows, cols)], at, mine, got
    )


def near_parts(at, mine, got, *ahead):
    blocks, rows, cols = mine.shape
    outs = [wide_of(blocks // 2, rows, cols), low_of(blocks // 2, rows, cols)]
    return call(near_kernel, outs, at, mine, got, *ahead)


def outer_send(sent, digits):
    return [rotate(part, digits[-3], step + 1) for step, part in enumerate(sent)]


def outer_sum(kept, got, digits):
    for part in got:
        kept = kept + part.astype(WIDE)
    for digit in reversed(digits[:-3]):
        size = digit[1]
        kept = kept.reshape((-1, size) + kept.shape[1:])
        at = digit_at(digit)
        take = lambda step: lax.dynamic_index_in_dim(kept, (at + step) % size, 1, keepdims=False)
        total = take(0)
        for step in range(1, size):
            total = total + rotate(take(step).astype(LOW), digit, step).astype(WIDE)
        kept = total
    return kept[0]


def fill_mask(mask, at, half_rows, mem_count, starts):
    rows = mask.shape[0]
    padded = rows // 2

    def places(shape, axis):
        spot = lax.broadcasted_iota(jnp.int32, shape, axis)
        second = spot >= padded
        within = jnp.where(second, spot - padded, spot)
        pos = within + jnp.where(second, half_rows, 0) - mem_count
        doc = jnp.zeros(shape, jnp.int32)
        for i in range(starts):
            doc = doc + (at[STARTS + i] <= pos).astype(jnp.int32)
        return within < half_rows, pos, doc

    _, q_pos, q_doc = places((rows, 1), 0)
    real, k_pos, k_doc = places((1, rows), 1)
    key_ok = real & (k_pos < at[LENGTH])
    for low in range(0, rows, CHUNK):
        qp, qd = q_pos[low : low + CHUNK], q_doc[low : low + CHUNK]
        same = (qd == k_doc) | (qp < 0) | (k_pos < 0)
        mask[low : low + CHUNK, :] = jnp.where(same & key_ok, 0.0, -1e9)


def heads_apart(pair):
    lane = lax.broadcasted_iota(jnp.int32, (1, PAIR), 1)
    zero = jnp.zeros((), LOW)
    return jnp.concatenate(
        [jnp.where(lane < HEAD, pair, zero), jnp.where(lane < HEAD, zero, pair)], axis=0
    )


def lanes(pair, count):
    return pl.ds(pl.multiple_of(pair * count, PAIR), count)


def forward_kernel(
    half_rows, mem_count, starts, first_bias,
    at, own, other, w, qkv, mix_own, mix_sent, lse, x, small, mask, s, mixed,
):
    rows, padded = x.shape[0], own.shape[0]
    t = at[T]
    part = mix_own.shape[1]
    fill_mask(mask, at, half_rows, mem_count, starts)
    lse[...] = jnp.zeros_like(lse)
    small[...] = w[:, 3 * part :].astype(WIDE).T[: small.shape[0]]
    x[pl.ds(pl.multiple_of(t * padded, 16), padded), :] = own[...]
    x[pl.ds(pl.multiple_of((1 - t) * padded, 16), padded), :] = other[...]
    row = lax.broadcasted_iota(jnp.int32, (32, 1), 0)
    fresh = (row < mem_count) & (at[FRESH] == 1)
    x[:32, :] = jnp.where(fresh, small[:32, :], x[:32, :].astype(WIDE)).astype(LOW)
    lane = lax.broadcasted_iota(jnp.int32, (1, PAIR), 1)
    scale = jnp.where(lax.broadcasted_iota(jnp.int32, (1, 3 * PAIR), 1) < PAIR, 0.125, 1.0)

    def one_pair(pair, _):
        here = pl.ds(pl.multiple_of(t * part + pair * PAIR, PAIR), PAIR)
        q_bias = small[first_bias : first_bias + 1, here]
        v_bias = small[first_bias + 1 : first_bias + 2, here]
        bias = jnp.concatenate([q_bias, jnp.zeros_like(q_bias), v_bias], axis=1)
        got = (nn(x[...], w[:, lanes(pair, 3 * PAIR)]) + bias).astype(LOW)
        got = (got.astype(WIDE) * scale).astype(LOW)
        qkv[:, lanes(pair, 3 * PAIR)] = got
        keys, values = got[:, PAIR : 2 * PAIR], got[:, 2 * PAIR :]
        q = heads_apart(got[:, :PAIR])
        for low in range(0, 2 * rows, FORWARD_BLOCK):
            here, there = slice(low, low + FORWARD_BLOCK), slice(low % rows, low % rows + FORWARD_BLOCK)
            v = nt(q[here], keys) + mask[there, :]
            top = jnp.max(v, axis=-1, keepdims=True)
            e = jnp.exp(v - top)
            total = jnp.sum(e, axis=-1, keepdims=True)
            out = nn((e * (1.0 / total)).astype(LOW), values)
            spot = lane == 2 * pair + low // rows
            lse[there, :] = jnp.where(spot, top + jnp.log(total), lse[there, :])
            if low < rows:
                s[there, :] = out
            else:
                mixed[there, :] = jnp.where(lane < HEAD, s[there, :], out).astype(LOW)
        mix_own[:, lanes(pair, PAIR)] = mixed[pl.ds(pl.multiple_of(t * padded, 16), padded), :]
        mix_sent[:, lanes(pair, PAIR)] = mixed[
            pl.ds(pl.multiple_of((1 - t) * padded, 16), padded), :
        ]
        return 0

    lax.fori_loop(0, part // PAIR, one_pair, 0)


def backward_kernel(
    half_rows, mem_count, starts, at, qkv, own, got, lse, dproj, sums, mask, s, p, ds, dmix
):
    rows, padded = qkv.shape[0], own.shape[0]
    part = own.shape[1]
    t = at[T]
    fill_mask(mask, at, half_rows, mem_count, starts)
    dmix[pl.ds(pl.multiple_of(t * padded, 16), padded), :] = own[...]
    dmix[pl.ds(pl.multiple_of((1 - t) * padded, 16), padded), :] = got[...]
    lane = lax.broadcasted_iota(jnp.int32, (1, PAIR), 1)
    zero = jnp.zeros((), LOW)

    def one_pair(pair, _):
        here = lanes(pair, 3 * PAIR)
        whole = qkv[:, here]
        keys, values = whole[:, PAIR : 2 * PAIR], whole[:, 2 * PAIR :]
        dm_pair = dmix[:, lanes(pair, PAIR)]
        q, dm = heads_apart(whole[:, :PAIR]), heads_apart(dm_pair)
        for low in range(0, 2 * rows, BACKWARD_BLOCK):
            block, there = slice(low, low + BACKWARD_BLOCK), slice(low % rows, low % rows + BACKWARD_BLOCK)
            spot = lane == 2 * pair + low // rows
            stat = jnp.sum(jnp.where(spot, lse[there, :], 0.0), axis=-1, keepdims=True)
            e = jnp.exp(nt(q[block], keys) + mask[there, :] - stat)
            d = nt(dm[block], values)
            dot = jnp.sum(e * d, axis=-1, keepdims=True)
            p[block, :] = e.astype(LOW)
            d = (e * (d - dot)).astype(LOW)
            ds[block, :] = d
            s[block, :] = nn(d, keys)
        dq = jnp.where(lane < HEAD, s[:rows, :], s[rows:, :]) * 0.125
        dk, dv = tn(ds[...], q), tn(p[...], dm)
        out = jnp.concatenate([dq, dk, dv], axis=1).astype(LOW)
        dproj[:, here] = out
        sums[:, here] = jnp.sum(out.astype(WIDE), axis=0, keepdims=True)
        return 0

    lax.fori_loop(0, part // PAIR, one_pair, 0)


def half_rows_of(ref, which, padded):
    return ref[pl.ds(pl.multiple_of(which * padded, 16), padded), :]


def projection_gradient_kernel(
    small_rows, lines, at, layer_in, d_projected, proj_sums, sums_one, two0, two1, up_sums, wqkv, d_attn,
    *refs,
):
    grads, (turn, rows) = refs[:-2], refs[-2:]
    cols = d_projected.shape[1]
    part = cols // 3
    first = at[T] == 0
    turn[...] = jnp.zeros_like(turn)
    (m0, m1), (v0, _), (g0, _) = small_rows
    count = m1 - m0
    memory = nt(d_projected[:32, :], wqkv[:, :cols])[:count]
    memory = memory + jnp.where(first, d_attn[:count, :], 0.0)
    turn[m0:m1, :] = jnp.where(at[FRESH] == 1, memory, 0.0)
    sums = [
        jnp.concatenate(
            [proj_sums[:, (3 * p + k) * PAIR : (3 * p + k + 1) * PAIR] for p in range(part // PAIR)],
            axis=1,
        )
        for k in (0, 2)
    ]
    for low, value in enumerate(sums, v0):
        turn[low : low + 1, :part] = jnp.where(first, value, 0.0)
        turn[low : low + 1, part:] = jnp.where(first, 0.0, value)
    sums_two = two0[...] + two1[...]
    turn[v0 + 2 : v0 + 4, :] = sums_one[0:2, :]
    turn[v0 + 4 : v0 + 6, :] = sums_two[0:2, :]
    turn[g0 : g0 + 1, :] = sums_one[2:3, :]
    turn[g0 + 1 : g0 + 2, :] = sums_two[2:3, :]
    rows[...] = turn[...].T
    half = rows.shape[0] // 2
    each = up_sums.shape[1] * lines // half
    for n in range(half // lines):
        value = up_sums[:, n * each : (n + 1) * each]
        for side, low in ((0, n * lines), (1, half + n * lines)):
            rows[low : low + 1, UP_AT : UP_AT + each] = jnp.where(at[T] == side, value, 0.0)
    small = rows[...]
    put_gradient(layer_in, d_projected, grads, at[CORE])
    if len(grads) == 1:
        grads[0][:, cols:] = small.astype(LOW)
    else:
        put_blocks(small, grads[0], grads[-1], at[CORE], cols)


def projection_back_kernel(at, d_projected, wqkv, d_attn, d_own, d_sent):
    padded, cols = d_own.shape[0], d_projected.shape[1]
    t = at[T]
    d_own[...] = d_attn[...] + nt(half_rows_of(d_projected, t, padded), wqkv[:, :cols])
    d_sent[...] = nt(half_rows_of(d_projected, 1 - t, padded), wqkv[:, :cols]).astype(LOW)


def finish_kernel(
    part, small_rows, count, at, *refs
):
    parts, (qkv, out, memory, vectors, gains, up, turn) = refs[:count], refs[count:]
    total = parts[0][...]
    for value in parts[1:]:
        total = total + value[...].astype(WIDE)
    lines = total.shape[0]
    cols, width = 3 * part, 2 * part
    mine, got = total[:, : cols + PAIR], total[:, cols + PAIR + width :]
    first = at[T] == 0
    for pair in range(part // PAIR):
        for kind in range(3):
            here = (3 * pair + kind) * PAIR
            a, b = mine[:, here : here + PAIR], got[:, here : here + PAIR]
            low = kind * width + pair * PAIR
            qkv[:, low : low + PAIR] = jnp.where(first, a, b)
            qkv[:, low + part : low + part + PAIR] = jnp.where(first, b, a)
    out[...] = total[:, cols + PAIR : cols + PAIR + width]
    turn[...] = jnp.zeros_like(turn)
    turn[:lines, :] = mine[:, cols:] + got[:, cols:]
    up[...] = turn[0:1, UP_AT : UP_AT + up.shape[1]]
    small = turn[...].T
    for target, (low, high) in zip((memory, vectors, gains), small_rows):
        target[...] = small[low:high, :lines]


def spread_of(v):
    return jnp.mean(v, axis=-1, keepdims=True)


def first_norm_kernel(bias, gain, at, own, got, wout, layer_in, small, mixed, unit, scale, normed, s):
    padded, part = own.shape
    first = at[T] == 0
    mixed[:, :part] = jnp.where(first, own[...], got[...])
    mixed[:, part:] = jnp.where(first, got[...], own[...])
    s[...] = nn(mixed[...], wout[...])
    for low in range(0, padded, ROWS):
        here = slice(low, low + ROWS)
        rows = layer_in[pl.ds(pl.multiple_of(at[T] * padded + low, ROWS), ROWS), :]
        total = rows.astype(WIDE) + (s[here, :] + small[bias + 2 : bias + 3, :])
        centered = total - spread_of(total)
        factor = lax.rsqrt(spread_of(centered * centered) + NORM_EPSILON)
        value = centered * factor
        unit[here, :] = value
        scale[here, :] = jnp.broadcast_to(factor, (ROWS, PAIR))
        value = value * small[gain : gain + 1, :] + small[bias + 3 : bias + 4, :]
        normed[here, :] = value.astype(LOW)


def add_sums(sums, values):
    sums[...] = jnp.zeros_like(sums)
    for n, value in enumerate(values):
        sums[n : n + 1, :] = jnp.sum(value, axis=0, keepdims=True)


def second_norm_kernel(
    bias, gain, start, at, unit, small, own, got, d_out, _, layer_out, d_second, d_ffn, sums
):
    width = unit.shape[1]
    real = d_out.shape[0] - start
    totals = [jnp.zeros((ROWS, width), WIDE)] * 3
    for low in range(0, got.shape[0], ROWS):
        here, there = slice(low, low + ROWS), slice(start + low, start + low + ROWS)
        count = min(ROWS, real - low)
        first = unit[there, :] * small[gain : gain + 1, :] + small[bias + 3 : bias + 4, :]
        ffn = own[there, :] + got[here, :].astype(WIDE) + small[bias + 4 : bias + 5, :]
        total = first + ffn
        centered = total - spread_of(total)
        factor = lax.rsqrt(spread_of(centered * centered) + NORM_EPSILON)
        value = centered * factor
        out = value * small[gain + 1 : gain + 2, :] + small[bias + 5 : bias + 6, :]
        layer_out[low : low + count, :] = out[:count].astype(LOW)
        cotangent = d_out[start + low : start + low + count, :].astype(WIDE)
        if count < ROWS:
            cotangent = jnp.concatenate(
                [cotangent, jnp.zeros((ROWS - count, width), WIDE)], axis=0
            )
        d_unit = cotangent * small[gain + 1 : gain + 2, :]
        back = factor * (d_unit - spread_of(d_unit) - value * spread_of(d_unit * value))
        d_second[here, :] = back
        rounded = back.astype(LOW)
        d_ffn[here, :] = rounded
        terms = (rounded.astype(WIDE), cotangent, cotangent * value)
        totals = [a + b for a, b in zip(totals, terms)]
    add_sums(sums, totals)


def first_back_kernel(
    gain, at, second0, second1, own, got, unit, scale, small, wout, d_attn_in, d_attn, mix_own, mix_sent, sums
):
    padded, width = unit.shape
    part = mix_own.shape[1]
    totals = [jnp.zeros((ROWS, width), WIDE)] * 3
    for low in range(0, padded, ROWS):
        here = slice(low, low + ROWS)
        cut = second0.shape[0]
        second = second0[here, :] if low < cut else second1[low - cut : low - cut + ROWS, :]
        cotangent = second + own[here, :] + got[here, :].astype(WIDE)
        value = unit[here, :]
        d_unit = cotangent * small[gain : gain + 1, :]
        back = d_unit - spread_of(d_unit) - value * spread_of(d_unit * value)
        back = scale[here, :1] * back
        d_attn_in[here, :] = back
        rounded = back.astype(LOW)
        d_attn[here, :] = rounded
        terms = (rounded.astype(WIDE), cotangent, cotangent * value)
        totals = [a + b for a, b in zip(totals, terms)]
    add_sums(sums, totals)
    mixed = nt(d_attn[...], wout[...]).astype(LOW)
    first = at[T] == 0
    mix_own[...] = jnp.where(first, mixed[:, :part], mixed[:, part:])
    mix_sent[...] = jnp.where(first, mixed[:, part:], mixed[:, :part])


def rows_kernel(mem_count, at, own, got, out):
    real = out.shape[0]
    row = lax.broadcasted_iota(jnp.int32, (32, 1), 0)
    fresh = (row < mem_count) & (at[FRESH] == 1) & (at[T] == 0)
    out[:32, 0, :] = jnp.where(fresh, 0.0, own[:32, :] + got[:32, :].astype(WIDE))
    out[32:, 0, :] = own[32:real, :] + got[32:real, :].astype(WIDE)


def gelu_parts(pre):
    cdf = 0.5 * (1.0 + lax.erf(pre * 0.7071067811865476))
    density = jnp.exp(-0.5 * pre * pre) * 0.3989422804014327
    return pre * cdf, cdf + pre * density


def shards(
    rows_in,
    d_out,
    starts,
    lengths,
    resets,
    qkv_weight,
    out_weight,
    bias_vec,
    gains,
    mem_init,
    ffn_up,
    up_bias,
    ffn_down,
):
    half_rows, seg_count, width = rows_in.shape
    assert seg_count == 1
    dp_count, t_count = lax.axis_size("dp"), lax.axis_size("tensor")
    assert t_count == 2
    digits = digits_of(dp_count)
    x_digit, core_digit = digits[-2:]
    padded = ceil_to(half_rows, 16)
    rows = 2 * padded
    mem_count = mem_init.shape[0]
    part = HEADS // t_count * HEAD
    cols = 3 * part
    hidden_mine = ffn_up.shape[1]
    feat = bias_vec.shape[1]
    lines = qkv_weight.shape[0]
    doc_count = starts.shape[1]
    counts = (mem_count, bias_vec.shape[0], gains.shape[0])
    edges = [sum(counts[:n]) for n in range(len(counts) + 1)]
    small_rows = tuple(zip(edges[:-1], edges[1:]))
    bias, gain = edges[1], edges[2]
    integers = [
        lax.axis_index("tensor"),
        digit_at(x_digit),
        digit_at(core_digit),
        digit_at(digits[-3]),
        lax.axis_index("dp"),
        resets[0],
        lengths[0],
    ]
    at = jnp.concatenate([jnp.stack(integers).astype(jnp.int32), starts[0]])

    side = lax.axis_index("tensor").astype(jnp.int32).reshape(1)
    (packed,) = call(
        functools.partial(columns_kernel, small_rows),
        [low_of(lines, 3 * width + PAIR + width)],
        side, qkv_weight, bias_vec, gains, mem_init, up_bias.reshape(1, -1), out_weight,
        scratch=[pltpu.VMEM((PAIR, PAIR), WIDE)],
        room=57 << 20,
    )
    rows_low = jnp.pad(tie(rows_in, packed)[:, 0, :], ((0, padded - half_rows), (0, 0)))
    rows_other = swap_tensor(rows_low)
    up_pair = spread_near(tie(ffn_up, packed), digits)
    first_z = spread_outer(packed, digits)
    rows_other, up_pair = join(rows_other, tie(up_pair, first_z))
    slots = first_z.shape[0]
    mine, other = call(
        functools.partial(halves_of_heads_kernel, part),
        [low_of(slots, lines, cols + PAIR + width), low_of(slots, lines, cols + PAIR)],
        at, first_z,
    )
    first_parts = [mine, swap_tensor(other), rotate(mine, x_digit, 1), swap_both(other, x_digit)]
    up_z = spread_far(up_pair, digits)
    down_pair = spread_near(tie(ffn_down.T, mine), digits)
    *first_parts, up_z, down_in = join(*first_parts, up_z, down_pair)
    first_parts = [jnp.concatenate(first_parts[n : n + 2], axis=2) for n in (0, 2)]
    core_parts = [rotate(value, core_digit, 1) for value in first_parts]
    sizes = tuple(size for _, size in digits)
    (wqkv,) = call(
        functools.partial(assemble_first_kernel, sizes),
        [low_of(dp_count, 2 * lines, cols + PAIR)],
        at, *first_parts, *core_parts,
    )
    wqkv = wqkv.reshape(width, cols + PAIR)
    (out_sent,) = call(
        functools.partial(beside_kernel, cols + PAIR),
        [low_of(dp_count // 2, lines, width)], at, *first_parts,
    )
    out_got = swap_tensor(out_sent)
    up_x = rotate(up_z, x_digit, 1)
    down_pieces = spread_far_pieces(down_in, digits)
    down_x = [rotate(down_pieces[0], x_digit, 1)]

    projected, mix_own, mix_sent, log_total, layer_in, small = call(
        functools.partial(forward_kernel, half_rows, mem_count, doc_count, bias),
        [
            low_of(rows, cols),
            low_of(padded, part),
            low_of(padded, part),
            wide_of(rows, PAIR),
            low_of(rows, width),
            wide_of(ceil_to(edges[-1], 32), width),
        ],
        at, rows_low, rows_other, wqkv,
        scratch=[
            pltpu.VMEM((rows, rows), WIDE),
            pltpu.VMEM((rows, PAIR), WIDE),
            pltpu.VMEM((rows, PAIR), LOW),
        ],
    )
    mix_got = swap_tensor(mix_sent)
    out_got = tie(out_got, mix_sent)
    (wout,) = call(
        functools.partial(assemble_out_kernel, sizes, cols + PAIR),
        [low_of(dp_count, 2 * lines, width)],
        at, *first_parts, *core_parts, out_got, rotate(out_got, core_digit, 1),
    )
    wout = wout.reshape(width, width)
    mix_got, *down_pieces = join(mix_got, *down_pieces)
    mixed, unit, scale, normed_own = call(
        functools.partial(first_norm_kernel, bias, gain),
        [low_of(padded, width), wide_of(padded, width), wide_of(padded, PAIR), low_of(padded, width)],
        at, mix_own, mix_got, wout, layer_in, small,
        scratch=[pltpu.VMEM((padded, width), WIDE)],
    )

    normed_got = swap_tensor(normed_own)
    up_x, up_z = tie(up_x, mix_sent), tie(up_z, mix_sent)
    down_pieces = [tie(piece, mix_sent) for piece in down_pieces]
    down_x = [tie(down_x[0], mix_sent)]
    up = assemble(at, swap_blocks(up_z, up_x, digits), digits, hidden_mine, paired=True)
    (up_b,) = call(
        functools.partial(up_row_kernel, lines), [wide_of(ROWS, hidden_mine)], at, wqkv,
        scratch=[pltpu.VMEM((1, hidden_mine), WIDE)],
    )
    down_pieces[1], down_x[0] = join(down_pieces[1], down_x[0])
    down_x.append(rotate(down_pieces[1], x_digit, 1))
    normed_got, up_b, up = join(normed_got, up_b, up)
    down_t = assemble(at, swap_pieces(down_pieces, down_x, digits), digits, hidden_mine, paired=True)

    def feed_forward(rows):
        pre_act = nn(rows, up).reshape(-1, *up_b.shape) + up_b
        hidden, slope = (part.reshape(rows.shape[0], -1) for part in gelu_parts(pre_act))
        hidden = hidden.astype(LOW)
        return hidden, slope, nt(hidden, down_t)

    cut = ceil_to(padded // 2, ROWS)
    pieces = ((0, cut), (cut, padded))
    hidden_got, slope_got, ffn_sent = feed_forward(normed_got)
    ffn_sent = ffn_sent.astype(LOW)
    (_, first_cut), (_, end) = pieces
    ffn_got = [swap_tensor(ffn_sent[:first_cut])]
    hidden_own, slope_own, ffn_own = call(
        own_forward_kernel,
        [low_of(padded, hidden_mine), wide_of(padded, hidden_mine), wide_of(padded, width)],
        at, normed_own, up, up_b, down_t, rotate(ffn_sent[:ROWS, :PAIR], core_digit, 1),
    )
    ffn_got.append(swap_tensor(tie(ffn_sent, ffn_own)[first_cut:end]))
    d_out_rows = d_out.reshape(half_rows, width)
    second, ahead = [], small
    for (low, high), got in zip(pieces, ffn_got):
        if second:
            ahead = rotate(second[-1][2][:ROWS, :PAIR], core_digit, 1)
        outs = [
            low_of(min(high, half_rows) - low, width),
            wide_of(high - low, width),
            low_of(high - low, width),
            wide_of(8, width),
        ]
        kernel = functools.partial(second_norm_kernel, bias, gain, low)
        second.append(call(kernel, outs, at, unit, small, ffn_own, got, d_out_rows, ahead))
    layer_out, d_second, d_ffn_sent, sums_two = zip(*second)

    d_ffn_got = jnp.concatenate([swap_tensor(piece) for piece in d_ffn_sent], axis=0)
    d_ffn_own = jnp.concatenate(d_ffn_sent, axis=0)

    def feed_back(rows, slope):
        d_pre = (slope * nn(rows, down_t)).astype(LOW)
        return d_pre, nt(d_pre, up)

    d_pre_own, d_first_own = feed_back(d_ffn_own, slope_own)
    down_own, up_own, sums_own = call(
        own_kernel,
        [wide_of(width, hidden_mine), wide_of(width, hidden_mine), wide_of(1, hidden_mine)],
        at, d_ffn_own, hidden_own, normed_own, d_pre_own,
    )
    d_ffn_got, d_first_own, down_own, up_own = join(d_ffn_got, d_first_own, down_own, up_own)
    d_pre_got, d_first_sent = feed_back(d_ffn_got, slope_got)
    d_first_sent = d_first_sent.astype(LOW)
    d_first_got = swap_tensor(d_first_sent)

    outs = gradient_outs(width, hidden_mine, dp_count)
    down_grads = call(
        rest_kernel, outs, at, down_own, tie(d_ffn_got, d_first_sent), hidden_got
    )
    down_kept, down_sent = halve(at, *swap_cores(down_grads, dp_count, core_digit))
    down_got = rotate(down_sent, x_digit, 1)
    up_sums, *up_grads = call(
        rest_sums_kernel, [wide_of(1, hidden_mine)] + outs,
        at, up_own, sums_own, normed_got, tie(d_pre_got, down_sent),
    )
    up_kept, up_sent = halve(at, *swap_cores(up_grads, dp_count, core_digit))

    d_attn_in, d_attn, d_mix_own, d_mix_sent, sums_one = call(
        functools.partial(first_back_kernel, gain),
        [
            wide_of(padded, width),
            low_of(padded, width),
            low_of(padded, part),
            low_of(padded, part),
            wide_of(8, width),
        ],
        at, *d_second, d_first_own, d_first_got, unit, scale, small, wout,
    )
    d_mix_got = swap_tensor(d_mix_sent)
    out_grads = call(
        out_gradient_kernel, gradient_outs(width, width, dp_count, OUT_TILE),
        at, mixed, tie(d_attn, d_mix_sent),
    )
    out_kept, out_parts = swap_cores(out_grads, dp_count, core_digit)
    out_kept, out_sent = call(
        rows_halves_kernel, [low_of(dp_count // 2, lines, width)] * 2, at, out_kept, *out_parts
    )
    down_kept, down_sent = far_parts(at, down_kept, down_got, digits)
    d_mix_got, out_sent, up_sent, down_sent = join(d_mix_got, out_sent, up_sent, down_sent)
    down_got = rotate(down_sent, digits[-3], 2)
    out_got = swap_tensor(out_sent)
    up_got = rotate(up_sent, x_digit, 1)

    d_projected, proj_sums = call(
        functools.partial(backward_kernel, half_rows, mem_count, doc_count),
        [low_of(rows, cols), wide_of(1, cols)],
        at, projected, d_mix_own, d_mix_got, log_total,
        scratch=[
            pltpu.VMEM((rows, rows), WIDE),
            pltpu.VMEM((2 * rows, PAIR), WIDE),
            pltpu.VMEM((2 * rows, rows), LOW),
            pltpu.VMEM((2 * rows, rows), LOW),
            pltpu.VMEM((rows, part), LOW),
        ],
    )
    up_kept, up_sent = far_parts(at, up_kept, up_got, digits)
    qkv_grads = call(
        functools.partial(projection_gradient_kernel, small_rows, lines),
        gradient_outs(width, cols + PAIR, dp_count),
        at, layer_in, d_projected, proj_sums, sums_one, *sums_two, up_sums, wqkv, d_attn_in,
        scratch=[pltpu.VMEM((PAIR, width), WIDE), pltpu.VMEM((width, PAIR), WIDE)],
    )
    out_got, down_got, *qkv_grads = join(out_got, down_got, *qkv_grads)
    down_kept, down_sent = near_parts(at, down_kept, down_got)
    qkv_kept, qkv_parts = swap_cores(qkv_grads, dp_count, core_digit)
    up_sent, *qkv_parts = join(up_sent, *qkv_parts)
    slots = dp_count // 4
    mine, to_x, to_y, to_both = call(
        quarter_kernel,
        [low_of(slots, lines, cols + PAIR + width)] * 2 + [low_of(slots, lines, cols + PAIR)] * 2,
        at, qkv_kept, *qkv_parts, out_kept, out_got,
    )

    both_got = [rotate(to_x, x_digit, 1), swap_tensor(to_y), swap_both(to_both, x_digit)]
    up_got = rotate(up_sent, digits[-3], 2)
    down_got = swap_near(down_sent, digits[-3])
    d_in_own, d_in_sent = call(
        projection_back_kernel, [wide_of(padded, width), low_of(padded, width)],
        at, tie(d_projected, to_x), wqkv, d_attn_in,
    )
    d_in_got = swap_tensor(d_in_sent)
    ahead = rotate(tie(d_in_sent, up_got)[:ROWS, :PAIR], core_digit, 1)
    up_kept, up_sent = near_parts(at, up_kept, up_got, ahead)
    *both_got, up_sent, down_got = join(*both_got, up_sent, down_got)
    up_got = swap_near(up_sent, digits[-3])
    both_kept, both_sent = outer_parts(at, digits, mine, *both_got)
    both_got = outer_send(both_sent, digits)
    grad_ffn_down = outer_sum(down_kept, [down_got], digits)
    grad_ffn_up = outer_sum(up_kept, [up_got], digits)
    (grad_rows,) = call(
        functools.partial(rows_kernel, mem_count), [wide_of(half_rows, 1, width)], at, d_in_own, d_in_got
    )
    grad_rows, *both_got = join(grad_rows, *both_got)

    if len(digits) == 3:
        parts = [both_kept[0], *[part[0] for part in both_got]]
    else:
        parts = [outer_sum(both_kept, both_got, digits)]
    grad_qkv, grad_out_weight, grad_mem, grad_vec, grad_gains, grad_up_bias = call(
        functools.partial(finish_kernel, part, small_rows, len(parts)),
        [wide_of(lines, 3 * width), wide_of(lines, width)]
        + [wide_of(n, feat) for n in counts]
        + [wide_of(1, up_bias.shape[0])],
        at, *parts,
        scratch=[pltpu.VMEM((PAIR, PAIR), WIDE)],
    )
    return (
        jnp.concatenate(layer_out, axis=0).reshape(half_rows, 1, width),
        grad_rows,
        grad_qkv,
        grad_out_weight,
        grad_vec,
        grad_gains,
        grad_mem,
        grad_ffn_up,
        grad_up_bias.reshape(up_bias.shape),
        grad_ffn_down.T,
    )


def solution(mesh):
    both = ("dp", "tensor")
    in_specs = (
        P("tensor", "dp", None),
        P("tensor", "dp", None),
        P("dp", None),
        P("dp"),
        P("dp"),
        P(both, None),
        P(both, None),
        P(None, both),
        P(None, both),
        P(None, both),
        P("dp", "tensor"),
        P(both),
        P("tensor", "dp"),
    )
    out_specs = (
        P("tensor", "dp", None),
        P("tensor", "dp", None),
        P(both, None),
        P(both, None),
        P(None, both),
        P(None, both),
        P(None, both),
        P("dp", "tensor"),
        P(both),
        P("tensor", "dp"),
    )
    return jax.shard_map(shards, mesh=mesh, in_specs=in_specs, out_specs=out_specs, check_vma=False)
```

```python
import functools

import jax
import jax.numpy as jnp
import numpy as np
from jax import lax
from jax.experimental import pallas as pl
from jax.experimental.pallas import tpu as pltpu
from jax.sharding import PartitionSpec as P

HEADS = 12
HEAD = 64
NORM_EPSILON = 1e-06
LOW = jnp.bfloat16
WIDE = jnp.float32
CHUNK = 32
FORWARD_BLOCK = 272
BACKWARD_BLOCK = 544
TILE = 384
OUT_TILE = 256
ROWS = 16
PAIR = 2 * HEAD
UP_AT = 32
QUICK = pl.CostEstimate(flops=1, bytes_accessed=1, transcendentals=0)
T, X, CORE, OUTER, DP, FRESH, LENGTH, STARTS = range(8)


def ceil_to(count, unit):
    return -(-count // unit) * unit


def nn(a, b):
    return lax.dot_general(a, b, (((1,), (0,)), ((), ())), preferred_element_type=WIDE)


def nt(a, b):
    return lax.dot_general(a, b, (((1,), (1,)), ((), ())), preferred_element_type=WIDE)


def tn(a, b):
    return lax.dot_general(a, b, (((0,), (0,)), ((), ())), preferred_element_type=WIDE)


def low_of(*shape):
    return jax.ShapeDtypeStruct(shape, LOW)


def wide_of(*shape):
    return jax.ShapeDtypeStruct(shape, WIDE)


def held_bytes(array):
    rows, cols = ((1,) + tuple(array.shape))[-2:]
    lead = int(np.prod(array.shape[:-2])) if len(array.shape) > 2 else 1
    return lead * ceil_to(rows, 16) * ceil_to(cols, 128) * jnp.dtype(array.dtype).itemsize


def call(kernel, outs, at, *arrays, scratch=(), room=0):
    room += sum(held_bytes(array) for array in (*arrays, *outs))
    room += sum(held_bytes(ref) for ref in scratch)
    return pl.pallas_call(
        kernel,
        in_specs=[pl.BlockSpec(memory_space=pltpu.SMEM)]
        + [pl.BlockSpec(memory_space=pltpu.VMEM)] * len(arrays),
        out_specs=[pl.BlockSpec(memory_space=pltpu.VMEM)] * len(outs),
        out_shape=list(outs),
        scratch_shapes=list(scratch),
        compiler_params=pltpu.CompilerParams(vmem_limit_bytes=room + (9 << 20)),
        cost_estimate=QUICK,
    )(at, *arrays)


def digits_of(dp_count):
    assert dp_count % 4 == 0
    sizes = [2, 2]
    left = dp_count // 4
    while left > 1:
        size = next((s for s in (4, 2, 3) if left % s == 0), left)
        sizes.append(size)
        left //= size
    if len(sizes) == 2:
        sizes.append(1)
    digits, stride = [], 1
    for size in sizes:
        digits.append((stride, size))
        stride *= size
    return digits[::-1]


def digit_at(digit):
    stride, size = digit
    return (lax.axis_index("dp") // stride) % size


def rotate(value, digit, step):
    stride, size = digit
    pairs = []
    for at in range(lax.axis_size("dp")):
        mine = (at // stride) % size
        pairs.append((at, at + ((mine + step) % size - mine) * stride))
    return lax.ppermute(value, "dp", pairs)


def swap_tensor(value):
    return lax.ppermute(value, "tensor", [(0, 1), (1, 0)])


def swap_both(value, digit):
    stride, _ = digit
    pairs = []
    for at in range(lax.axis_size("dp")):
        other = at + stride if (at // stride) % 2 == 0 else at - stride
        pairs += [(2 * at + side, 2 * other + 1 - side) for side in range(2)]
    return lax.ppermute(value, ("dp", "tensor"), pairs)


def tie(value, *others):
    return lax.optimization_barrier((value,) + others)[0]


join = lambda *values: lax.optimization_barrier(values)


def spread_outer(value, digits):
    for digit in reversed(digits[:-2]):
        got = [value] + [rotate(value, digit, step) for step in range(1, digit[1])]
        value = jnp.stack(got)
    return value.reshape((-1,) + value.shape[-2:])


def swap_near(value, digit):
    stride, _ = digit
    pairs = []
    for at in range(lax.axis_size("dp")):
        pairs.append((at, at + stride if (at // stride) % 2 == 0 else at - stride))
    return lax.ppermute(value, "dp", pairs)


def spread_near(value, digits):
    assert digits[-3][1] == 4
    return jnp.stack([value, swap_near(value, digits[-3])])


def spread_far(pair, digits):
    value = jnp.concatenate([pair, rotate(pair, digits[-3], 2)], axis=0)
    for digit in reversed(digits[:-3]):
        value = jnp.stack([value] + [rotate(value, digit, step) for step in range(1, digit[1])])
    return value.reshape((-1,) + value.shape[-2:])


def spread_far_pieces(pair, digits):
    pieces = [pair, rotate(pair, digits[-3], 2)]
    for digit in reversed(digits[:-3]):
        for n, value in enumerate(pieces):
            value = jnp.stack([value] + [rotate(value, digit, step) for step in range(1, digit[1])])
            pieces[n] = value.reshape((-1,) + value.shape[-2:])
    return pieces


def placer(sizes, me, paired):
    outer, digits = sizes[:-2], []
    for size in reversed(sizes):
        digits.append(lax.rem(me, size))
        me = lax.div(me, size)
    digits = digits[::-1]

    def place_of(swap_core, swap_x, slot):
        steps = []
        for size in reversed(outer):
            steps.append(slot % size)
            slot //= size
        place = 0
        for n, (size, digit, step) in enumerate(zip(outer, digits, steps[::-1])):
            if paired and n == len(outer) - 1:
                at = lax.bitwise_xor(digit, step)
            else:
                at = lax.rem(digit + (size - step), size)
            place = place * size + at
        x, core = digits[-2], digits[-1]
        place = place * 2 + (1 - x if swap_x else x)
        return place * 2 + (1 - core if swap_core else core)

    return place_of


def assemble_kernel(sizes, paired, at, *refs):
    *parts, whole = refs
    cols = whole.shape[2]
    pieces = len(parts) // 4
    place_of = placer(sizes, at[DP], paired)
    for swap_core in range(2):
        for swap_x in range(2):
            for piece in range(pieces):
                source = parts[pieces * (2 * swap_core + swap_x) + piece]
                for block in range(source.shape[0]):
                    slot = 2 * (pieces * (block // 2) + piece) + block % 2
                    whole[place_of(swap_core, swap_x, slot)] = source[block, :, :cols]


def swap_blocks(mine, x_got, digits):
    core = digits[-1]
    return [mine, x_got, rotate(mine, core, 1), rotate(x_got, core, 1)]


def swap_pieces(mine, x_got, digits):
    core = digits[-1]
    return [*mine, *x_got] + [rotate(piece, core, 1) for piece in (*mine, *x_got)]


def assemble(at, parts, digits, cols, paired=False):
    rows = parts[0].shape[1]
    blocks = sum(part.shape[0] for part in parts)
    sizes = tuple(size for _, size in digits)
    (whole,) = call(
        functools.partial(assemble_kernel, sizes, paired),
        [low_of(blocks, rows, cols)],
        at,
        *parts,
    )
    return whole.reshape(blocks * rows, cols)


def assemble_first_kernel(sizes, at, *refs):
    parts, whole = refs[:4], refs[4]
    lines, cols = whole.shape[1] // 2, whole.shape[2]
    place_of = placer(sizes, at[DP], False)
    first = at[T] == 0
    for swap_core in range(2):
        for swap_x in range(2):
            source = parts[2 * swap_core + swap_x]
            far = source.shape[2] - cols
            for slot in range(source.shape[0]):
                place = place_of(swap_core, swap_x, slot)
                a, b = source[slot, :, :cols], source[slot, :, far:]
                whole[place, :lines] = jnp.where(first, a, b)
                whole[place, lines:] = jnp.where(first, b, a)


def assemble_out_kernel(sizes, cols, at, *refs):
    parts, gots, whole = refs[:4], refs[4:6], refs[6]
    place_of = placer(sizes, at[DP], False)
    first = at[T] == 0
    lines, width = whole.shape[1] // 2, whole.shape[2]
    for swap_core in range(2):
        for swap_x in range(2):
            source, got = parts[2 * swap_core + swap_x], gots[swap_core]
            slots = source.shape[0]
            for slot in range(slots):
                mine, other = source[slot, :, cols : cols + width], got[swap_x * slots + slot]
                place = place_of(swap_core, swap_x, slot)
                whole[place, :lines] = jnp.where(first, mine, other)
                whole[place, lines:] = jnp.where(first, other, mine)


def columns_kernel(small_rows, at, weight, vectors, gains, memory, up, out, packed, turn):
    lines, width = weight.shape
    packed[:, :width] = weight[...]
    turn[...] = jnp.zeros_like(turn)
    for source, (low, high) in zip((memory, vectors, gains), small_rows):
        turn[low:high, :lines] = source[...].astype(WIDE)
    columns = turn[...].T[:lines]
    turn[:lines, :] = columns
    turn[0:1, UP_AT : UP_AT + up.shape[1]] = up[...].astype(WIDE)
    packed[:, width : width + PAIR] = turn[:lines, :].astype(LOW)
    packed[:, width + PAIR :] = out[...]


def halves_of_heads_kernel(part, at, packed, mine, other):
    width = 6 * part
    first = at[T] == 0
    for slot in range(packed.shape[0]):
        for pair in range(part // PAIR):
            for kind in range(3):
                low = 2 * kind * part + pair * PAIR
                a = packed[slot, :, low : low + PAIR]
                b = packed[slot, :, low + part : low + part + PAIR]
                here = (3 * pair + kind) * PAIR
                mine[slot, :, here : here + PAIR] = jnp.where(first, a, b)
                other[slot, :, here : here + PAIR] = jnp.where(first, b, a)
        mine[slot, :, 3 * part :] = packed[slot, :, width:]
        other[slot, :, 3 * part :] = packed[slot, :, width : width + PAIR]


def beside_kernel(cols, at, mine, x_got, out):
    slots = mine.shape[0]
    for n, source in enumerate((mine, x_got)):
        for slot in range(slots):
            out[n * slots + slot] = source[slot, :, cols : cols + out.shape[2]]


def put_blocks(total, kept, sent, core, at):
    groups, rows, _ = kept.shape
    cols = total.shape[1]
    total = total.astype(LOW).reshape(2 * groups, rows, cols)
    second = core == 1
    for group in range(groups):
        even, odd = total[2 * group], total[2 * group + 1]
        kept[group, :, at : at + cols] = jnp.where(second, odd, even)
        sent[group] = jnp.where(second, even, odd)


def put_gradient(a, b, outs, core, own=None, tile=TILE):
    whole = tn(a[...], b[...])
    for n, low in enumerate(range(0, b.shape[1], tile)):
        total = whole[:, low : low + tile]
        if own is not None:
            total = total + own[:, low : low + tile]
        if len(outs) == 1:
            outs[0][:, low : low + tile] = total.astype(LOW)
        else:
            put_blocks(total, outs[0], outs[1 + n], core, low)


def gradient_outs(width, cols, dp_count, tile=TILE):
    rows = width // dp_count
    if rows % 16:
        return [low_of(width, cols)]
    tiles = [min(tile, cols - low) for low in range(0, cols, tile)]
    return [low_of(dp_count // 2, rows, n) for n in [cols] + tiles]


def swap_cores(outs, dp_count, digit):
    if len(outs) == 1:
        whole = outs[0].reshape(dp_count // 2, 2, -1, outs[0].shape[1])
        core = digit_at(digit)
        take = lambda which: lax.dynamic_index_in_dim(whole, which, 1, keepdims=False)
        outs = [take(core), take(1 - core)]
    return outs[0], [rotate(part, digit, 1) for part in outs[1:]]


def out_gradient_kernel(at, a, b, *outs):
    put_gradient(a, b, outs, at[CORE], tile=OUT_TILE)


def rows_halves_kernel(at, mine, *refs):
    got, (kept, sent) = refs[:-2], refs[-2:]
    lines = kept.shape[1]
    first = at[T] == 0
    for group in range(mine.shape[0]):
        low = 0
        for part in got:
            high = low + part.shape[2]
            total = mine[group, :, low:high].astype(WIDE) + part[group].astype(WIDE)
            a, b = total[:lines], total[lines:]
            kept[group, :, low:high] = jnp.where(first, a, b).astype(LOW)
            sent[group, :, low:high] = jnp.where(first, b, a).astype(LOW)
            low = high


def own_forward_kernel(at, normed, up, up_b, down_t, _, hidden, slope, out):
    pre_act = nn(normed[...], up[...]).reshape(-1, *up_b.shape) + up_b[...]
    active, slopes = (value.reshape(hidden.shape) for value in gelu_parts(pre_act))
    hidden[...] = active.astype(LOW)
    slope[...] = slopes
    out[...] = nt(hidden[...], down_t[...])


def own_kernel(at, a_down, b_down, a_up, b_up, down, up, sums):
    tile = 384
    for low in range(0, b_down.shape[1], tile):
        here = slice(low, low + tile)
        down[:, here] = tn(a_down[...], b_down[:, here])
        up[:, here] = tn(a_up[...], b_up[:, here])
    sums[...] = jnp.sum(b_up[...].astype(WIDE), axis=0, keepdims=True)


def rest_kernel(at, own, a, b, *outs):
    put_gradient(a, b, outs, at[CORE], own=own)


def rest_sums_kernel(at, own, own_sums, a, b, sums, *outs):
    put_gradient(a, b, outs, at[CORE], own=own)
    sums[...] = own_sums[...] + jnp.sum(b[...].astype(WIDE), axis=0, keepdims=True)


def up_row_kernel(lines, at, w, row, line):
    half, each = w.shape[0] // 2, row.shape[1] * lines * 2 // w.shape[0]
    low = w.shape[1] - PAIR
    for n in range(half // lines):
        a = w[n * lines : n * lines + 1, low:].astype(WIDE)
        b = w[half + n * lines : half + n * lines + 1, low:].astype(WIDE)
        value = jnp.where(at[T] == 0, a, b)[:, UP_AT : UP_AT + each]
        line[:, n * each : (n + 1) * each] = value
    row[...] = jnp.broadcast_to(line[...], row.shape)


def halve_kernel(at, mine, *refs):
    got, (kept, sent) = refs[:-2], refs[-2:]
    x = at[X]
    for group in range(kept.shape[0]):
        for other, out in ((0, kept), (1, sent)):
            place = 2 * group + (1 - x if other else x)
            low = 0
            for part in got:
                high = low + part.shape[2]
                total = mine[place, :, low:high].astype(WIDE) + part[place].astype(WIDE)
                out[group, :, low:high] = total.astype(LOW)
                low = high


def halve(at, mine, got):
    groups, rows, cols = mine.shape
    return call(halve_kernel, [low_of(groups // 2, rows, cols)] * 2, at, mine, *got)


def quarter_kernel(at, mine, *refs):
    got, (out_mine, out_got, keep, to_x, to_y, to_both) = refs[:-6], refs[-6:]
    lines, cols = to_y.shape[1:]
    first = at[T] == 0
    for group in range(keep.shape[0]):
        own, other = 2 * group + at[X], 2 * group + 1 - at[X]
        for place, same, across in ((own, keep, to_y), (other, to_x, to_both)):
            low = 0
            for part in got:
                high = low + part.shape[2]
                total = mine[place, :, low:high].astype(WIDE) + part[place].astype(WIDE)
                a, b = total[:lines], total[lines:]
                same[group, :, low:high] = jnp.where(first, a, b).astype(LOW)
                across[group, :, low:high] = jnp.where(first, b, a).astype(LOW)
                low = high
            total = out_mine[place].astype(WIDE) + out_got[place].astype(WIDE)
            same[group, :, cols:] = total.astype(LOW)


def parts_kernel(size, at, mine, x_got, y_got, both_got, *outs):
    me = at[OUTER]
    cols = mine.shape[2]
    for group in range(outs[0].shape[0]):
        for step, out in enumerate(outs):
            place = group * size + lax.rem(me + step, size)
            total = mine[place].astype(WIDE) + x_got[place].astype(WIDE)
            out[group, :, :cols] = total.astype(out.dtype)
            total = y_got[place].astype(WIDE) + both_got[place].astype(WIDE)
            out[group, :, cols:] = total.astype(out.dtype)


def outer_parts(at, digits, *parts):
    size = digits[-3][1]
    blocks, rows, cols = parts[0].shape
    shape = (blocks // size, rows, cols + parts[2].shape[2])
    outs = [wide_of(*shape)] + [low_of(*shape)] * (size - 1)
    kept, *sent = call(functools.partial(parts_kernel, size), outs, at, *parts)
    return kept, sent


def far_kernel(at, mine, got, kept, sent):
    me = at[OUTER]
    pair = lax.bitwise_xor(me, 1)
    for group in range(kept.shape[0] // 2):
        for n, block in enumerate((me, pair)):
            for out, place in ((kept, block), (sent, lax.bitwise_xor(block, 2))):
                spot = 4 * group + place
                total = mine[spot].astype(WIDE) + got[spot].astype(WIDE)
                out[2 * group + n] = total.astype(out.dtype)


def near_kernel(at, mine, got, *refs):
    kept, sent = refs[-2:]
    for group in range(kept.shape[0]):
        kept[group] = mine[2 * group] + got[2 * group].astype(WIDE)
        total = mine[2 * group + 1] + got[2 * group + 1].astype(WIDE)
        sent[group] = total.astype(LOW)


def far_parts(at, mine, got, digits):
    assert digits[-3][1] == 4
    blocks, rows, cols = mine.shape
    return call(
        far_kernel, [wide_of(blocks // 2, rows, cols), low_of(blocks // 2, rows, cols)], at, mine, got
    )


def near_parts(at, mine, got, *ahead):
    blocks, rows, cols = mine.shape
    outs = [wide_of(blocks // 2, rows, cols), low_of(blocks // 2, rows, cols)]
    return call(near_kernel, outs, at, mine, got, *ahead)


def outer_send(sent, digits):
    return [rotate(part, digits[-3], step + 1) for step, part in enumerate(sent)]


def outer_sum(kept, got, digits):
    for part in got:
        kept = kept + part.astype(WIDE)
    for digit in reversed(digits[:-3]):
        size = digit[1]
        kept = kept.reshape((-1, size) + kept.shape[1:])
        at = digit_at(digit)
        take = lambda step: lax.dynamic_index_in_dim(kept, (at + step) % size, 1, keepdims=False)
        total = take(0)
        for step in range(1, size):
            total = total + rotate(take(step).astype(LOW), digit, step).astype(WIDE)
        kept = total
    return kept[0]


def fill_mask(mask, at, half_rows, mem_count, starts):
    rows = mask.shape[0]
    padded = rows // 2

    def places(shape, axis):
        spot = lax.broadcasted_iota(jnp.int32, shape, axis)
        second = spot >= padded
        within = jnp.where(second, spot - padded, spot)
        pos = within + jnp.where(second, half_rows, 0) - mem_count
        doc = jnp.zeros(shape, jnp.int32)
        for i in range(starts):
            doc = doc + (at[STARTS + i] <= pos).astype(jnp.int32)
        return within < half_rows, pos, doc

    _, q_pos, q_doc = places((rows, 1), 0)
    real, k_pos, k_doc = places((1, rows), 1)
    key_ok = real & (k_pos < at[LENGTH])
    for low in range(0, rows, CHUNK):
        qp, qd = q_pos[low : low + CHUNK], q_doc[low : low + CHUNK]
        same = (qd == k_doc) | (qp < 0) | (k_pos < 0)
        mask[low : low + CHUNK, :] = jnp.where(same & key_ok, 0.0, -1e9)


def heads_apart(pair):
    lane = lax.broadcasted_iota(jnp.int32, (1, PAIR), 1)
    zero = jnp.zeros((), LOW)
    return jnp.concatenate(
        [jnp.where(lane < HEAD, pair, zero), jnp.where(lane < HEAD, zero, pair)], axis=0
    )


def lanes(pair, count):
    return pl.ds(pl.multiple_of(pair * count, PAIR), count)


def forward_kernel(
    half_rows, mem_count, starts, first_bias,
    at, own, other, w, qkv, mix_own, mix_sent, lse, x, small, mask, s, mixed,
):
    rows, padded = x.shape[0], own.shape[0]
    t = at[T]
    part = mix_own.shape[1]
    fill_mask(mask, at, half_rows, mem_count, starts)
    lse[...] = jnp.zeros_like(lse)
    small[...] = w[:, 3 * part :].astype(WIDE).T[: small.shape[0]]
    x[pl.ds(pl.multiple_of(t * padded, 16), padded), :] = own[...]
    x[pl.ds(pl.multiple_of((1 - t) * padded, 16), padded), :] = other[...]
    row = lax.broadcasted_iota(jnp.int32, (32, 1), 0)
    fresh = (row < mem_count) & (at[FRESH] == 1)
    x[:32, :] = jnp.where(fresh, small[:32, :], x[:32, :].astype(WIDE)).astype(LOW)
    lane = lax.broadcasted_iota(jnp.int32, (1, PAIR), 1)
    scale = jnp.where(lax.broadcasted_iota(jnp.int32, (1, 3 * PAIR), 1) < PAIR, 0.125, 1.0)

    def one_pair(pair, _):
        here = pl.ds(pl.multiple_of(t * part + pair * PAIR, PAIR), PAIR)
        q_bias = small[first_bias : first_bias + 1, here]
        v_bias = small[first_bias + 1 : first_bias + 2, here]
        bias = jnp.concatenate([q_bias, jnp.zeros_like(q_bias), v_bias], axis=1)
        got = (nn(x[...], w[:, lanes(pair, 3 * PAIR)]) + bias).astype(LOW)
        got = (got.astype(WIDE) * scale).astype(LOW)
        qkv[:, lanes(pair, 3 * PAIR)] = got
        keys, values = got[:, PAIR : 2 * PAIR], got[:, 2 * PAIR :]
        q = heads_apart(got[:, :PAIR])
        for low in range(0, 2 * rows, FORWARD_BLOCK):
            here, there = slice(low, low + FORWARD_BLOCK), slice(low % rows, low % rows + FORWARD_BLOCK)
            v = nt(q[here], keys) + mask[there, :]
            top = jnp.max(v, axis=-1, keepdims=True)
            e = jnp.exp(v - top)
            total = jnp.sum(e, axis=-1, keepdims=True)
            out = nn((e * (1.0 / total)).astype(LOW), values)
            spot = lane == 2 * pair + low // rows
            lse[there, :] = jnp.where(spot, top + jnp.log(total), lse[there, :])
            if low < rows:
                s[there, :] = out
            else:
                mixed[there, :] = jnp.where(lane < HEAD, s[there, :], out).astype(LOW)
        mix_own[:, lanes(pair, PAIR)] = mixed[pl.ds(pl.multiple_of(t * padded, 16), padded), :]
        mix_sent[:, lanes(pair, PAIR)] = mixed[
            pl.ds(pl.multiple_of((1 - t) * padded, 16), padded), :
        ]
        return 0

    lax.fori_loop(0, part // PAIR, one_pair, 0)


def backward_kernel(
    half_rows, mem_count, starts, at, qkv, own, got, lse, dproj, sums, mask, s, p, ds, dmix
):
    rows, padded = qkv.shape[0], own.shape[0]
    part = own.shape[1]
    t = at[T]
    fill_mask(mask, at, half_rows, mem_count, starts)
    dmix[pl.ds(pl.multiple_of(t * padded, 16), padded), :] = own[...]
    dmix[pl.ds(pl.multiple_of((1 - t) * padded, 16), padded), :] = got[...]
    lane = lax.broadcasted_iota(jnp.int32, (1, PAIR), 1)
    zero = jnp.zeros((), LOW)

    def one_pair(pair, _):
        here = lanes(pair, 3 * PAIR)
        whole = qkv[:, here]
        keys, values = whole[:, PAIR : 2 * PAIR], whole[:, 2 * PAIR :]
        dm_pair = dmix[:, lanes(pair, PAIR)]
        q, dm = heads_apart(whole[:, :PAIR]), heads_apart(dm_pair)
        for low in range(0, 2 * rows, BACKWARD_BLOCK):
            block, there = slice(low, low + BACKWARD_BLOCK), slice(low % rows, low % rows + BACKWARD_BLOCK)
            spot = lane == 2 * pair + low // rows
            stat = jnp.sum(jnp.where(spot, lse[there, :], 0.0), axis=-1, keepdims=True)
            e = jnp.exp(nt(q[block], keys) + mask[there, :] - stat)
            d = nt(dm[block], values)
            dot = jnp.sum(e * d, axis=-1, keepdims=True)
            p[block, :] = e.astype(LOW)
            d = (e * (d - dot)).astype(LOW)
            ds[block, :] = d
            s[block, :] = nn(d, keys)
        dq = jnp.where(lane < HEAD, s[:rows, :], s[rows:, :]) * 0.125
        dk, dv = tn(ds[...], q), tn(p[...], dm)
        out = jnp.concatenate([dq, dk, dv], axis=1).astype(LOW)
        dproj[:, here] = out
        sums[:, here] = jnp.sum(out.astype(WIDE), axis=0, keepdims=True)
        return 0

    lax.fori_loop(0, part // PAIR, one_pair, 0)


def half_rows_of(ref, which, padded):
    return ref[pl.ds(pl.multiple_of(which * padded, 16), padded), :]


def projection_gradient_kernel(
    small_rows, lines, at, layer_in, d_projected, proj_sums, sums_one, two0, two1, up_sums, wqkv, d_attn,
    *refs,
):
    grads, (turn, rows) = refs[:-2], refs[-2:]
    cols = d_projected.shape[1]
    part = cols // 3
    first = at[T] == 0
    turn[...] = jnp.zeros_like(turn)
    (m0, m1), (v0, _), (g0, _) = small_rows
    count = m1 - m0
    memory = nt(d_projected[:32, :], wqkv[:, :cols])[:count]
    memory = memory + jnp.where(first, d_attn[:count, :], 0.0)
    turn[m0:m1, :] = jnp.where(at[FRESH] == 1, memory, 0.0)
    sums = [
        jnp.concatenate(
            [proj_sums[:, (3 * p + k) * PAIR : (3 * p + k + 1) * PAIR] for p in range(part // PAIR)],
            axis=1,
        )
        for k in (0, 2)
    ]
    for low, value in enumerate(sums, v0):
        turn[low : low + 1, :part] = jnp.where(first, value, 0.0)
        turn[low : low + 1, part:] = jnp.where(first, 0.0, value)
    sums_two = two0[...] + two1[...]
    turn[v0 + 2 : v0 + 4, :] = sums_one[0:2, :]
    turn[v0 + 4 : v0 + 6, :] = sums_two[0:2, :]
    turn[g0 : g0 + 1, :] = sums_one[2:3, :]
    turn[g0 + 1 : g0 + 2, :] = sums_two[2:3, :]
    rows[...] = turn[...].T
    half = rows.shape[0] // 2
    each = up_sums.shape[1] * lines // half
    for n in range(half // lines):
        value = up_sums[:, n * each : (n + 1) * each]
        for side, low in ((0, n * lines), (1, half + n * lines)):
            rows[low : low + 1, UP_AT : UP_AT + each] = jnp.where(at[T] == side, value, 0.0)
    small = rows[...]
    put_gradient(layer_in, d_projected, grads, at[CORE])
    if len(grads) == 1:
        grads[0][:, cols:] = small.astype(LOW)
    else:
        put_blocks(small, grads[0], grads[-1], at[CORE], cols)


def projection_back_kernel(at, d_projected, wqkv, d_attn, d_own, d_sent):
    padded, cols = d_own.shape[0], d_projected.shape[1]
    t = at[T]
    d_own[...] = d_attn[...] + nt(half_rows_of(d_projected, t, padded), wqkv[:, :cols])
    d_sent[...] = nt(half_rows_of(d_projected, 1 - t, padded), wqkv[:, :cols]).astype(LOW)


def finish_kernel(
    part, small_rows, count, at, *refs
):
    parts, (qkv, out, memory, vectors, gains, up, turn) = refs[:count], refs[count:]
    total = parts[0][...]
    for value in parts[1:]:
        total = total + value[...].astype(WIDE)
    lines = total.shape[0]
    cols, width = 3 * part, 2 * part
    mine, got = total[:, : cols + PAIR], total[:, cols + PAIR + width :]
    first = at[T] == 0
    for pair in range(part // PAIR):
        for kind in range(3):
            here = (3 * pair + kind) * PAIR
            a, b = mine[:, here : here + PAIR], got[:, here : here + PAIR]
            low = kind * width + pair * PAIR
            qkv[:, low : low + PAIR] = jnp.where(first, a, b)
            qkv[:, low + part : low + part + PAIR] = jnp.where(first, b, a)
    out[...] = total[:, cols + PAIR : cols + PAIR + width]
    turn[...] = jnp.zeros_like(turn)
    turn[:lines, :] = mine[:, cols:] + got[:, cols:]
    up[...] = turn[0:1, UP_AT : UP_AT + up.shape[1]]
    small = turn[...].T
    for target, (low, high) in zip((memory, vectors, gains), small_rows):
        target[...] = small[low:high, :lines]


def spread_of(v):
    return jnp.mean(v, axis=-1, keepdims=True)


def first_norm_kernel(bias, gain, at, own, got, wout, layer_in, small, mixed, unit, scale, normed, s):
    padded, part = own.shape
    first = at[T] == 0
    mixed[:, :part] = jnp.where(first, own[...], got[...])
    mixed[:, part:] = jnp.where(first, got[...], own[...])
    s[...] = nn(mixed[...], wout[...])
    for low in range(0, padded, ROWS):
        here = slice(low, low + ROWS)
        rows = layer_in[pl.ds(pl.multiple_of(at[T] * padded + low, ROWS), ROWS), :]
        total = rows.astype(WIDE) + (s[here, :] + small[bias + 2 : bias + 3, :])
        centered = total - spread_of(total)
        factor = lax.rsqrt(spread_of(centered * centered) + NORM_EPSILON)
        value = centered * factor
        unit[here, :] = value
        scale[here, :] = jnp.broadcast_to(factor, (ROWS, PAIR))
        value = value * small[gain : gain + 1, :] + small[bias + 3 : bias + 4, :]
        normed[here, :] = value.astype(LOW)


def add_sums(sums, values):
    sums[...] = jnp.zeros_like(sums)
    for n, value in enumerate(values):
        sums[n : n + 1, :] = jnp.sum(value, axis=0, keepdims=True)


def second_norm_kernel(
    bias, gain, start, at, unit, small, own, got, d_out, _, layer_out, d_second, d_ffn, sums
):
    width = unit.shape[1]
    real = d_out.shape[0] - start
    totals = [jnp.zeros((ROWS, width), WIDE)] * 3
    for low in range(0, got.shape[0], ROWS):
        here, there = slice(low, low + ROWS), slice(start + low, start + low + ROWS)
        count = min(ROWS, real - low)
        first = unit[there, :] * small[gain : gain + 1, :] + small[bias + 3 : bias + 4, :]
        ffn = own[there, :] + got[here, :].astype(WIDE) + small[bias + 4 : bias + 5, :]
        total = first + ffn
        centered = total - spread_of(total)
        factor = lax.rsqrt(spread_of(centered * centered) + NORM_EPSILON)
        value = centered * factor
        out = value * small[gain + 1 : gain + 2, :] + small[bias + 5 : bias + 6, :]
        layer_out[low : low + count, :] = out[:count].astype(LOW)
        cotangent = d_out[start + low : start + low + count, :].astype(WIDE)
        if count < ROWS:
            cotangent = jnp.concatenate(
                [cotangent, jnp.zeros((ROWS - count, width), WIDE)], axis=0
            )
        d_unit = cotangent * small[gain + 1 : gain + 2, :]
        back = factor * (d_unit - spread_of(d_unit) - value * spread_of(d_unit * value))
        d_second[here, :] = back
        rounded = back.astype(LOW)
        d_ffn[here, :] = rounded
        terms = (rounded.astype(WIDE), cotangent, cotangent * value)
        totals = [a + b for a, b in zip(totals, terms)]
    add_sums(sums, totals)


def first_back_kernel(
    gain, at, second0, second1, own, got, unit, scale, small, wout, d_attn_in, d_attn, mix_own, mix_sent, sums
):
    padded, width = unit.shape
    part = mix_own.shape[1]
    totals = [jnp.zeros((ROWS, width), WIDE)] * 3
    for low in range(0, padded, ROWS):
        here = slice(low, low + ROWS)
        cut = second0.shape[0]
        second = second0[here, :] if low < cut else second1[low - cut : low - cut + ROWS, :]
        cotangent = second + own[here, :] + got[here, :].astype(WIDE)
        value = unit[here, :]
        d_unit = cotangent * small[gain : gain + 1, :]
        back = d_unit - spread_of(d_unit) - value * spread_of(d_unit * value)
        back = scale[here, :1] * back
        d_attn_in[here, :] = back
        rounded = back.astype(LOW)
        d_attn[here, :] = rounded
        terms = (rounded.astype(WIDE), cotangent, cotangent * value)
        totals = [a + b for a, b in zip(totals, terms)]
    add_sums(sums, totals)
    mixed = nt(d_attn[...], wout[...]).astype(LOW)
    first = at[T] == 0
    mix_own[...] = jnp.where(first, mixed[:, :part], mixed[:, part:])
    mix_sent[...] = jnp.where(first, mixed[:, part:], mixed[:, :part])


def rows_kernel(mem_count, at, own, got, out):
    real = out.shape[0]
    row = lax.broadcasted_iota(jnp.int32, (32, 1), 0)
    fresh = (row < mem_count) & (at[FRESH] == 1) & (at[T] == 0)
    out[:32, 0, :] = jnp.where(fresh, 0.0, own[:32, :] + got[:32, :].astype(WIDE))
    out[32:, 0, :] = own[32:real, :] + got[32:real, :].astype(WIDE)


def gelu_parts(pre):
    cdf = 0.5 * (1.0 + lax.erf(pre * 0.7071067811865476))
    density = jnp.exp(-0.5 * pre * pre) * 0.3989422804014327
    return pre * cdf, cdf + pre * density


def shards(
    rows_in,
    d_out,
    starts,
    lengths,
    resets,
    qkv_weight,
    out_weight,
    bias_vec,
    gains,
    mem_init,
    ffn_up,
    up_bias,
    ffn_down,
):
    half_rows, seg_count, width = rows_in.shape
    assert seg_count == 1
    dp_count, t_count = lax.axis_size("dp"), lax.axis_size("tensor")
    assert t_count == 2
    digits = digits_of(dp_count)
    x_digit, core_digit = digits[-2:]
    padded = ceil_to(half_rows, 16)
    rows = 2 * padded
    mem_count = mem_init.shape[0]
    part = HEADS // t_count * HEAD
    cols = 3 * part
    hidden_mine = ffn_up.shape[1]
    feat = bias_vec.shape[1]
    lines = qkv_weight.shape[0]
    doc_count = starts.shape[1]
    counts = (mem_count, bias_vec.shape[0], gains.shape[0])
    edges = [sum(counts[:n]) for n in range(len(counts) + 1)]
    small_rows = tuple(zip(edges[:-1], edges[1:]))
    bias, gain = edges[1], edges[2]
    integers = [
        lax.axis_index("tensor"),
        digit_at(x_digit),
        digit_at(core_digit),
        digit_at(digits[-3]),
        lax.axis_index("dp"),
        resets[0],
        lengths[0],
    ]
    at = jnp.concatenate([jnp.stack(integers).astype(jnp.int32), starts[0]])

    side = lax.axis_index("tensor").astype(jnp.int32).reshape(1)
    (packed,) = call(
        functools.partial(columns_kernel, small_rows),
        [low_of(lines, 3 * width + PAIR + width)],
        side, qkv_weight, bias_vec, gains, mem_init, up_bias.reshape(1, -1), out_weight,
        scratch=[pltpu.VMEM((PAIR, PAIR), WIDE)],
        room=57 << 20,
    )
    rows_low = jnp.pad(tie(rows_in, packed)[:, 0, :], ((0, padded - half_rows), (0, 0)))
    rows_other = swap_tensor(rows_low)
    up_pair = spread_near(ffn_up, digits)
    first_z = spread_outer(packed, digits)
    rows_other, up_pair = join(rows_other, tie(up_pair, first_z))
    slots = first_z.shape[0]
    mine, other = call(
        functools.partial(halves_of_heads_kernel, part),
        [low_of(slots, lines, cols + PAIR + width), low_of(slots, lines, cols + PAIR)],
        at, first_z,
    )
    first_parts = [mine, swap_tensor(other), rotate(mine, x_digit, 1), swap_both(other, x_digit)]
    up_z = spread_far(up_pair, digits)
    down_pair = spread_near(tie(ffn_down.T, mine), digits)
    *first_parts, up_z, down_in = join(*first_parts, up_z, down_pair)
    first_parts = [jnp.concatenate(first_parts[n : n + 2], axis=2) for n in (0, 2)]
    core_parts = [rotate(value, core_digit, 1) for value in first_parts]
    sizes = tuple(size for _, size in digits)
    (wqkv,) = call(
        functools.partial(assemble_first_kernel, sizes),
        [low_of(dp_count, 2 * lines, cols + PAIR)],
        at, *first_parts, *core_parts,
    )
    wqkv = wqkv.reshape(width, cols + PAIR)
    (out_sent,) = call(
        functools.partial(beside_kernel, cols + PAIR),
        [low_of(dp_count // 2, lines, width)], at, *first_parts,
    )
    out_got = swap_tensor(out_sent)
    up_x = rotate(up_z, x_digit, 1)
    down_pieces = spread_far_pieces(down_in, digits)
    down_x = [rotate(down_pieces[0], x_digit, 1)]

    projected, mix_own, mix_sent, log_total, layer_in, small = call(
        functools.partial(forward_kernel, half_rows, mem_count, doc_count, bias),
        [
            low_of(rows, cols),
            low_of(padded, part),
            low_of(padded, part),
            wide_of(rows, PAIR),
            low_of(rows, width),
            wide_of(ceil_to(edges[-1], 32), width),
        ],
        at, rows_low, rows_other, wqkv,
        scratch=[
            pltpu.VMEM((rows, rows), WIDE),
            pltpu.VMEM((rows, PAIR), WIDE),
            pltpu.VMEM((rows, PAIR), LOW),
        ],
    )
    mix_got = swap_tensor(mix_sent)
    out_got = tie(out_got, mix_sent)
    (wout,) = call(
        functools.partial(assemble_out_kernel, sizes, cols + PAIR),
        [low_of(dp_count, 2 * lines, width)],
        at, *first_parts, *core_parts, out_got, rotate(out_got, core_digit, 1),
    )
    wout = wout.reshape(width, width)
    mix_got, *down_pieces = join(mix_got, *down_pieces)
    mixed, unit, scale, normed_own = call(
        functools.partial(first_norm_kernel, bias, gain),
        [low_of(padded, width), wide_of(padded, width), wide_of(padded, PAIR), low_of(padded, width)],
        at, mix_own, mix_got, wout, layer_in, small,
        scratch=[pltpu.VMEM((padded, width), WIDE)],
    )

    normed_got = swap_tensor(normed_own)
    up_x, up_z = tie(up_x, mix_sent), tie(up_z, mix_sent)
    down_pieces = [tie(piece, mix_sent) for piece in down_pieces]
    down_x = [tie(down_x[0], mix_sent)]
    up = assemble(at, swap_blocks(up_z, up_x, digits), digits, hidden_mine, paired=True)
    (up_b,) = call(
        functools.partial(up_row_kernel, lines), [wide_of(ROWS, hidden_mine)], at, wqkv,
        scratch=[pltpu.VMEM((1, hidden_mine), WIDE)],
    )
    down_pieces[1], down_x[0] = join(down_pieces[1], down_x[0])
    down_x.append(rotate(down_pieces[1], x_digit, 1))
    normed_got, up_b, up = join(normed_got, up_b, up)
    down_t = assemble(at, swap_pieces(down_pieces, down_x, digits), digits, hidden_mine, paired=True)

    def feed_forward(rows):
        pre_act = nn(rows, up).reshape(-1, *up_b.shape) + up_b
        hidden, slope = (part.reshape(rows.shape[0], -1) for part in gelu_parts(pre_act))
        hidden = hidden.astype(LOW)
        return hidden, slope, nt(hidden, down_t)

    cut = ceil_to(padded // 2, ROWS)
    pieces = ((0, cut), (cut, padded))
    hidden_got, slope_got, ffn_sent = feed_forward(normed_got)
    ffn_sent = ffn_sent.astype(LOW)
    (_, first_cut), (_, end) = pieces
    ffn_got = [swap_tensor(ffn_sent[:first_cut])]
    hidden_own, slope_own, ffn_own = call(
        own_forward_kernel,
        [low_of(padded, hidden_mine), wide_of(padded, hidden_mine), wide_of(padded, width)],
        at, normed_own, up, up_b, down_t, rotate(ffn_sent[:ROWS, :PAIR], core_digit, 1),
    )
    ffn_got.append(swap_tensor(tie(ffn_sent, ffn_own)[first_cut:end]))
    d_out_rows = d_out.reshape(half_rows, width)
    second, ahead = [], small
    for (low, high), got in zip(pieces, ffn_got):
        if second:
            ahead = rotate(second[-1][2][:ROWS, :PAIR], core_digit, 1)
        outs = [
            low_of(min(high, half_rows) - low, width),
            wide_of(high - low, width),
            low_of(high - low, width),
            wide_of(8, width),
        ]
        kernel = functools.partial(second_norm_kernel, bias, gain, low)
        second.append(call(kernel, outs, at, unit, small, ffn_own, got, d_out_rows, ahead))
    layer_out, d_second, d_ffn_sent, sums_two = zip(*second)

    d_ffn_got = jnp.concatenate([swap_tensor(piece) for piece in d_ffn_sent], axis=0)
    d_ffn_own = jnp.concatenate(d_ffn_sent, axis=0)

    def feed_back(rows, slope):
        d_pre = (slope * nn(rows, down_t)).astype(LOW)
        return d_pre, nt(d_pre, up)

    d_pre_own, d_first_own = feed_back(d_ffn_own, slope_own)
    down_own, up_own, sums_own = call(
        own_kernel,
        [wide_of(width, hidden_mine), wide_of(width, hidden_mine), wide_of(1, hidden_mine)],
        at, d_ffn_own, hidden_own, normed_own, d_pre_own,
    )
    d_ffn_got, d_first_own, down_own, up_own = join(d_ffn_got, d_first_own, down_own, up_own)
    d_pre_got, d_first_sent = feed_back(d_ffn_got, slope_got)
    d_first_sent = d_first_sent.astype(LOW)
    d_first_got = swap_tensor(d_first_sent)

    outs = gradient_outs(width, hidden_mine, dp_count)
    down_grads = call(
        rest_kernel, outs, at, down_own, tie(d_ffn_got, d_first_sent), hidden_got
    )
    down_kept, down_sent = halve(at, *swap_cores(down_grads, dp_count, core_digit))
    down_got = rotate(down_sent, x_digit, 1)
    up_sums, *up_grads = call(
        rest_sums_kernel, [wide_of(1, hidden_mine)] + outs,
        at, up_own, sums_own, normed_got, tie(d_pre_got, down_sent),
    )
    up_kept, up_sent = halve(at, *swap_cores(up_grads, dp_count, core_digit))

    d_attn_in, d_attn, d_mix_own, d_mix_sent, sums_one = call(
        functools.partial(first_back_kernel, gain),
        [
            wide_of(padded, width),
            low_of(padded, width),
            low_of(padded, part),
            low_of(padded, part),
            wide_of(8, width),
        ],
        at, *d_second, d_first_own, d_first_got, unit, scale, small, wout,
    )
    d_mix_got = swap_tensor(d_mix_sent)
    out_grads = call(
        out_gradient_kernel, gradient_outs(width, width, dp_count, OUT_TILE),
        at, mixed, tie(d_attn, d_mix_sent),
    )
    out_kept, out_parts = swap_cores(out_grads, dp_count, core_digit)
    out_kept, out_sent = call(
        rows_halves_kernel, [low_of(dp_count // 2, lines, width)] * 2, at, out_kept, *out_parts
    )
    down_kept, down_sent = far_parts(at, down_kept, down_got, digits)
    d_mix_got, out_sent, up_sent, down_sent = join(d_mix_got, out_sent, up_sent, down_sent)
    down_got = rotate(down_sent, digits[-3], 2)
    out_got = swap_tensor(out_sent)
    up_got = rotate(up_sent, x_digit, 1)

    d_projected, proj_sums = call(
        functools.partial(backward_kernel, half_rows, mem_count, doc_count),
        [low_of(rows, cols), wide_of(1, cols)],
        at, projected, d_mix_own, d_mix_got, log_total,
        scratch=[
            pltpu.VMEM((rows, rows), WIDE),
            pltpu.VMEM((2 * rows, PAIR), WIDE),
            pltpu.VMEM((2 * rows, rows), LOW),
            pltpu.VMEM((2 * rows, rows), LOW),
            pltpu.VMEM((rows, part), LOW),
        ],
    )
    up_kept, up_sent = far_parts(at, up_kept, up_got, digits)
    qkv_grads = call(
        functools.partial(projection_gradient_kernel, small_rows, lines),
        gradient_outs(width, cols + PAIR, dp_count),
        at, layer_in, d_projected, proj_sums, sums_one, *sums_two, up_sums, wqkv, d_attn_in,
        scratch=[pltpu.VMEM((PAIR, width), WIDE), pltpu.VMEM((width, PAIR), WIDE)],
    )
    out_got, down_got, *qkv_grads = join(out_got, down_got, *qkv_grads)
    down_kept, down_sent = near_parts(at, down_kept, down_got)
    qkv_kept, qkv_parts = swap_cores(qkv_grads, dp_count, core_digit)
    up_sent, *qkv_parts = join(up_sent, *qkv_parts)
    slots = dp_count // 4
    mine, to_x, to_y, to_both = call(
        quarter_kernel,
        [low_of(slots, lines, cols + PAIR + width)] * 2 + [low_of(slots, lines, cols + PAIR)] * 2,
        at, qkv_kept, *qkv_parts, out_kept, out_got,
    )

    both_got = [rotate(to_x, x_digit, 1), swap_tensor(to_y), swap_both(to_both, x_digit)]
    up_got = rotate(up_sent, digits[-3], 2)
    down_got = swap_near(down_sent, digits[-3])
    d_in_own, d_in_sent = call(
        projection_back_kernel, [wide_of(padded, width), low_of(padded, width)],
        at, tie(d_projected, to_x), wqkv, d_attn_in,
    )
    d_in_got = swap_tensor(d_in_sent)
    ahead = rotate(tie(d_in_sent, up_got)[:ROWS, :PAIR], core_digit, 1)
    up_kept, up_sent = near_parts(at, up_kept, up_got, ahead)
    *both_got, up_sent, down_got = join(*both_got, up_sent, down_got)
    up_got = swap_near(up_sent, digits[-3])
    both_kept, both_sent = outer_parts(at, digits, mine, *both_got)
    both_got = outer_send(both_sent, digits)
    grad_ffn_down = outer_sum(down_kept, [down_got], digits)
    grad_ffn_up = outer_sum(up_kept, [up_got], digits)
    (grad_rows,) = call(
        functools.partial(rows_kernel, mem_count), [wide_of(half_rows, 1, width)], at, d_in_own, d_in_got
    )
    grad_rows, *both_got = join(grad_rows, *both_got)

    if len(digits) == 3:
        parts = [both_kept[0], *[part[0] for part in both_got]]
    else:
        parts = [outer_sum(both_kept, both_got, digits)]
    grad_qkv, grad_out_weight, grad_mem, grad_vec, grad_gains, grad_up_bias = call(
        functools.partial(finish_kernel, part, small_rows, len(parts)),
        [wide_of(lines, 3 * width), wide_of(lines, width)]
        + [wide_of(n, feat) for n in counts]
        + [wide_of(1, up_bias.shape[0])],
        at, *parts,
        scratch=[pltpu.VMEM((PAIR, PAIR), WIDE)],
    )
    return (
        jnp.concatenate(layer_out, axis=0).reshape(half_rows, 1, width),
        grad_rows,
        grad_qkv,
        grad_out_weight,
        grad_vec,
        grad_gains,
        grad_mem,
        grad_ffn_up,
        grad_up_bias.reshape(up_bias.shape),
        grad_ffn_down.T,
    )


def solution(mesh):
    both = ("dp", "tensor")
    in_specs = (
        P("tensor", "dp", None),
        P("tensor", "dp", None),
        P("dp", None),
        P("dp"),
        P("dp"),
        P(both, None),
        P(both, None),
        P(None, both),
        P(None, both),
        P(None, both),
        P("dp", "tensor"),
        P(both),
        P("tensor", "dp"),
    )
    out_specs = (
        P("tensor", "dp", None),
        P("tensor", "dp", None),
        P(both, None),
        P(both, None),
        P(None, both),
        P(None, both),
        P(None, both),
        P("dp", "tensor"),
        P(both),
        P("tensor", "dp"),
    )
    return jax.shard_map(shards, mesh=mesh, in_specs=in_specs, out_specs=out_specs, check_vma=False)
```
